32 devices in a mesh: dp: 16 (over z, x, core), mp: 2 (over y).
Axes of the slice: x: 2, y: 2, z: 4, core: 2. Of those that a mesh axis runs over, the one named last changes fastest.
Arguments:
- block_input: bfloat16 [16384, 1152], P(('dp', 'mp')), may hold values from -6 to 6
- out_grad: bfloat16 [16384, 1152], P(('dp', 'mp')), may hold values from -6 to 6
- time_table: bfloat16 [1000, 1152], replicated, may hold values from -6 to 6
- class_table: bfloat16 [1001, 1152], replicated, may hold values from -6 to 6
- time_ids: int32 [64], P('dp'), may hold values from 0 to 999
- class_ids: int32 [64], P('dp'), may hold values from 0 to 1000
- image_patches: int32 [16], P('dp'), may hold values from 256 to 1024, as said below
- ada_weight: bfloat16 [1152, 6912], P(None, 'dp'), may hold values from -0.1875 to 0.1875
- ada_bias: bfloat16 [6912], P('dp'), may hold values from -3 to 3
- proj_weight: bfloat16 [4, 1152, 1152], P(None, 'dp', 'mp'), may hold values from -0.1875 to 0.1875
- decay_down: bfloat16 [1152, 16], replicated, may hold values from -0.1875 to 0.1875
- decay_up: bfloat16 [16, 1152], replicated, may hold values from -1.5 to 1.5
- decay_bias: bfloat16 [1152], replicated, may hold values from 0.5 to 7
- head_gain: bfloat16 [72], replicated, may hold values from 0.25 to 1.75
- conv_taps: bfloat16 [9, 1152], replicated, may hold values from -1.75 to 1.75
- out_weight: bfloat16 [1152, 1152], P('mp', 'dp'), may hold values from -0.1875 to 0.1875
- fc1_weight: bfloat16 [1152, 4608], P('dp', 'mp'), may hold values from -0.1875 to 0.1875
- fc2_weight: bfloat16 [4608, 1152], P('mp', 'dp'), may hold values from -0.09375 to 0.09375
Outputs:
- block_out: bfloat16 [16384, 1152], P(('dp', 'mp'))
- input_grad: float32 [16384, 1152], P(('dp', 'mp'))
- cond_grad: float32 [64, 1152], P('dp')
- ada_weight_grad: float32 [1152, 6912], P(None, 'dp')
- ada_bias_grad: float32 [6912], P('dp')
- proj_grad: float32 [4, 1152, 1152], P(None, 'dp', 'mp')
- decay_down_grad: float32 [1152, 16], replicated
- decay_up_grad: float32 [16, 1152], replicated
- decay_bias_grad: float32 [1152], replicated
- gain_grad: float32 [72], replicated
- conv_grad: float32 [9, 1152], replicated
- out_weight_grad: float32 [1152, 1152], P('mp', 'dp')
- fc1_grad: float32 [1152, 4608], P('dp', 'mp')
- fc2_grad: float32 [4608, 1152], P('mp', 'dp')
The draws below stay inside these ranges and needn't reach their ends.
Inputs may be any that keep to these rules, and one draw needn't show every extreme that they name: `image_patches`: each unit holds images of one size: its value is 16 * 16 (four small images) or 4 * 16 * 16 (one large image); half of all units, rounded down, hold a large image.
All inputs are finite; a program needn't handle non-finite values.
Results may differ from the reference program's by a relative error of at most 0.0095.
The reference program's roundings to bfloat16 on the way count: a program that leaves them out, or rounds other values in their place, can miss the bound.
Values may be sent and summed in bfloat16 or wider, within the bound.
No kernel may reach another device: no remote copies, remote signals or barrier semaphores. Data moves between devices by JAX's collectives and lax.ppermute only.
A program may use at most 320 MiB of HBM per device.

```python
from functools import partial
import jax
import jax.numpy as jnp
from jax import lax

D = 1152
HDIM = 72
FF = 4608
LOWRANK = 16
BLOCK_LEN = 64
SIDE = 16
TSTEPS = 1000
CLASSES = 1001
UNITS = 1
GROUPS = 16
TOKENS = 16384
SLOTS = 64


def draw_image_patches(key, part):
    unit_count = UNITS * GROUPS
    ranking = jax.random.permutation(key, unit_count)
    return jnp.where(ranking < unit_count // 2, 4 * SIDE * SIDE, SIDE * SIDE).astype(jnp.int32)


def place_ends(values, key, smallest, largest):
    dims = values.shape
    spot = [jax.random.randint(jax.random.fold_in(key, axis), (), 0, dims[axis]) for axis in range(len(dims))]
    values = values.at[tuple(spot)].set(smallest)
    longest = dims.index(max(dims))
    spot[longest] = (spot[longest] + 1) % dims[longest]
    return values.at[tuple(spot)].set(largest)


def steps_of(rng, shape, cuts, low, largest):
    def one(dim, parts):
        heights = jax.random.uniform(jax.random.fold_in(jax.random.fold_in(rng, 6), dim), (parts,), jnp.float32, low / len(cuts), largest / len(cuts))
        return jnp.repeat(jnp.exp(heights), shape[dim] // parts).reshape((-1,) + (1,) * (len(shape) - dim - 1))

    factor_of = one(*cuts[0])
    for cut in cuts[1:]:
        factor_of = factor_of * one(*cut)
    return factor_of


def scatter_about(own_key, extent, scale, most, shards=(), dtype=jnp.bfloat16):
    loudness = steps_of(own_key, extent, shards, -0.22, 0.18) if shards else 1.0
    array = jax.random.normal(own_key, extent, jnp.float32) * scale * loudness
    return jnp.minimum(jnp.maximum(array, -most), most).astype(dtype)


def setup_inputs(seed: int = 0) -> dict:
    keys = jax.random.split(jax.random.key(seed), 19)
    return {
        "block_input": scatter_about(keys[0], (TOKENS, D), 1.0, 6.0, ((0, 32),)),
        "out_grad": scatter_about(keys[1], (TOKENS, D), 1.0, 6.0, ((0, 32),)),
        "time_table": scatter_about(keys[2], (TSTEPS, D), 1.0, 6.0),
        "class_table": scatter_about(keys[3], (CLASSES, D), 1.0, 6.0),
        "time_ids": place_ends(jax.random.randint(keys[4], (SLOTS,), 0, TSTEPS), jax.random.fold_in(keys[4], 1), 0, TSTEPS - 1).astype(jnp.int32),
        "class_ids": place_ends(jax.random.randint(keys[5], (SLOTS,), 0, CLASSES), jax.random.fold_in(keys[5], 1), 0, CLASSES - 1).astype(jnp.int32),
        "image_patches": draw_image_patches(jax.random.fold_in(keys[18], 71), 0),
        "ada_weight": scatter_about(keys[7], (D, 6 * D), D ** -0.5, 0.1875, ((1, 16),)),
        "ada_bias": scatter_about(keys[8], (6 * D,), 0.5, 3.0, ((0, 16),)),
        "proj_weight": scatter_about(keys[9], (4, D, D), D ** -0.5, 0.1875, ((1, 16), (2, 2))),
        "decay_down": scatter_about(keys[10], (D, LOWRANK), D ** -0.5, 0.1875),
        "decay_up": scatter_about(keys[11], (LOWRANK, D), LOWRANK ** -0.5, 1.5),
        "decay_bias": jnp.clip(jax.random.uniform(keys[12], (D,), jnp.float32, 0.5, 7.0), 0.5, 7.0).astype(jnp.bfloat16),
        "head_gain": jnp.clip(1.0 + 0.15 * jax.random.normal(keys[13], (HDIM,), jnp.float32), 0.25, 1.75).astype(jnp.bfloat16),
        "conv_taps": scatter_about(keys[14], (9, D), 0.3, 1.75),
        "out_weight": scatter_about(keys[15], (D, D), D ** -0.5, 0.1875, ((0, 2), (1, 16))),
        "fc1_weight": scatter_about(keys[16], (D, FF), D ** -0.5, 0.1875, ((0, 16), (1, 2))),
        "fc2_weight": scatter_about(keys[17], (FF, D), FF ** -0.5, 0.09375, ((0, 2), (1, 16))),
    }


@jax.custom_vjp
def low(v):
    return lax.optimization_barrier(v.astype(jnp.bfloat16)).astype(jnp.float32)

@jax.custom_vjp
def low_back(v):
    return v

def low_keep(v):
    return (low(v), None)

def low_pass(kept, grad):
    return (grad,)

def back_keep(v):
    return (v, None)

def back_low(kept, grad):
    return (low(grad),)
low.defvjp(low_keep, low_pass)
low_back.defvjp(back_keep, back_low)
maximum_precision = lax.Precision.HIGHEST
norm_eps = 1e-06
head_eps = 1e-05
gate_norm = 16.0

def product(left, right):
    return jnp.dot(left, right, precision=maximum_precision, preferred_element_type=jnp.float32)

def shifted(unit_grid, offset):
    row_total = unit_grid.shape[1]
    margin = abs(offset)
    padded = jnp.pad(unit_grid, ((0, 0), (margin, margin), (0, 0)))
    return lax.slice_in_dim(padded, margin + offset, margin + offset + row_total, axis=1)

def depthwise(big_unit, value_matrix, conv_taps):
    row_total, channels = value_matrix.shape
    unit_count = big_unit.shape[0]
    unit_rows = row_total // unit_count
    unit_grid = value_matrix.reshape(unit_count, unit_rows, channels)
    positions = jnp.arange(unit_rows)
    small_pos = positions % (SIDE * SIDE)
    small_row = small_pos // SIDE
    small_col = small_pos % SIDE
    big_row = positions // (2 * SIDE)
    big_col = positions % (2 * SIDE)
    summed = jnp.zeros_like(unit_grid)
    tap_index = 0
    for row_step in (-1, 0, 1):
        for col_step in (-1, 0, 1):
            small_ok = ((small_row + row_step >= 0) & (small_row + row_step < SIDE) & (small_col + col_step >= 0) & (small_col + col_step < SIDE)).astype(jnp.float32)
            big_ok = ((big_row + row_step >= 0) & (big_row + row_step < 2 * SIDE) & (big_col + col_step >= 0) & (big_col + col_step < 2 * SIDE)).astype(jnp.float32)
            small_val = shifted(unit_grid, row_step * SIDE + col_step) * small_ok[None, :, None]
            big_val = shifted(unit_grid, row_step * 2 * SIDE + col_step) * big_ok[None, :, None]
            chosen = jnp.where(big_unit[:, None, None], big_val, small_val)
            summed = summed + chosen * conv_taps[tap_index]
            tap_index = tap_index + 1
    return summed.reshape(row_total, channels)

def block_step(running_state, inputs):
    query_rows, key_matrix, value_matrix, log_decay, start = inputs
    running_state = jnp.where(start, jnp.zeros_like(running_state), running_state)
    length = query_rows.shape[1]
    prefix_decay = jnp.cumsum(log_decay, axis=1)
    final_decay = prefix_decay[:, -1, :]
    causal = jnp.arange(length)[:, None] >= jnp.arange(length)[None, :]
    spread = prefix_decay[:, :, None, :] - prefix_decay[:, None, :, :]
    spread = jnp.where(causal[None, :, :, None], spread, -1e+30)
    scores = jnp.einsum('hik,hjk,hijk->hij', query_rows, key_matrix, jnp.exp(spread), precision=maximum_precision)
    inside = jnp.einsum('hij,hjv->hiv', scores, value_matrix, precision=maximum_precision)
    incoming_state = jnp.einsum('rqo,rol->rql', query_rows * jnp.exp(prefix_decay), running_state, precision=maximum_precision)
    fresh_contributions = jnp.einsum('rig,ril->rgl', key_matrix * jnp.exp(final_decay[:, None, :] - prefix_decay), value_matrix, precision=maximum_precision)
    running_state = running_state * jnp.exp(final_decay)[:, :, None] + fresh_contributions
    return (running_state, inside + incoming_state)

def gla_mixer(big_unit, query_rows, key_matrix, value_matrix, gate_rows, decay_pre, head_gain, conv_taps):
    row_total, channels = query_rows.shape
    head_count = channels // HDIM
    blocks = row_total // BLOCK_LEN

    def to_blocks(values):
        return values.reshape(blocks, BLOCK_LEN, head_count, HDIM).transpose(0, 2, 1, 3)
    per_unit = blocks // big_unit.shape[0]
    period = SIDE * SIDE // BLOCK_LEN
    block_ids = jnp.arange(blocks)
    position = block_ids % per_unit
    starts = jnp.where(big_unit[block_ids // per_unit], position == 0, position % period == 0)
    log_decay = jax.nn.log_sigmoid(decay_pre) / gate_norm
    scaled = query_rows * HDIM ** (-0.5)
    initial = jnp.zeros((head_count, HDIM, HDIM), jnp.float32)
    _, outputs = lax.scan(jax.checkpoint(block_step), initial, (to_blocks(scaled), to_blocks(key_matrix), to_blocks(value_matrix), to_blocks(log_decay), starts))
    outputs = outputs.transpose(0, 2, 1, 3).reshape(row_total, head_count, HDIM)
    local_term = depthwise(big_unit, value_matrix, conv_taps)
    combined = outputs + local_term.reshape(row_total, head_count, HDIM)
    normed = combined * lax.rsqrt(lax.optimization_barrier(jnp.mean(combined * combined, axis=-1, keepdims=True)) + head_eps) * head_gain
    return normed.reshape(row_total, channels) * jax.nn.silu(gate_rows)

def modulate(row_slots, shift, scale):
    center = row_slots - lax.optimization_barrier(jnp.mean(row_slots, axis=-1, keepdims=True))
    normed = center * lax.rsqrt(lax.optimization_barrier(jnp.mean(center * center, axis=-1, keepdims=True)) + norm_eps)
    return normed * (1.0 + scale[:, None, :]) + shift[:, None, :]

def effective(big_unit, modulation):
    unit_count = big_unit.shape[0]
    grouped = modulation.reshape(unit_count, 4, modulation.shape[-1])
    leading = jnp.broadcast_to(grouped[:, :1], grouped.shape)
    return jnp.where(big_unit[:, None, None], leading, grouped).reshape(modulation.shape)

def group_forward(weights, row_block, cond_rows, big_unit):
    ada_matrix, ada_offset, proj_matrix, down_matrix, up_matrix, decay_offset, gain_vector, conv_matrix, out_matrix, first_matrix, second_matrix = weights
    model_width = row_block.shape[1]
    slot_rows = SIDE * SIDE
    slot_total = cond_rows.shape[0]
    silu_low = low(jax.nn.silu(cond_rows))
    modulation = effective(big_unit, product(silu_low, ada_matrix) + ada_offset)
    pieces = [modulation[:, part_index * model_width:(part_index + 1) * model_width] for part_index in range(6)]
    residual = row_block.reshape(slot_total, slot_rows, model_width)
    hidden = low(modulate(residual, pieces[0], pieces[1]).reshape(-1, model_width))
    projected = low_back(jnp.einsum('rd,gde->gre', hidden, proj_matrix, precision=maximum_precision, preferred_element_type=jnp.float32))
    latent = product(hidden, down_matrix)
    decay_pre = product(latent, up_matrix) + decay_offset
    mixed = low(gla_mixer(big_unit, projected[0], projected[1], projected[2], projected[3], decay_pre, gain_vector, conv_matrix))
    attention = low_back(product(mixed, out_matrix)).reshape(slot_total, slot_rows, model_width)
    after_attn = residual + pieces[2][:, None, :] * attention
    hidden_two = low(modulate(after_attn, pieces[3], pieces[4]).reshape(-1, model_width))
    up_proj = low_back(product(hidden_two, first_matrix))
    active = low(jax.nn.gelu(up_proj, approximate=True))
    feed_out = low_back(product(active, second_matrix)).reshape(slot_total, slot_rows, model_width)
    return (after_attn + pieces[5][:, None, :] * feed_out).reshape(-1, model_width)

def reference(block_input, out_grad, time_table, class_table, time_ids, class_ids, image_patches, ada_weight, ada_bias, proj_weight, decay_down, decay_up, decay_bias, head_gain, conv_taps, out_weight, fc1_weight, fc2_weight):
    model_width = block_input.shape[1]
    group_rows = 4 * UNITS * SIDE * SIDE
    group_count = block_input.shape[0] // group_rows
    slots_group = 4 * UNITS
    condition = time_table[time_ids].astype(jnp.float32) + class_table[class_ids].astype(jnp.float32)
    big_all = (image_patches == 4 * SIDE * SIDE).reshape(group_count, UNITS)

    def whole_block(all_rows, all_cond, ada_matrix, ada_offset, proj_matrix, down_matrix, up_matrix, decay_offset, gain_vector, conv_matrix, out_matrix, first_matrix, second_matrix):
        weights = (ada_matrix, ada_offset, proj_matrix, down_matrix, up_matrix, decay_offset, gain_vector, conv_matrix, out_matrix, first_matrix, second_matrix)
        checked = jax.checkpoint(partial(group_forward, weights))

        def group_step(carry_value, group_in):
            row_block, cond_rows, big_unit = group_in
            return (carry_value, checked(row_block, cond_rows, big_unit))
        _, outputs = lax.scan(group_step, None, (all_rows.reshape(group_count, group_rows, model_width), all_cond.reshape(group_count, slots_group, model_width), big_all))
        return outputs.reshape(-1, model_width)
    result, back_fn = jax.vjp(whole_block, block_input.astype(jnp.float32), condition, ada_weight.astype(jnp.float32), ada_bias.astype(jnp.float32), proj_weight.astype(jnp.float32), decay_down.astype(jnp.float32), decay_up.astype(jnp.float32), decay_bias.astype(jnp.float32), head_gain.astype(jnp.float32), conv_taps.astype(jnp.float32), out_weight.astype(jnp.float32), fc1_weight.astype(jnp.float32), fc2_weight.astype(jnp.float32))
    grads = back_fn(out_grad.astype(jnp.float32))
    return (result.astype(jnp.bfloat16), grads[0], grads[1], grads[2], grads[3], grads[4], grads[5], grads[6], grads[7], grads[8], grads[9], grads[10], grads[11], grads[12])
```

```python
import functools
import math

import jax
import jax.numpy as jnp
from jax import lax
from jax.experimental import pallas as pl
from jax.experimental.pallas import tpu as pltpu
from jax.sharding import Mesh
from jax.sharding import PartitionSpec as P

f32=jnp.float32; bf16=jnp.bfloat16
HDIM=72; SIDE=16; LANES=128; CHUNK=128; MARGIN=64
LEVELS=(64,32,16,8,4,2,1)
GATE_NORM=16.0; head_eps=1e-5
LOG2E=math.log2(math.e)

def parts(x, n):
    out=[]
    for _ in range(n-1):
        p=x.astype(bf16); out.append(p); x=x-p.astype(f32)
    out.append(x.astype(bf16)); return out

def mm(a,b,ca,cb):
    return lax.dot_general(a,b,(((ca,),(cb,)),((),())),preferred_element_type=f32)

def mmx(a,b,ca,cb,n):
    if n==1: return mm(a.astype(bf16),b.astype(bf16),ca,cb)
    ah,al=parts(a,2); bh,bl=parts(b,2)
    return mm(ah,bh,ca,cb)+(mm(ah,bl,ca,cb)+mm(al,bh,ca,cb))

def sel_mm(m,x,n):
    ps=parts(x,n)
    r=mm(m,ps[-1],1,0)
    for p in ps[-2::-1]: r=mm(m,p,1,0)+r
    return r

def iota2(shape,d): return lax.broadcasted_iota(jnp.int32,shape,d)

def level_matrix():
    i=iota2((CHUNK,CHUNK),0); j=iota2((CHUNK,CHUNK),1)
    x=i^j
    lvl=jnp.zeros((CHUNK,CHUNK),jnp.int32)
    for b in LEVELS[::-1]: lvl=jnp.where(x>=b,b,lvl)
    return lvl,i,j

def level_ops(q,k,L,lw):
    row=iota2((CHUNK,LANES),0)
    out=[]
    for b in LEVELS:
        n=CHUNK//(2*b)
        if b>=8:
            L3=L.reshape(n,2*b,LANES); D=L3-L3[:,b-1:b,:]
            E=jnp.exp2(-jnp.abs(D)).reshape(CHUNK,LANES)
            q3=q.reshape(n,2*b,LANES); k3=k.reshape(n,2*b,LANES)
            X=jnp.concatenate([k3[:,:b],q3[:,b:]],axis=1).reshape(CHUNK,LANES)
        else:
            right=(row&b)!=0
            X=jnp.where(right,q,k)
            L3=L.reshape(CHUNK//8,8,LANES)
            if b==4:
                D=(L3-L3[:,3:4,:]).reshape(CHUNK,LANES); E=jnp.exp2(-jnp.abs(D))
            elif b==2:
                s=lax.broadcasted_iota(jnp.int32,L3.shape,1)
                R=jnp.where(s<4,L3[:,1:2,:],L3[:,5:6,:])
                E=jnp.exp2(-jnp.abs(L3-R)).reshape(CHUNK,LANES)
            else:
                E=jnp.exp2(jnp.where(right,lw,0.0))
        out.append((b,E,X*E))
    return out

def log_decay2(pre):
    return (jnp.minimum(pre,0.0)-jnp.log1p(jnp.exp(-jnp.abs(pre))))*(LOG2E/GATE_NORM)

def image_masks(base,rows,width,height):
    p=iota2((rows,LANES),0)+base
    col=p&(width-1)
    r=(p//width)&(height-1)
    return col,r

def conv_forward(vp,up,um,taps,store,total,width,height):
    tiles=total//CHUNK
    for t in range(tiles):
        o=MARGIN+t*CHUNK
        col,_=image_masks(0,CHUNK,width,height)
        c=vp[o:o+CHUNK,:]
        left=jnp.where(col!=0,vp[o-1:o-1+CHUNK,:],0.0)
        right=jnp.where(col!=width-1,vp[o+1:o+1+CHUNK,:],0.0)
        def comb(a): return left*taps[3*a:3*a+1,:]+c*taps[3*a+1:3*a+2,:]+right*taps[3*a+2:3*a+3,:]
        um[o:o+CHUNK,:]=comb(0)
        store(t,comb(1))
        up[o:o+CHUNK,:]=comb(2)

def conv_finish(up,um,add,total,width,height):
    for t in range(total//CHUNK):
        o=MARGIN+t*CHUNK
        _,r=image_masks(t*CHUNK,CHUNK,width,height)
        down=jnp.where(r!=height-1,up[o+width:o+width+CHUNK,:],0.0)
        upv=jnp.where(r!=0,um[o-width:o-width+CHUNK,:],0.0)
        add(t,down+upv)

def fwd_kernel(PS,PA,total,big_ref,q_ref,k_ref,v_ref,g_ref,p_ref,taps_ref,gain_ref,mixed_ref,comb_ref,a_ref,s_ref,vp,up,um,lvl_ref,tri_ref,st):
    chunks=total//CHUNK
    @pl.when(pl.program_id(0)==0)
    def _():
        lvl,i,j=level_matrix()
        lvl_ref[...]=jnp.where(i>j,lvl,jnp.where(i==j,-1,-2))
        tri_ref[...]=jnp.where(i>=j,1.0,0.0).astype(bf16)
        z=jnp.zeros((MARGIN,LANES),f32)
        for r in (vp,up,um):
            r[0:MARGIN,:]=z; r[MARGIN+total:,:]=z
    big=big_ref[0]==4*SIDE*SIDE
    taps=taps_ref[0]; gain=gain_ref[...]
    vp[MARGIN:MARGIN+total,:]=v_ref[0]
    def conv(width):
        def store(t,x): comb_ref[0,t*CHUNK:(t+1)*CHUNK,:]=x
        def add(t,x): comb_ref[0,t*CHUNK:(t+1)*CHUNK,:]+=x
        conv_forward(vp,up,um,taps,store,total,width,width)
        conv_finish(up,um,add,total,width,width)
    @pl.when(big)
    def _(): conv(2*SIDE)
    @pl.when(jnp.logical_not(big))
    def _(): conv(SIDE)
    per=SIDE*SIDE//CHUNK
    def step(c,_):
        rows=pl.ds(pl.multiple_of(c*CHUNK,CHUNK),CHUNK)
        start=jnp.where(big,c==0,lax.rem(c,per)==0)
        S=jnp.where(start,0.0,st[...])
        s_ref[0,c]=S
        q=q_ref[0,rows,:]*(HDIM**-0.5); k=k_ref[0,rows,:]; v=v_ref[0,rows,:]
        lw=log_decay2(p_ref[0,rows,:])
        L=sel_mm(tri_ref[...],lw,3)
        lvl=lvl_ref[...]
        diag=jnp.sum(q*k,axis=1,keepdims=True)
        A=jnp.where(lvl==-1,diag,0.0)
        for b,E,W in level_ops(q,k,L,lw):
            A=jnp.where(lvl==b,mmx(W,W,1,1,PS),A)
        a_ref[0,c]=A.astype(a_ref.dtype)
        last=L[CHUNK-1:CHUNK,:]
        o=mmx(A,v,1,0,PA)+mmx(q*jnp.exp2(L),S,1,1,PA)
        st[...]=S*jnp.exp2(last)+mmx(v,k*jnp.exp2(last-L),0,0,PA)
        cb=comb_ref[0,rows,:]+o
        comb_ref[0,rows,:]=cb
        g=g_ref[0,rows,:]
        r=lax.rsqrt(jnp.sum(cb*cb,axis=1,keepdims=True)*(1.0/HDIM)+head_eps)
        mixed_ref[0,rows,:]=(cb*r*gain*(g/(1.0+jnp.exp(-g)))).astype(bf16)
        return 0
    lax.fori_loop(0,chunks,step,0)

def gla_forward(big,qkvg,pre,taps,gain,PS=2,PA=2,adt=f32):
    _,H,total,_=qkvg.shape; chunks=total//CHUNK
    row=pl.BlockSpec((1,total,LANES),lambda h:(h,0,0))
    def of(i): return pl.BlockSpec((None,1,total,LANES),lambda h:(i,h,0,0))
    return pl.pallas_call(
        functools.partial(fwd_kernel,PS,PA,total),
        grid=(H,),
        in_specs=[pl.BlockSpec(memory_space=pltpu.SMEM)]+[of(i) for i in range(4)]+[row]+[pl.BlockSpec((1,16,LANES),lambda h:(h,0,0)),pl.BlockSpec((1,LANES),lambda h:(0,0))],
        out_specs=[row,row,pl.BlockSpec((1,chunks,CHUNK,CHUNK),lambda h:(h,0,0,0)),pl.BlockSpec((1,chunks,LANES,LANES),lambda h:(h,0,0,0))],
        out_shape=[jax.ShapeDtypeStruct((H,total,LANES),bf16),jax.ShapeDtypeStruct((H,total,LANES),f32),
                   jax.ShapeDtypeStruct((H,chunks,CHUNK,CHUNK),adt),jax.ShapeDtypeStruct((H,chunks,LANES,LANES),f32)],
        scratch_shapes=[pltpu.VMEM((total+2*MARGIN,LANES),f32)]*3+[pltpu.VMEM((CHUNK,CHUNK),jnp.int32),pltpu.VMEM((CHUNK,CHUNK),bf16),pltpu.VMEM((LANES,LANES),f32)],
        compiler_params=pltpu.CompilerParams(vmem_limit_bytes=40*2**20,dimension_semantics=("arbitrary",)),
        name="gla_forward",
    )(big,qkvg,qkvg,qkvg,qkvg,pre,taps,gain)

def bwd_kernel(PS,PA,total,big_ref,q_ref,k_ref,v_ref,g_ref,p_ref,comb_ref,a_ref,s_ref,gm_ref,taps_ref,gain_ref,
               dqk_ref,dpre_ref,dtaps_ref,dvec_ref,vp,dcp,gl,gr,dvl,lvl_ref,tri_ref,ds,car):
    chunks=total//CHUNK
    @pl.when(pl.program_id(0)==0)
    def _():
        lvl,i,j=level_matrix()
        lvl_ref[...]=jnp.where(i==j,-1,lvl)
        tri_ref[0]=jnp.where(i>=j,1.0,0.0).astype(bf16)
        tri_ref[1]=jnp.where(i<=j,1.0,0.0).astype(bf16)
        z=jnp.zeros((MARGIN,LANES),f32)
        for r in (vp,dcp,gl,gr):
            r[0:MARGIN,:]=z; r[MARGIN+total:,:]=z
    big=big_ref[0]==4*SIDE*SIDE
    taps=taps_ref[0]; gain=gain_ref[...]
    vp[MARGIN:MARGIN+total,:]=v_ref[0]
    def rowwise(c,acc):
        rows=pl.ds(pl.multiple_of(c*CHUNK,CHUNK),CHUNK)
        cb=comb_ref[0,rows,:]; g=g_ref[0,rows,:]; gm=gm_ref[0,rows,:].astype(f32)
        r=lax.rsqrt(jnp.sum(cb*cb,axis=1,keepdims=True)*(1.0/HDIM)+head_eps)
        n=cb*r
        sg=1.0/(1.0+jnp.exp(-g)); silu=g*sg
        dqk_ref[3,0,rows,:]=(gm*n*gain*(sg+silu*(1.0-sg))).astype(bf16)
        dn=gm*silu
        acc=acc+jnp.sum((dn*n).reshape(CHUNK//8,8,LANES),axis=0)
        dn=dn*gain
        dc=r*(dn-n*(jnp.sum(dn*n,axis=1,keepdims=True)*(1.0/HDIM)))
        dcp[pl.ds(pl.multiple_of(MARGIN+c*CHUNK,MARGIN),CHUNK),:]=dc
        return acc
    dgain=lax.fori_loop(0,chunks,rowwise,jnp.zeros((8,LANES),f32))
    dvec_ref[0,0:1,:]=jnp.sum(dgain,axis=0,keepdims=True)
    def conv(width):
        height=width
        accs=[jnp.zeros((8,LANES),f32) for _ in range(9)]
        for t in range(chunks):
            o=MARGIN+t*CHUNK
            col,r=image_masks(t*CHUNK,CHUNK,width,height)
            zs=[jnp.where(r!=height-1,dcp[o+width:o+width+CHUNK,:],0.0),dcp[o:o+CHUNK,:],jnp.where(r!=0,dcp[o-width:o-width+CHUNK,:],0.0)]
            vs=[jnp.where(col!=0,vp[o-1:o-1+CHUNK,:],0.0),vp[o:o+CHUNK,:],jnp.where(col!=width-1,vp[o+1:o+1+CHUNK,:],0.0)]
            for a in range(3):
                for b in range(3):
                    accs[3*a+b]=accs[3*a+b]+jnp.sum((zs[a]*vs[b]).reshape(CHUNK//8,8,LANES),axis=0)
            def comb(b): return zs[0]*taps[b:b+1,:]+zs[1]*taps[3+b:4+b,:]+zs[2]*taps[6+b:7+b,:]
            gl[o:o+CHUNK,:]=comb(0)
            dvl[t*CHUNK:(t+1)*CHUNK,:]=comb(1)
            gr[o:o+CHUNK,:]=comb(2)
        for i in range(9):
            dtaps_ref[0,i:i+1,:]=jnp.sum(accs[i],axis=0,keepdims=True)
        for t in range(chunks):
            o=MARGIN+t*CHUNK
            col,_=image_masks(0,CHUNK,width,height)
            dvl[t*CHUNK:(t+1)*CHUNK,:]+=jnp.where(col!=width-1,gl[o+1:o+1+CHUNK,:],0.0)+jnp.where(col!=0,gr[o-1:o-1+CHUNK,:],0.0)
    @pl.when(big)
    def _(): conv(2*SIDE)
    @pl.when(jnp.logical_not(big))
    def _(): conv(SIDE)
    per=SIDE*SIDE//CHUNK
    row=iota2((CHUNK,LANES),0)
    def step(i,acc):
        c=chunks-1-i
        rows=pl.ds(pl.multiple_of(c*CHUNK,CHUNK),CHUNK)
        end=jnp.where(big,c==chunks-1,lax.rem(c,per)==per-1)
        dS=jnp.where(end,0.0,ds[...])
        carry=jnp.where(end,0.0,car[0:1,:])
        q=q_ref[0,rows,:]*(HDIM**-0.5); k=k_ref[0,rows,:]; v=v_ref[0,rows,:]
        pre=p_ref[0,rows,:]
        lw=log_decay2(pre)
        L=sel_mm(tri_ref[0],lw,3)
        do=dcp[pl.ds(pl.multiple_of(MARGIN+c*CHUNK,MARGIN),CHUNK),:]
        lvl=lvl_ref[...]
        low=tri_ref[0].astype(f32)>0.5
        G=jnp.where(low,mmx(do,v,1,1,PS),mmx(v,do,1,1,PS))
        last=L[CHUNK-1:CHUNK,:]
        eL=jnp.exp2(L); eR=jnp.exp2(last-L)
        S=s_ref[0,c]
        dq=eL*mmx(do,S,1,0,PA)
        kR=k*eR
        dk=eR*mmx(v,dS,1,0,PA)
        dv=dvl[rows,:]+mmx(a_ref[0,c].astype(f32),do,0,0,PA)+mmx(kR,dS,1,1,PA)
        ds[...]=dS*jnp.exp2(last)+mmx(do,q*eL,0,0,PA)
        for b,E,W in level_ops(q,k,L,lw):
            Y=E*mmx(jnp.where(lvl==b,G,0.0),W,1,0,PS)
            right=(row&b)!=0
            dq=dq+jnp.where(right,Y,0.0); dk=dk+jnp.where(right,0.0,Y)
        z=q*dq-k*dk
        suf=sel_mm(tri_ref[1],z,3)+carry
        car[0:1,:]=suf[0:1,:]
        dp=suf*((1.0/GATE_NORM)/(1.0+jnp.exp(pre)))
        dpre_ref[0,rows,:]=dp
        t=jnp.sum(do*v,axis=1,keepdims=True)
        dqk_ref[0,0,rows,:]=((dq+t*k)*(HDIM**-0.5)).astype(bf16)
        dqk_ref[1,0,rows,:]=(dk+t*q).astype(bf16)
        dqk_ref[2,0,rows,:]=dv.astype(bf16)
        return acc+jnp.sum(dp.reshape(CHUNK//8,8,LANES),axis=0)
    db=lax.fori_loop(0,chunks,step,jnp.zeros((8,LANES),f32))
    dvec_ref[0,1:2,:]=jnp.sum(db,axis=0,keepdims=True)

def gla_backward(big,qkvg,pre,comb,A,S,gm,taps,gain,PS=2,PA=2):
    _,H,total,_=qkvg.shape; chunks=total//CHUNK
    row=pl.BlockSpec((1,total,LANES),lambda h:(h,0,0))
    def of(i): return pl.BlockSpec((None,1,total,LANES),lambda h:(i,h,0,0))
    return pl.pallas_call(
        functools.partial(bwd_kernel,PS,PA,total),
        grid=(H,),
        in_specs=[pl.BlockSpec(memory_space=pltpu.SMEM)]+[of(i) for i in range(4)]+[row]*2+[pl.BlockSpec((1,chunks,CHUNK,CHUNK),lambda h:(h,0,0,0)),pl.BlockSpec((1,chunks,LANES,LANES),lambda h:(h,0,0,0)),row,
                  pl.BlockSpec((1,16,LANES),lambda h:(h,0,0)),pl.BlockSpec((1,LANES),lambda h:(0,0))],
        out_specs=[pl.BlockSpec((4,1,total,LANES),lambda h:(0,h,0,0)),row,pl.BlockSpec((1,16,LANES),lambda h:(h,0,0)),pl.BlockSpec((1,8,LANES),lambda h:(h,0,0))],
        out_shape=[jax.ShapeDtypeStruct((4,H,total,LANES),bf16),jax.ShapeDtypeStruct((H,total,LANES),f32),
                   jax.ShapeDtypeStruct((H,16,LANES),f32),jax.ShapeDtypeStruct((H,8,LANES),f32)],
        scratch_shapes=[pltpu.VMEM((total+2*MARGIN,LANES),f32)]*4+[pltpu.VMEM((total,LANES),f32),pltpu.VMEM((CHUNK,CHUNK),jnp.int32),pltpu.VMEM((2,CHUNK,CHUNK),bf16),pltpu.VMEM((LANES,LANES),f32),pltpu.VMEM((8,LANES),f32)],
        compiler_params=pltpu.CompilerParams(vmem_limit_bytes=48*2**20,dimension_semantics=("arbitrary",)),
        name="gla_backward",
    )(big,qkvg,qkvg,qkvg,qkvg,pre,comb,A,S,gm,taps,gain)


ROWS = 256


def head_window(res, column):
    base = column // LANES * LANES
    off = column - base
    width = LANES if off + HDIM <= LANES else 2 * LANES
    part = res[:, base : base + width]
    if off:
        part = pltpu.roll(part, width - off, 1)
    part = part[:, :LANES]
    return jnp.where(iota2(part.shape, 1) < HDIM, part, 0.0)


def heads_joined(pieces):
    blocks = [None] * (len(pieces) * HDIM // LANES + 1)

    def put(index, value):
        blocks[index] = value if blocks[index] is None else blocks[index] + value

    for h, x in enumerate(pieces):
        index, off = h * HDIM // LANES, h * HDIM % LANES
        if off == 0:
            put(index, x)
            continue
        r = pltpu.roll(x, off, 1)
        if off + HDIM <= LANES:
            put(index, r)
        else:
            lane = iota2(r.shape, 1)
            put(index, jnp.where(lane >= off, r, 0.0))
            put(index + 1, jnp.where(lane < off, r, 0.0))
    total = len(pieces) * HDIM
    blocks = [b for b in blocks if b is not None]
    return jnp.concatenate(blocks, axis=1)[:, :total]


def project_kernel(H, turn_ref, x_ref, w_ref, down_ref, up_ref, bias_ref, out_ref, pre_ref, lat_ref):
    x = x_ref[...]
    span = 2 * H * HDIM
    for s in range(2):
        res = mm(x, w_ref[:, s * span : (s + 1) * span], 1, 0)
        for i in range(2 * H):
            out_ref[2 * s + i // H, i % H] = head_window(res, i * HDIM)
    latent = mm(x, down_ref[...], 1, 0)
    lat_ref[...] = latent
    pre = bias_ref[...] + sum(mm(p, up_ref[...], 1, 0) for p in parts(latent, 3)[::-1])
    for h in range(H):
        pre_ref[h] = pre[:, h * LANES : (h + 1) * LANES]


def project(turn, x, w, down, up, bias, H):
    total, width = x.shape
    tiles = total // ROWS

    def turned(i, t):
        return lax.rem(i + t[0], tiles)

    full = lambda a: pl.BlockSpec(a.shape, lambda i, t: (0, 0))
    return pl.pallas_call(
        functools.partial(project_kernel, H),
        grid_spec=pltpu.PrefetchScalarGridSpec(
            num_scalar_prefetch=1,
            grid=(tiles,),
            in_specs=[pl.BlockSpec((ROWS, width), lambda i, t: (i, 0)), full(w), full(down), full(up), full(bias)],
            out_specs=[
                pl.BlockSpec((4, H, ROWS, LANES), lambda i, t: (0, 0, turned(i, t), 0)),
                pl.BlockSpec((H, ROWS, LANES), lambda i, t: (0, turned(i, t), 0)),
                pl.BlockSpec((ROWS, LANES), lambda i, t: (turned(i, t), 0)),
            ],
        ),
        out_shape=[
            jax.ShapeDtypeStruct((4, H, total, LANES), f32),
            jax.ShapeDtypeStruct((H, total, LANES), f32),
            jax.ShapeDtypeStruct((total, LANES), f32),
        ],
        compiler_params=pltpu.CompilerParams(vmem_limit_bytes=56 * 2**20, dimension_semantics=("arbitrary",)),
        name="project",
    )(turn, x, w, down, up, bias)


def attend_kernel(H, turn_ref, m_ref, w_ref, out_ref, cat_ref):
    cat = heads_joined([m_ref[h].astype(f32) for h in range(H)]).astype(bf16)
    cat_ref[...] = cat
    out_ref[...] = mm(cat, w_ref[...], 1, 1)


def attend(turn, mixed, w):
    H, total, _ = mixed.shape
    tiles = total // ROWS
    inner = H * HDIM
    return pl.pallas_call(
        functools.partial(attend_kernel, H),
        grid_spec=pltpu.PrefetchScalarGridSpec(
            num_scalar_prefetch=1,
            grid=(tiles,),
            in_specs=[
                pl.BlockSpec((H, ROWS, LANES), lambda i, t: (0, lax.rem(i + t[0], tiles), 0)),
                pl.BlockSpec(w.shape, lambda i, t: (0, 0)),
            ],
            out_specs=[pl.BlockSpec((ROWS, w.shape[0]), lambda i, t: (i, 0)), pl.BlockSpec((ROWS, inner), lambda i, t: (i, 0))],
        ),
        out_shape=[jax.ShapeDtypeStruct((total, w.shape[0]), f32), jax.ShapeDtypeStruct((total, inner), bf16)],
        compiler_params=pltpu.CompilerParams(vmem_limit_bytes=40 * 2**20, dimension_semantics=("arbitrary",)),
        name="attend",
    )(turn, mixed, w)


def attend_back_kernel(H, turn_ref, g_ref, w_ref, out_ref):
    res = mm(g_ref[...], w_ref[...], 1, 0)
    res = jnp.concatenate([res, jnp.zeros((ROWS, -res.shape[1] % LANES), f32)], axis=1)
    for h in range(H):
        out_ref[h] = head_window(res, h * HDIM)


def attend_back(turn, grad, w, H):
    total, width = grad.shape
    tiles = total // ROWS
    return pl.pallas_call(
        functools.partial(attend_back_kernel, H),
        grid_spec=pltpu.PrefetchScalarGridSpec(
            num_scalar_prefetch=1,
            grid=(tiles,),
            in_specs=[pl.BlockSpec((ROWS, width), lambda i, t: (i, 0)), pl.BlockSpec(w.shape, lambda i, t: (0, 0))],
            out_specs=pl.BlockSpec((H, ROWS, LANES), lambda i, t: (0, lax.rem(i + t[0], tiles), 0)),
        ),
        out_shape=jax.ShapeDtypeStruct((H, total, LANES), f32),
        compiler_params=pltpu.CompilerParams(vmem_limit_bytes=40 * 2**20, dimension_semantics=("arbitrary",)),
        name="attend_back",
    )(turn, grad, w)


def project_back_kernel(H, turn_ref, d_ref, p_ref, lat_ref, w_ref, down_ref, up_ref, out_ref, cat_ref, glat_ref, dup_ref):
    @pl.when(pl.program_id(0) == 0)
    def _():
        dup_ref[...] = jnp.zeros_like(dup_ref)

    lat = parts(lat_ref[...], 2)
    glat = jnp.zeros((ROWS, LANES), f32)
    for h in range(H):
        dp = parts(p_ref[h], 3)
        up = up_ref[:, h * LANES : (h + 1) * LANES]
        glat = glat + (mm(dp[2], up, 1, 1) + mm(dp[1], up, 1, 1) + mm(dp[0], up, 1, 1))
        dup_ref[h] += mm(lat[0], dp[1], 0, 0) + mm(lat[1], dp[0], 0, 0) + mm(lat[0], dp[0], 0, 0)
    glat_ref[...] = glat
    span = 2 * H * HDIM
    acc = sum(mm(p, down_ref[...], 1, 1) for p in parts(glat, 2)[::-1])
    for s in range(2):
        cat = heads_joined([d_ref[2 * s + i // H, i % H].astype(f32) for i in range(2 * H)]).astype(bf16)
        cat_ref[:, s * span : (s + 1) * span] = cat
        acc = acc + mm(cat, w_ref[:, s * span : (s + 1) * span], 1, 1)
    out_ref[...] = acc


def project_back(turn, d, dpre, latent, w, down, up):
    _, H, total, _ = d.shape
    tiles = total // ROWS
    width, cols = w.shape

    def turned(i, t):
        return lax.rem(i + t[0], tiles)

    full = lambda a: pl.BlockSpec(a.shape, lambda i, t: (0, 0))
    return pl.pallas_call(
        functools.partial(project_back_kernel, H),
        grid_spec=pltpu.PrefetchScalarGridSpec(
            num_scalar_prefetch=1,
            grid=(tiles,),
            in_specs=[
                pl.BlockSpec((4, H, ROWS, LANES), lambda i, t: (0, 0, turned(i, t), 0)),
                pl.BlockSpec((H, ROWS, LANES), lambda i, t: (0, turned(i, t), 0)),
                pl.BlockSpec((ROWS, LANES), lambda i, t: (turned(i, t), 0)),
                full(w), full(down), full(up),
            ],
            out_specs=[
                pl.BlockSpec((ROWS, width), lambda i, t: (i, 0)),
                pl.BlockSpec((ROWS, cols), lambda i, t: (i, 0)),
                pl.BlockSpec((ROWS, LANES), lambda i, t: (i, 0)),
                pl.BlockSpec((H, LANES, LANES), lambda i, t: (0, 0, 0)),
            ],
        ),
        out_shape=[
            jax.ShapeDtypeStruct((total, width), f32),
            jax.ShapeDtypeStruct((total, cols), bf16),
            jax.ShapeDtypeStruct((total, LANES), f32),
            jax.ShapeDtypeStruct((H, LANES, LANES), f32),
        ],
        compiler_params=pltpu.CompilerParams(vmem_limit_bytes=56 * 2**20, dimension_semantics=("arbitrary",)),
        name="project_back",
    )(turn, d, dpre, latent, w, down, up)


NORM_EPS = 1e-06
FLIP = [(0, 1), (1, 0)]
EVERY = ("dq", "mp")
COLUMNS = ("dq", "core")


def swap(x):
    return lax.ppermute(x, ("core", "mp"), [(0, 0), (1, 2), (2, 1), (3, 3)])


def other(x):
    return lax.ppermute(x, "core", FLIP)


def both(x):
    return jnp.concatenate([x, other(x)], axis=0)


def summed(x):
    half = x.shape[0] // 2
    return x[:half] + other(x[half:])


def gathered(x):
    return lax.all_gather(x, EVERY, axis=0, tiled=True)


def reduced(x):
    return lax.psum_scatter(x.astype(bf16), EVERY, scatter_dimension=0, tiled=True).astype(f32)


def modulate(rows, shift, scale):
    center = rows - jnp.mean(rows, axis=-1, keepdims=True)
    normed = center * lax.rsqrt(jnp.mean(center * center, axis=-1, keepdims=True) + NORM_EPS)
    return normed * (1.0 + scale[:, None, :]) + shift[:, None, :]


def per_head(x, heads, rows):
    x = x.reshape(x.shape[0], heads, HDIM)
    return jnp.pad(x, ((0, rows - x.shape[0]), (0, 0), (0, LANES - HDIM)))


def contract(a, b, i, j):
    return lax.dot_general(a, b, (((i,), (j,)), ((), ())), preferred_element_type=f32)


def silu(v):
    return v * jax.nn.sigmoid(v)


def on_device(
    block_input, out_grad, time_table, class_table, time_ids, class_ids, image_patches, ada_weight, ada_bias,
    proj_weight, decay_down, decay_up, decay_bias, head_gain, conv_taps, out_weight, fc1_weight, fc2_weight,
):
    rows, width = block_input.shape
    inner = proj_weight.shape[2]
    heads = inner // HDIM
    core = lax.axis_index("core")
    y = lax.axis_index("mp")
    dq = lax.axis_size("dq")
    slot_rows = SIDE * SIDE
    own_slots = rows // slot_rows
    unit_slots = 2 * own_slots

    w_proj = gathered(swap(proj_weight.transpose(1, 0, 2).reshape(-1, 4 * inner)))
    x = swap(block_input)
    w_out = gathered(swap(out_weight.T))
    w_fc1 = gathered(swap(fc1_weight))
    w_fc2 = gathered(swap(fc2_weight.T))
    g_rows = swap(out_grad)

    ids = jnp.concatenate([time_ids, class_ids, image_patches])[None]
    ids = lax.all_to_all(jnp.broadcast_to(ids, (2 * dq, ids.shape[1])), COLUMNS, split_axis=0, concat_axis=0, tiled=True)
    t_all, c_all = ids[:, :unit_slots].reshape(-1), ids[:, unit_slots : 2 * unit_slots].reshape(-1)
    big_all = ids[:, 2 * unit_slots] == 4 * slot_rows
    me = 2 * lax.axis_index("dq") + y
    patches = lax.dynamic_slice_in_dim(ids[:, 2 * unit_slots], me, 1)
    condition = time_table[t_all].astype(f32) + class_table[c_all].astype(f32)
    silu_all = silu(condition).astype(bf16)
    columns = jnp.dot(silu_all, ada_weight, preferred_element_type=f32) + ada_bias.astype(f32)
    part = columns.shape[1]
    columns = columns.reshape(2 * dq, unit_slots, part)
    columns = jnp.where(big_all[:, None, None], columns[:, :1], columns)
    columns = lax.dynamic_index_in_dim(columns.reshape(dq, 2, 2, own_slots, part), y, 1, keepdims=False)
    columns = lax.all_to_all(columns.reshape(2 * dq, own_slots, part), COLUMNS, split_axis=0, concat_axis=0, tiled=True)
    modulation = columns.transpose(1, 0, 2).reshape(own_slots, 6 * width)
    shift1, scale1, gate1, shift2, scale2, gate2 = jnp.split(modulation, 6, axis=1)

    start = core * inner
    up_local = lax.dynamic_slice_in_dim(decay_up, start, inner, 1)
    bias_local = lax.dynamic_slice_in_dim(decay_bias, start, inner, 0)
    taps_local = lax.dynamic_slice_in_dim(conv_taps, start, inner, 1)
    lowrank = decay_down.shape[1]
    down_pad = jnp.pad(decay_down, ((0, 0), (0, LANES - lowrank)))
    up_pad = per_head(up_local, heads, LANES).reshape(LANES, heads * LANES)
    bias_pad = per_head(bias_local[None].astype(f32), heads, 1).reshape(1, heads * LANES)
    taps_pad = per_head(taps_local.astype(f32), heads, 16).transpose(1, 0, 2)
    gain_pad = jnp.pad(head_gain.astype(f32), (0, LANES - HDIM))[None]
    turn = (core * (rows // ROWS)).astype(jnp.int32)[None]

    residual = x.astype(f32).reshape(own_slots, slot_rows, width)
    hidden, norm_back_one = jax.vjp(modulate, residual, shift1, scale1)
    hidden_all = both(hidden.reshape(rows, width).astype(bf16))
    qkvg, pre, latent = project(turn, hidden_all, w_proj, down_pad, up_pad, bias_pad, heads)
    mixed, comb, scores, states = gla_forward(patches, qkvg, pre, taps_pad, gain_pad)
    attn_part, mixed_cat = attend(turn, mixed, w_out)
    attention = summed(attn_part).reshape(own_slots, slot_rows, width)
    after_attn = residual + gate1[:, None, :] * attention
    hidden_two, norm_back_two = jax.vjp(modulate, after_attn, shift2, scale2)
    hidden_two_all = both(hidden_two.reshape(rows, width).astype(bf16))
    up_proj = jnp.dot(hidden_two_all, w_fc1, preferred_element_type=f32)
    active, gelu_back = jax.vjp(functools.partial(jax.nn.gelu, approximate=True), up_proj)
    active_low = active.astype(bf16)
    feed_out = summed(contract(active_low, w_fc2, 1, 1)).reshape(own_slots, slot_rows, width)
    result = after_attn + gate2[:, None, :] * feed_out
    block_out = swap(result.reshape(rows, width).astype(bf16))

    grad_rows = g_rows.astype(f32).reshape(own_slots, slot_rows, width)
    grad_gate_two = jnp.sum(grad_rows * feed_out, axis=1)
    grad_feed_all = both((grad_rows * gate2[:, None, :]).astype(bf16).reshape(rows, width))
    grad_active = jnp.dot(grad_feed_all, w_fc2, preferred_element_type=f32)
    grad_fc2 = reduced(contract(grad_feed_all, active_low, 0, 0))
    grad_up = gelu_back(grad_active)[0].astype(bf16)
    grad_fc1 = reduced(contract(hidden_two_all, grad_up, 0, 0))
    grad_hidden_two = summed(contract(grad_up, w_fc1, 1, 1))
    grad_after, grad_shift_two, grad_scale_two = norm_back_two(grad_hidden_two.reshape(own_slots, slot_rows, width))
    grad_after = grad_after + grad_rows
    grad_gate_one = jnp.sum(grad_after * attention, axis=1)
    grad_attn_all = both((grad_after * gate1[:, None, :]).astype(bf16).reshape(rows, width))
    grad_mixed = attend_back(turn, grad_attn_all, w_out, heads)
    grad_out = reduced(contract(grad_attn_all, mixed_cat, 0, 0))
    d_qkvg, d_pre, d_taps, d_vec = gla_backward(patches, qkvg, pre, comb, scores, states, grad_mixed, taps_pad, gain_pad)
    hidden_part, d_cat, grad_latent, d_up = project_back(turn, d_qkvg, d_pre, latent, w_proj, down_pad, up_pad)
    grad_proj = reduced(contract(hidden_all, d_cat, 0, 0))
    grad_residual, grad_shift_one, grad_scale_one = norm_back_one(summed(hidden_part).reshape(own_slots, slot_rows, width))
    input_grad = swap((grad_residual + grad_after).reshape(rows, width))

    lat_hi = grad_latent[:, :lowrank].astype(bf16)
    lat_lo = (grad_latent[:, :lowrank] - lat_hi.astype(f32)).astype(bf16)
    d_down = contract(hidden_all, jnp.concatenate([lat_hi, lat_lo], axis=1), 0, 0)
    d_down = d_down[:, :lowrank] + d_down[:, lowrank:]

    def placed(value):
        return lax.dynamic_update_slice_in_dim(jnp.zeros((value.shape[0], width), f32), value, start, 1)

    d_up = d_up[:, :lowrank, :HDIM].transpose(1, 0, 2).reshape(lowrank, inner)
    d_taps = d_taps[:, :9, :HDIM].transpose(1, 0, 2).reshape(9, inner)
    d_bias = d_vec[:, 1, :HDIM].reshape(1, inner)
    d_gain = jnp.sum(d_vec[:, 0, :HDIM], axis=0)
    stacked = placed(jnp.concatenate([d_up, d_taps, d_bias], axis=0))
    flat = jnp.concatenate([d_down.reshape(lowrank, width), stacked, jnp.pad(d_gain, (0, width - HDIM))[None]], axis=0)
    for bit in range(dq.bit_length() - 1):
        flat = flat + lax.ppermute(flat, "dq", [(i, i ^ (1 << bit)) for i in range(dq)])
    flat = flat + lax.ppermute(flat, "mp", FLIP)
    flat = flat + other(flat)
    down_sum = flat[:lowrank].reshape(width, lowrank)
    up_sum = flat[lowrank : 2 * lowrank]
    taps_sum = flat[2 * lowrank : 2 * lowrank + 9]
    bias_sum = flat[2 * lowrank + 9]
    gain_sum = flat[2 * lowrank + 10, :HDIM]

    grad_mod = jnp.concatenate(
        [grad_shift_one, grad_scale_one, grad_gate_one, grad_shift_two, grad_scale_two, grad_gate_two], axis=1
    ).astype(bf16)
    grad_mod = grad_mod.reshape(own_slots, 2 * dq, part).transpose(1, 0, 2)
    got = lax.all_to_all(grad_mod, COLUMNS, split_axis=0, concat_axis=0, tiled=True).reshape(dq, 1, unit_slots, part)
    away = lax.ppermute(got, "mp", FLIP)
    got = jnp.where(y == 0, jnp.concatenate([got, away], axis=1), jnp.concatenate([away, got], axis=1))
    got = got.reshape(2 * dq, unit_slots, part).astype(f32)
    folded = jnp.sum(got, axis=1, keepdims=True)
    first = jnp.arange(unit_slots)[None, :, None] == 0
    got = jnp.where(big_all[:, None, None], jnp.where(first, folded, 0.0), got).reshape(-1, part)
    ada_bias_grad = jnp.sum(got, axis=0)
    ada_weight_grad = jnp.dot(silu_all.astype(f32).T, got, precision=lax.Precision.HIGHEST, preferred_element_type=f32)
    grad_silu = jnp.dot(got, ada_weight.astype(f32).T, precision=lax.Precision.HIGHEST, preferred_element_type=f32)
    grad_silu = lax.all_to_all(grad_silu, COLUMNS, split_axis=0, concat_axis=0, tiled=True)
    grad_silu = jnp.sum(grad_silu.reshape(2 * dq, unit_slots, width), axis=0)
    own_cond = time_table[time_ids].astype(f32) + class_table[class_ids].astype(f32)
    gate = jax.nn.sigmoid(own_cond)
    cond_grad = grad_silu * (gate * (1.0 + own_cond * (1.0 - gate)))

    proj_grad = swap(grad_proj).reshape(-1, 4, inner).transpose(1, 0, 2)
    return (
        block_out, input_grad, cond_grad, ada_weight_grad, ada_bias_grad, proj_grad, down_sum, up_sum, bias_sum,
        gain_sum, taps_sum, swap(grad_out).T, swap(grad_fc1), swap(grad_fc2).T,
    )


def solution(mesh):
    dp, mp = mesh.shape["dp"], mesh.shape["mp"]
    split = Mesh(mesh.devices.reshape(dp // 2, 2, mp), ("dq", "core", "mp"))
    d = ("dq", "core")
    every = ("dq", "core", "mp")
    return jax.shard_map(
        on_device,
        mesh=split,
        in_specs=(
            P(every, None), P(every, None), P(), P(), P(d), P(d), P(d), P(None, d), P(d), P(None, d, "mp"),
            P(), P(), P(), P(), P(), P("mp", d), P(d, "mp"), P("mp", d),
        ),
        out_specs=(
            P(every, None), P(every, None), P(d, None), P(None, d), P(d), P(None, d, "mp"),
            P(), P(), P(), P(), P(), P("mp", d), P(d, "mp"), P("mp", d),
        ),
        check_vma=False,
    )
```

```python
import functools
import math

import jax
import jax.numpy as jnp
from jax import lax
from jax.experimental import pallas as pl
from jax.experimental.pallas import tpu as pltpu
from jax.sharding import Mesh
from jax.sharding import PartitionSpec as P

f32=jnp.float32; bf16=jnp.bfloat16
HDIM=72; SIDE=16; LANES=128; CHUNK=128; MARGIN=64
LEVELS=(64,32,16,8,4,2,1)
GATE_NORM=16.0; head_eps=1e-5
LOG2E=math.log2(math.e)

def cost(us):
    return pl.CostEstimate(flops=us*900*10**6, bytes_accessed=10**6, transcendentals=0)

def parts(x, n):
    out=[]
    for _ in range(n-1):
        p=x.astype(bf16); out.append(p); x=x-p.astype(f32)
    out.append(x.astype(bf16)); return out

def mm(a,b,ca,cb):
    return lax.dot_general(a,b,(((ca,),(cb,)),((),())),preferred_element_type=f32)

def mmx(a,b,ca,cb,n):
    if n==1: return mm(a.astype(bf16),b.astype(bf16),ca,cb)
    ah,al=parts(a,2); bh,bl=parts(b,2)
    return mm(ah,bh,ca,cb)+(mm(ah,bl,ca,cb)+mm(al,bh,ca,cb))

def sel_mm(m,x,n):
    ps=parts(x,n)
    r=mm(m,ps[-1],1,0)
    for p in ps[-2::-1]: r=mm(m,p,1,0)+r
    return r

def iota2(shape,d): return lax.broadcasted_iota(jnp.int32,shape,d)

def level_matrix():
    i=iota2((CHUNK,CHUNK),0); j=iota2((CHUNK,CHUNK),1)
    x=i^j
    lvl=jnp.zeros((CHUNK,CHUNK),jnp.int32)
    for b in LEVELS[::-1]: lvl=jnp.where(x>=b,b,lvl)
    return lvl,i,j

def level_ops(q,k,L,lw):
    row=iota2((CHUNK,LANES),0)
    out=[]
    for b in LEVELS:
        n=CHUNK//(2*b)
        if b>=8:
            L3=L.reshape(n,2*b,LANES); D=L3-L3[:,b-1:b,:]
            E=jnp.exp2(-jnp.abs(D)).reshape(CHUNK,LANES)
            q3=q.reshape(n,2*b,LANES); k3=k.reshape(n,2*b,LANES)
            X=jnp.concatenate([k3[:,:b],q3[:,b:]],axis=1).reshape(CHUNK,LANES)
        else:
            right=(row&b)!=0
            X=jnp.where(right,q,k)
            L3=L.reshape(CHUNK//8,8,LANES)
            if b==4:
                D=(L3-L3[:,3:4,:]).reshape(CHUNK,LANES); E=jnp.exp2(-jnp.abs(D))
            elif b==2:
                s=lax.broadcasted_iota(jnp.int32,L3.shape,1)
                R=jnp.where(s<4,L3[:,1:2,:],L3[:,5:6,:])
                E=jnp.exp2(-jnp.abs(L3-R)).reshape(CHUNK,LANES)
            else:
                E=jnp.exp2(jnp.where(right,lw,0.0))
        out.append((b,E,X*E))
    return out

def log_decay2(pre):
    return (jnp.minimum(pre,0.0)-jnp.log1p(jnp.exp(-jnp.abs(pre))))*(LOG2E/GATE_NORM)

def image_masks(base,rows,width,height):
    p=iota2((rows,LANES),0)+base
    col=p&(width-1)
    r=(p//width)&(height-1)
    return col,r

def conv_forward(vp,up,um,taps,store,total,width,height):
    tiles=total//CHUNK
    for t in range(tiles):
        o=MARGIN+t*CHUNK
        col,_=image_masks(0,CHUNK,width,height)
        c=vp[o:o+CHUNK,:]
        left=jnp.where(col!=0,vp[o-1:o-1+CHUNK,:],0.0)
        right=jnp.where(col!=width-1,vp[o+1:o+1+CHUNK,:],0.0)
        def comb(a): return left*taps[3*a:3*a+1,:]+c*taps[3*a+1:3*a+2,:]+right*taps[3*a+2:3*a+3,:]
        um[o:o+CHUNK,:]=comb(0)
        store(t,comb(1))
        up[o:o+CHUNK,:]=comb(2)

def conv_finish(up,um,add,total,width,height):
    for t in range(total//CHUNK):
        o=MARGIN+t*CHUNK
        _,r=image_masks(t*CHUNK,CHUNK,width,height)
        down=jnp.where(r!=height-1,up[o+width:o+width+CHUNK,:],0.0)
        upv=jnp.where(r!=0,um[o-width:o-width+CHUNK,:],0.0)
        add(t,down+upv)

def fwd_kernel(PS,PA,total,big_ref,q_ref,k_ref,v_ref,g_ref,p_ref,taps_ref,gain_ref,mixed_ref,comb_ref,a_ref,s_ref,vp,up,um,lvl_ref,tri_ref,st):
    chunks=total//CHUNK
    @pl.when(pl.program_id(0)==0)
    def _():
        lvl,i,j=level_matrix()
        lvl_ref[...]=jnp.where(i>j,lvl,jnp.where(i==j,-1,-2))
        tri_ref[...]=jnp.where(i>=j,1.0,0.0).astype(bf16)
        z=jnp.zeros((MARGIN,LANES),f32)
        for r in (vp,up,um):
            r[0:MARGIN,:]=z; r[MARGIN+total:,:]=z
    big=big_ref[0]==4*SIDE*SIDE
    taps=taps_ref[0]; gain=gain_ref[...]
    vp[MARGIN:MARGIN+total,:]=v_ref[0]
    def conv(width):
        def store(t,x): comb_ref[0,t*CHUNK:(t+1)*CHUNK,:]=x
        def add(t,x): comb_ref[0,t*CHUNK:(t+1)*CHUNK,:]+=x
        conv_forward(vp,up,um,taps,store,total,width,width)
        conv_finish(up,um,add,total,width,width)
    @pl.when(big)
    def _(): conv(2*SIDE)
    @pl.when(jnp.logical_not(big))
    def _(): conv(SIDE)
    per=SIDE*SIDE//CHUNK
    def step(c,_):
        rows=pl.ds(pl.multiple_of(c*CHUNK,CHUNK),CHUNK)
        start=jnp.where(big,c==0,lax.rem(c,per)==0)
        S=jnp.where(start,0.0,st[...])
        s_ref[0,c]=S
        q=q_ref[0,rows,:]*(HDIM**-0.5); k=k_ref[0,rows,:]; v=v_ref[0,rows,:]
        lw=log_decay2(p_ref[0,rows,:])
        L=sel_mm(tri_ref[...],lw,3)
        lvl=lvl_ref[...]
        diag=jnp.sum(q*k,axis=1,keepdims=True)
        A=jnp.where(lvl==-1,diag,0.0)
        for b,E,W in level_ops(q,k,L,lw):
            A=jnp.where(lvl==b,mmx(W,W,1,1,PS),A)
        a_ref[0,c]=A.astype(a_ref.dtype)
        last=L[CHUNK-1:CHUNK,:]
        o=mmx(A,v,1,0,PA)+mmx(q*jnp.exp2(L),S,1,1,PA)
        st[...]=S*jnp.exp2(last)+mmx(v,k*jnp.exp2(last-L),0,0,PA)
        cb=comb_ref[0,rows,:]+o
        comb_ref[0,rows,:]=cb
        g=g_ref[0,rows,:]
        r=lax.rsqrt(jnp.sum(cb*cb,axis=1,keepdims=True)*(1.0/HDIM)+head_eps)
        mixed_ref[0,rows,:]=(cb*r*gain*(g/(1.0+jnp.exp(-g)))).astype(bf16)
        return 0
    lax.fori_loop(0,chunks,step,0,unroll=4)

def gla_forward(big,qkvg,pre,taps,gain,PS=2,PA=2,adt=f32):
    _,H,total,_=qkvg.shape; chunks=total//CHUNK
    row=pl.BlockSpec((1,total,LANES),lambda h:(h,0,0))
    def of(i): return pl.BlockSpec((None,1,total,LANES),lambda h:(i,h,0,0))
    return pl.pallas_call(
        functools.partial(fwd_kernel,PS,PA,total),
        grid=(H,),
        in_specs=[pl.BlockSpec(memory_space=pltpu.SMEM)]+[of(i) for i in range(4)]+[row]+[pl.BlockSpec((1,16,LANES),lambda h:(h,0,0)),pl.BlockSpec((1,LANES),lambda h:(0,0))],
        out_specs=[row,row,pl.BlockSpec((1,chunks,CHUNK,CHUNK),lambda h:(h,0,0,0)),pl.BlockSpec((1,chunks,LANES,LANES),lambda h:(h,0,0,0))],
        out_shape=[jax.ShapeDtypeStruct((H,total,LANES),bf16),jax.ShapeDtypeStruct((H,total,LANES),f32),
                   jax.ShapeDtypeStruct((H,chunks,CHUNK,CHUNK),adt),jax.ShapeDtypeStruct((H,chunks,LANES,LANES),f32)],
        scratch_shapes=[pltpu.VMEM((total+2*MARGIN,LANES),f32)]*3+[pltpu.VMEM((CHUNK,CHUNK),jnp.int32),pltpu.VMEM((CHUNK,CHUNK),bf16),pltpu.VMEM((LANES,LANES),f32)],
        compiler_params=pltpu.CompilerParams(vmem_limit_bytes=40*2**20,dimension_semantics=("arbitrary",)),
        name="gla_forward", cost_estimate=cost(65),
    )(big,qkvg,qkvg,qkvg,qkvg,pre,taps,gain)

def bwd_kernel(PS,PA,total,big_ref,q_ref,k_ref,v_ref,g_ref,p_ref,comb_ref,a_ref,s_ref,gm_ref,taps_ref,gain_ref,
               dqk_ref,dpre_ref,dtaps_ref,dvec_ref,vp,dcp,gl,gr,dvl,lvl_ref,tri_ref,ds,car):
    chunks=total//CHUNK
    @pl.when(pl.program_id(0)==0)
    def _():
        lvl,i,j=level_matrix()
        lvl_ref[...]=jnp.where(i==j,-1,lvl)
        tri_ref[0]=jnp.where(i>=j,1.0,0.0).astype(bf16)
        tri_ref[1]=jnp.where(i<=j,1.0,0.0).astype(bf16)
        z=jnp.zeros((MARGIN,LANES),f32)
        for r in (vp,dcp,gl,gr):
            r[0:MARGIN,:]=z; r[MARGIN+total:,:]=z
    big=big_ref[0]==4*SIDE*SIDE
    taps=taps_ref[0]; gain=gain_ref[...]
    vp[MARGIN:MARGIN+total,:]=v_ref[0]
    def rowwise(c,acc):
        rows=pl.ds(pl.multiple_of(c*CHUNK,CHUNK),CHUNK)
        cb=comb_ref[0,rows,:]; g=g_ref[0,rows,:]; gm=gm_ref[0,rows,:].astype(f32)
        r=lax.rsqrt(jnp.sum(cb*cb,axis=1,keepdims=True)*(1.0/HDIM)+head_eps)
        n=cb*r
        sg=1.0/(1.0+jnp.exp(-g)); silu=g*sg
        dqk_ref[3,0,rows,:]=(gm*n*gain*(sg+silu*(1.0-sg))).astype(bf16)
        dn=gm*silu
        acc=acc+jnp.sum((dn*n).reshape(CHUNK//8,8,LANES),axis=0)
        dn=dn*gain
        dc=r*(dn-n*(jnp.sum(dn*n,axis=1,keepdims=True)*(1.0/HDIM)))
        dcp[pl.ds(pl.multiple_of(MARGIN+c*CHUNK,MARGIN),CHUNK),:]=dc
        return acc
    dgain=lax.fori_loop(0,chunks,rowwise,jnp.zeros((8,LANES),f32))
    dvec_ref[0,0:1,:]=jnp.sum(dgain,axis=0,keepdims=True)
    def conv(width):
        height=width
        accs=[jnp.zeros((8,LANES),f32) for _ in range(9)]
        for t in range(chunks):
            o=MARGIN+t*CHUNK
            col,r=image_masks(t*CHUNK,CHUNK,width,height)
            zs=[jnp.where(r!=height-1,dcp[o+width:o+width+CHUNK,:],0.0),dcp[o:o+CHUNK,:],jnp.where(r!=0,dcp[o-width:o-width+CHUNK,:],0.0)]
            vs=[jnp.where(col!=0,vp[o-1:o-1+CHUNK,:],0.0),vp[o:o+CHUNK,:],jnp.where(col!=width-1,vp[o+1:o+1+CHUNK,:],0.0)]
            for a in range(3):
                for b in range(3):
                    accs[3*a+b]=accs[3*a+b]+jnp.sum((zs[a]*vs[b]).reshape(CHUNK//8,8,LANES),axis=0)
            def comb(b): return zs[0]*taps[b:b+1,:]+zs[1]*taps[3+b:4+b,:]+zs[2]*taps[6+b:7+b,:]
            gl[o:o+CHUNK,:]=comb(0)
            dvl[t*CHUNK:(t+1)*CHUNK,:]=comb(1)
            gr[o:o+CHUNK,:]=comb(2)
        for i in range(9):
            dtaps_ref[0,i:i+1,:]=jnp.sum(accs[i],axis=0,keepdims=True)
        for t in range(chunks):
            o=MARGIN+t*CHUNK
            col,_=image_masks(0,CHUNK,width,height)
            dvl[t*CHUNK:(t+1)*CHUNK,:]+=jnp.where(col!=width-1,gl[o+1:o+1+CHUNK,:],0.0)+jnp.where(col!=0,gr[o-1:o-1+CHUNK,:],0.0)
    @pl.when(big)
    def _(): conv(2*SIDE)
    @pl.when(jnp.logical_not(big))
    def _(): conv(SIDE)
    per=SIDE*SIDE//CHUNK
    row=iota2((CHUNK,LANES),0)
    def step(i,acc):
        c=chunks-1-i
        rows=pl.ds(pl.multiple_of(c*CHUNK,CHUNK),CHUNK)
        end=jnp.where(big,c==chunks-1,lax.rem(c,per)==per-1)
        dS=jnp.where(end,0.0,ds[...])
        carry=jnp.where(end,0.0,car[0:1,:])
        q=q_ref[0,rows,:]*(HDIM**-0.5); k=k_ref[0,rows,:]; v=v_ref[0,rows,:]
        pre=p_ref[0,rows,:]
        lw=log_decay2(pre)
        L=sel_mm(tri_ref[0],lw,3)
        do=dcp[pl.ds(pl.multiple_of(MARGIN+c*CHUNK,MARGIN),CHUNK),:]
        lvl=lvl_ref[...]
        low=tri_ref[0].astype(f32)>0.5
        G=jnp.where(low,mmx(do,v,1,1,PS),mmx(v,do,1,1,PS))
        last=L[CHUNK-1:CHUNK,:]
        eL=jnp.exp2(L); eR=jnp.exp2(last-L)
        S=s_ref[0,c]
        dq=eL*mmx(do,S,1,0,PA)
        kR=k*eR
        dk=eR*mmx(v,dS,1,0,PA)
        dv=dvl[rows,:]+mmx(a_ref[0,c].astype(f32),do,0,0,PA)+mmx(kR,dS,1,1,PA)
        ds[...]=dS*jnp.exp2(last)+mmx(do,q*eL,0,0,PA)
        for b,E,W in level_ops(q,k,L,lw):
            Y=E*mmx(jnp.where(lvl==b,G,0.0),W,1,0,PS)
            right=(row&b)!=0
            dq=dq+jnp.where(right,Y,0.0); dk=dk+jnp.where(right,0.0,Y)
        z=q*dq-k*dk
        suf=sel_mm(tri_ref[1],z,3)+carry
        car[0:1,:]=suf[0:1,:]
        dp=suf*((1.0/GATE_NORM)/(1.0+jnp.exp(pre)))
        dpre_ref[0,rows,:]=dp
        t=jnp.sum(do*v,axis=1,keepdims=True)
        dqk_ref[0,0,rows,:]=((dq+t*k)*(HDIM**-0.5)).astype(bf16)
        dqk_ref[1,0,rows,:]=(dk+t*q).astype(bf16)
        dqk_ref[2,0,rows,:]=dv.astype(bf16)
        return acc+jnp.sum(dp.reshape(CHUNK//8,8,LANES),axis=0)
    db=lax.fori_loop(0,chunks,step,jnp.zeros((8,LANES),f32),unroll=4)
    dvec_ref[0,1:2,:]=jnp.sum(db,axis=0,keepdims=True)

def gla_backward(big,qkvg,pre,comb,A,S,gm,taps,gain,PS=2,PA=2):
    _,H,total,_=qkvg.shape; chunks=total//CHUNK
    row=pl.BlockSpec((1,total,LANES),lambda h:(h,0,0))
    def of(i): return pl.BlockSpec((None,1,total,LANES),lambda h:(i,h,0,0))
    return pl.pallas_call(
        functools.partial(bwd_kernel,PS,PA,total),
        grid=(H,),
        in_specs=[pl.BlockSpec(memory_space=pltpu.SMEM)]+[of(i) for i in range(4)]+[row]*2+[pl.BlockSpec((1,chunks,CHUNK,CHUNK),lambda h:(h,0,0,0)),pl.BlockSpec((1,chunks,LANES,LANES),lambda h:(h,0,0,0)),row,
                  pl.BlockSpec((1,16,LANES),lambda h:(h,0,0)),pl.BlockSpec((1,LANES),lambda h:(0,0))],
        out_specs=[pl.BlockSpec((4,1,total,LANES),lambda h:(0,h,0,0)),row,pl.BlockSpec((1,16,LANES),lambda h:(h,0,0)),pl.BlockSpec((1,8,LANES),lambda h:(h,0,0))],
        out_shape=[jax.ShapeDtypeStruct((4,H,total,LANES),bf16),jax.ShapeDtypeStruct((H,total,LANES),f32),
                   jax.ShapeDtypeStruct((H,16,LANES),f32),jax.ShapeDtypeStruct((H,8,LANES),f32)],
        scratch_shapes=[pltpu.VMEM((total+2*MARGIN,LANES),f32)]*4+[pltpu.VMEM((total,LANES),f32),pltpu.VMEM((CHUNK,CHUNK),jnp.int32),pltpu.VMEM((2,CHUNK,CHUNK),bf16),pltpu.VMEM((LANES,LANES),f32),pltpu.VMEM((8,LANES),f32)],
        compiler_params=pltpu.CompilerParams(vmem_limit_bytes=48*2**20,dimension_semantics=("arbitrary",)),
        name="gla_backward", cost_estimate=cost(80),
    )(big,qkvg,qkvg,qkvg,qkvg,pre,comb,A,S,gm,taps,gain)


ROWS = 256


def head_window(res, column):
    base = column // LANES * LANES
    off = column - base
    width = LANES if off + HDIM <= LANES else 2 * LANES
    part = res[:, base : base + width]
    if off:
        part = pltpu.roll(part, width - off, 1)
    part = part[:, :LANES]
    return jnp.where(iota2(part.shape, 1) < HDIM, part, 0.0)


def heads_joined(pieces):
    blocks = [None] * (len(pieces) * HDIM // LANES + 1)

    def put(index, value):
        blocks[index] = value if blocks[index] is None else blocks[index] + value

    for h, x in enumerate(pieces):
        index, off = h * HDIM // LANES, h * HDIM % LANES
        if off == 0:
            put(index, x)
            continue
        r = pltpu.roll(x, off, 1)
        if off + HDIM <= LANES:
            put(index, r)
        else:
            lane = iota2(r.shape, 1)
            put(index, jnp.where(lane >= off, r, 0.0))
            put(index + 1, jnp.where(lane < off, r, 0.0))
    total = len(pieces) * HDIM
    blocks = [b for b in blocks if b is not None]
    return jnp.concatenate(blocks, axis=1)[:, :total]


def first_rows(tiles, width):
    return pl.BlockSpec((ROWS, width), lambda i, t: (jnp.minimum(i, tiles // 2 - 1), 0))


def last_rows(tiles, width):
    return pl.BlockSpec((ROWS, width), lambda i, t: (jnp.maximum(i - tiles // 2, 0), 0))


def put_half(half, value, own_ref, away_ref):
    @pl.when(pl.program_id(0) < half)
    def _():
        own_ref[...] = value.astype(own_ref.dtype)

    @pl.when(pl.program_id(0) >= half)
    def _():
        away_ref[...] = value.astype(away_ref.dtype)


def project_kernel(H, half, turn_ref, x_ref, y_ref, wa_ref, wb_ref, down_ref, up_ref, bias_ref, out_ref, pre_ref, lat_ref):
    x = jnp.where(pl.program_id(0) < half, x_ref[...], y_ref[...])
    span = 2 * H * HDIM
    for s in range(2):
        res = mm(x, (wa_ref, wb_ref)[s][:, :span], 1, 0)
        for i in range(2 * H):
            out_ref[2 * s + i // H, i % H] = head_window(res, i * HDIM)
    latent = mm(x, down_ref[...], 1, 0)
    lat_ref[...] = latent
    pre = bias_ref[...] + sum(mm(p, up_ref[...], 1, 0) for p in parts(latent, 3)[::-1])
    for h in range(H):
        pre_ref[h] = pre[:, h * LANES : (h + 1) * LANES]


def project(turn, x, away, wa, wb, down, up, bias, H):
    total, width = 2 * x.shape[0], x.shape[1]
    tiles = total // ROWS

    def turned(i, t):
        return lax.rem(i + t[0], tiles)

    full = lambda a: pl.BlockSpec(a.shape, lambda i, t: (0, 0))
    return pl.pallas_call(
        functools.partial(project_kernel, H, tiles // 2),
        grid_spec=pltpu.PrefetchScalarGridSpec(
            num_scalar_prefetch=1,
            grid=(tiles,),
            in_specs=[first_rows(tiles, width), last_rows(tiles, width), full(wa), full(wb), full(down), full(up), full(bias)],
            out_specs=[
                pl.BlockSpec((4, H, ROWS, LANES), lambda i, t: (0, 0, turned(i, t), 0)),
                pl.BlockSpec((H, ROWS, LANES), lambda i, t: (0, turned(i, t), 0)),
                pl.BlockSpec((ROWS, LANES), lambda i, t: (turned(i, t), 0)),
            ],
        ),
        out_shape=[
            jax.ShapeDtypeStruct((4, H, total, LANES), f32),
            jax.ShapeDtypeStruct((H, total, LANES), f32),
            jax.ShapeDtypeStruct((total, LANES), f32),
        ],
        compiler_params=pltpu.CompilerParams(vmem_limit_bytes=56 * 2**20, dimension_semantics=("arbitrary",)),
        name="project", cost_estimate=cost(15),
    )(turn, x, away, wa, wb, down, up, bias)


def attend_kernel(H, half, turn_ref, m_ref, w_ref, own_ref, away_ref, cat_ref):
    cat = heads_joined([m_ref[h].astype(f32) for h in range(H)]).astype(bf16)
    cat_ref[...] = cat
    put_half(half, mm(cat, w_ref[...], 1, 1), own_ref, away_ref)


def attend(turn, mixed, w):
    H, total, _ = mixed.shape
    tiles = total // ROWS
    inner = H * HDIM
    return pl.pallas_call(
        functools.partial(attend_kernel, H, tiles // 2),
        grid_spec=pltpu.PrefetchScalarGridSpec(
            num_scalar_prefetch=1,
            grid=(tiles,),
            in_specs=[
                pl.BlockSpec((H, ROWS, LANES), lambda i, t: (0, lax.rem(i + t[0], tiles), 0)),
                pl.BlockSpec(w.shape, lambda i, t: (0, 0)),
            ],
            out_specs=[first_rows(tiles, w.shape[0]), last_rows(tiles, w.shape[0]), pl.BlockSpec((ROWS, inner), lambda i, t: (i, 0))],
        ),
        out_shape=[jax.ShapeDtypeStruct((total // 2, w.shape[0]), f32)] * 2 + [jax.ShapeDtypeStruct((total, inner), bf16)],
        compiler_params=pltpu.CompilerParams(vmem_limit_bytes=40 * 2**20, dimension_semantics=("arbitrary",)),
        name="attend", cost_estimate=cost(4),
    )(turn, mixed, w)


def attend_back_kernel(H, turn_ref, g_ref, w_ref, out_ref):
    res = mm(g_ref[...], w_ref[...], 1, 0)
    res = jnp.concatenate([res, jnp.zeros((ROWS, -res.shape[1] % LANES), f32)], axis=1)
    for h in range(H):
        out_ref[h] = head_window(res, h * HDIM)


def attend_back(turn, grad, w, H):
    total, width = grad.shape
    tiles = total // ROWS
    return pl.pallas_call(
        functools.partial(attend_back_kernel, H),
        grid_spec=pltpu.PrefetchScalarGridSpec(
            num_scalar_prefetch=1,
            grid=(tiles,),
            in_specs=[pl.BlockSpec((ROWS, width), lambda i, t: (i, 0)), pl.BlockSpec(w.shape, lambda i, t: (0, 0))],
            out_specs=pl.BlockSpec((H, ROWS, LANES), lambda i, t: (0, lax.rem(i + t[0], tiles), 0)),
        ),
        out_shape=jax.ShapeDtypeStruct((H, total, LANES), f32),
        compiler_params=pltpu.CompilerParams(vmem_limit_bytes=40 * 2**20, dimension_semantics=("arbitrary",)),
        name="attend_back", cost_estimate=cost(4),
    )(turn, grad, w)


def join_kernel(H, turn_ref, d_ref, cata_ref, catb_ref):
    for s in range(2):
        cat = heads_joined([d_ref[2 * s + i // H, i % H].astype(f32) for i in range(2 * H)])
        (cata_ref, catb_ref)[s][...] = cat.astype(bf16)


def join(turn, d):
    _, H, total, _ = d.shape
    tiles = total // ROWS
    cols = 2 * H * HDIM
    return pl.pallas_call(
        functools.partial(join_kernel, H),
        grid_spec=pltpu.PrefetchScalarGridSpec(
            num_scalar_prefetch=1,
            grid=(tiles,),
            in_specs=[pl.BlockSpec((4, H, ROWS, LANES), lambda i, t: (0, 0, lax.rem(i + t[0], tiles), 0))],
            out_specs=[pl.BlockSpec((ROWS, cols), lambda i, t: (i, 0))] * 2,
        ),
        out_shape=[jax.ShapeDtypeStruct((total, cols), bf16)] * 2,
        compiler_params=pltpu.CompilerParams(vmem_limit_bytes=40 * 2**20, dimension_semantics=("arbitrary",)),
        name="join", cost_estimate=cost(8),
    )(turn, d)


def project_back_kernel(H, half, turn_ref, x_ref, cata_ref, catb_ref, p_ref, lat_ref, wa_ref, wb_ref, down_ref, up_ref, own_ref, away_ref, ddown_ref, dup_ref):
    @pl.when(pl.program_id(0) == 0)
    def _():
        dup_ref[...] = jnp.zeros_like(dup_ref)
        ddown_ref[...] = jnp.zeros_like(ddown_ref)

    lat = parts(lat_ref[...], 2)
    glat = jnp.zeros((ROWS, LANES), f32)
    for h in range(H):
        dp = parts(p_ref[h], 3)
        up = up_ref[:, h * LANES : (h + 1) * LANES]
        glat = glat + (mm(dp[2], up, 1, 1) + mm(dp[1], up, 1, 1) + mm(dp[0], up, 1, 1))
        dup_ref[h] += mm(lat[0], dp[1], 0, 0) + mm(lat[1], dp[0], 0, 0) + mm(lat[0], dp[0], 0, 0)
    split = parts(glat, 2)[::-1]
    ddown_ref[...] += sum(mm(x_ref[...], p, 0, 0) for p in split)
    acc = sum(mm(p, down_ref[...], 1, 1) for p in split)
    acc = acc + mm(cata_ref[...], wa_ref[:, : cata_ref.shape[1]], 1, 1) + mm(catb_ref[...], wb_ref[:, : catb_ref.shape[1]], 1, 1)
    put_half(half, acc, own_ref, away_ref)


def project_back(turn, x, cat_a, cat_b, dpre, latent, wa, wb, down, up):
    H, total, _ = dpre.shape
    tiles = total // ROWS
    width, cols = x.shape[1], cat_a.shape[1]

    def turned(i, t):
        return lax.rem(i + t[0], tiles)

    full = lambda a: pl.BlockSpec(a.shape, lambda i, t: (0, 0))
    return pl.pallas_call(
        functools.partial(project_back_kernel, H, tiles // 2),
        grid_spec=pltpu.PrefetchScalarGridSpec(
            num_scalar_prefetch=1,
            grid=(tiles,),
            in_specs=[
                pl.BlockSpec((ROWS, width), lambda i, t: (i, 0)),
                pl.BlockSpec((ROWS, cols), lambda i, t: (i, 0)),
                pl.BlockSpec((ROWS, cols), lambda i, t: (i, 0)),
                pl.BlockSpec((H, ROWS, LANES), lambda i, t: (0, turned(i, t), 0)),
                pl.BlockSpec((ROWS, LANES), lambda i, t: (turned(i, t), 0)),
                full(wa), full(wb), full(down), full(up),
            ],
            out_specs=[
                first_rows(tiles, width),
                last_rows(tiles, width),
                pl.BlockSpec((width, LANES), lambda i, t: (0, 0)),
                pl.BlockSpec((H, LANES, LANES), lambda i, t: (0, 0, 0)),
            ],
        ),
        out_shape=[
            jax.ShapeDtypeStruct((total // 2, width), f32),
            jax.ShapeDtypeStruct((total // 2, width), f32),
            jax.ShapeDtypeStruct((width, LANES), f32),
            jax.ShapeDtypeStruct((H, LANES, LANES), f32),
        ],
        compiler_params=pltpu.CompilerParams(vmem_limit_bytes=56 * 2**20, dimension_semantics=("arbitrary",)),
        name="project_back", cost_estimate=cost(2),
    )(turn, x, cat_a, cat_b, dpre, latent, wa, wb, down, up)


NORM_EPS = 1e-06
FLIP = [(0, 1), (1, 0)]
COLUMNS = ("dq", "core")


def swap(x):
    away = lax.ppermute(x, ("core", "mp"), [(1, 2), (2, 1)])
    return jnp.where(lax.axis_index("core") == lax.axis_index("mp"), x, away)


def other(x):
    return lax.ppermute(x, "core", FLIP)


def both(x):
    return jnp.concatenate([x, other(x)], axis=0)


def summed(x):
    half = x.shape[0] // 2
    return x[:half] + other(x[half:])


def across(x):
    return lax.ppermute(x, "mp", FLIP)


def bits():
    count = lax.axis_size("dq").bit_length() - 1
    return [("dq", count - 1 - i) for i in range(count)] + [("mp", 0)]


def flipped(x, bit):
    axis, place = bit
    return lax.ppermute(x, axis, [(i, i ^ (1 << place)) for i in range(lax.axis_size(axis))])


def own_bit(bit):
    return (lax.axis_index(bit[0]) >> bit[1]) & 1


def orders():
    count = len(bits())
    far = list(range(count - 2))
    return far + [count - 1, count - 2], far + [count - 2, count - 1]


def spread(x, order, steps):
    names = bits()
    for step in steps:
        place = order[step]
        away, mine = flipped(x, names[place]), own_bit(names[place])
        at = sum(h < place for h in order[:step])
        x = jnp.stack([jnp.where(mine == 0, x, away), jnp.where(mine == 0, away, x)], axis=at)
    return x.reshape(-1, x.shape[-1]) if len(order) - 1 in steps else x


def fold_step(x, order, step):
    names = bits()
    if step == 0:
        x = x.reshape((2,) * len(names) + (-1, x.shape[-1]))
    left = sorted(order[: len(order) - step])
    place = order[len(order) - 1 - step]
    at, mine = left.index(place), own_bit(names[place])
    send = lax.dynamic_index_in_dim(x, 1 - mine, at, keepdims=False)
    keep = lax.dynamic_index_in_dim(x, mine, at, keepdims=False)
    x = keep.astype(f32) + flipped(send, names[place]).astype(f32)
    return x if len(left) == 1 else x.astype(bf16)


def folded_in(x, order, gates):
    sums = [x]
    for step in range(1, len(order)):
        for gate in gates.get(len(order) - step, ()):
            x = after(x, gate)
        x = fold_step(x, order, step)
        sums.append(x)
    return sums


def after(x, *first):
    marks = sum(f[(0,) * f.ndim].astype(f32) for f in first)
    return jnp.where(jnp.isnan(marks), jnp.zeros_like(x), x)


def modulate(rows, shift, scale):
    center = rows - jnp.mean(rows, axis=-1, keepdims=True)
    normed = center * lax.rsqrt(jnp.mean(center * center, axis=-1, keepdims=True) + NORM_EPS)
    return normed * (1.0 + scale[:, None, :]) + shift[:, None, :]


def per_head(x, heads, rows):
    x = x.reshape(x.shape[0], heads, HDIM)
    return jnp.pad(x, ((0, rows - x.shape[0]), (0, 0), (0, LANES - HDIM)))


def contract(a, b, i, j):
    return lax.dot_general(a, b, (((i,), (j,)), ((), ())), preferred_element_type=f32)


def silu(v):
    return v * jax.nn.sigmoid(v)


def on_device(
    block_input, out_grad, time_table, class_table, time_ids, class_ids, image_patches, ada_weight, ada_bias,
    proj_weight, decay_down, decay_up, decay_bias, head_gain, conv_taps, out_weight, fc1_weight, fc2_weight,
):
    rows, width = block_input.shape
    inner = proj_weight.shape[2]
    heads = inner // HDIM
    core = lax.axis_index("core")
    y = lax.axis_index("mp")
    dq = lax.axis_size("dq")
    slot_rows = SIDE * SIDE
    own_slots = rows // slot_rows
    unit_slots = 2 * own_slots

    cut = 2 * inner
    order_a, order_b = orders()
    last = len(order_a)
    w_part = swap(proj_weight.transpose(1, 0, 2).reshape(-1, 4 * inner))
    w_out = lax.all_gather(swap(out_weight.T), ("dq", "mp"), axis=0, tiled=True)
    w_a = spread(w_part[:, :cut], order_a, range(1))
    w_b = spread(w_part[:, cut:], order_b, range(1))

    ids = jnp.concatenate([time_ids, class_ids, image_patches])[None]
    ids = after(ids, w_part)
    ids = lax.all_to_all(jnp.broadcast_to(ids, (2 * dq, ids.shape[1])), COLUMNS, split_axis=0, concat_axis=0, tiled=True)
    ids = after(ids, w_a, w_b)
    w_a = spread(w_a, order_a, range(1, last - 2))
    w_b = spread(w_b, order_b, range(1, last - 2))

    x = swap(block_input)
    t_all, c_all = ids[:, :unit_slots].reshape(-1), ids[:, unit_slots : 2 * unit_slots].reshape(-1)
    big_all = ids[:, 2 * unit_slots] == 4 * slot_rows
    me = 2 * lax.axis_index("dq") + y
    patches = lax.dynamic_slice_in_dim(ids[:, 2 * unit_slots], me, 1)
    condition = time_table[t_all].astype(f32) + class_table[c_all].astype(f32)
    silu_all = silu(condition).astype(bf16)
    columns = jnp.dot(silu_all, ada_weight, preferred_element_type=f32) + ada_bias.astype(f32)
    part = columns.shape[1]
    columns = columns.reshape(2 * dq, unit_slots, part)
    columns = jnp.where(big_all[:, None, None], columns[:, :1], columns)
    columns = lax.dynamic_index_in_dim(columns.reshape(dq, 2, 2, own_slots, part), y, 1, keepdims=False)
    columns = after(columns.reshape(2 * dq, own_slots, part), w_a, w_b)
    received = lax.all_to_all(columns, COLUMNS, split_axis=0, concat_axis=0, tiled=True)
    modulation = received.transpose(1, 0, 2).reshape(own_slots, 6 * width)
    shift1, scale1, gate1, shift2, scale2, gate2 = jnp.split(modulation, 6, axis=1)
    residual = x.astype(f32).reshape(own_slots, slot_rows, width)
    hidden, norm_back_one = jax.vjp(modulate, residual, shift1, scale1)
    hidden = hidden.reshape(rows, width).astype(bf16)
    hidden_away = other(hidden)
    hidden_all = jnp.concatenate([hidden, hidden_away], axis=0)

    away = lax.ppermute(out_grad, "mp", FLIP)
    straight = core == y
    g_rows = jnp.where(straight, out_grad, other(away))
    g_away = jnp.where(straight, other(out_grad), away)
    w_a = spread(after(w_a, x, away), order_a, range(last - 2, last - 1))
    w_b = spread(after(w_b, x, away), order_b, range(last - 2, last - 1))
    w_a = spread(after(w_a, received), order_a, range(last - 1, last))
    w_b = spread(after(w_b, received), order_b, range(last - 1, last))
    hidden_units = fc1_weight.shape[1]
    w_rest = jnp.concatenate([fc1_weight, fc2_weight.T], axis=1)
    w_rest = lax.all_gather(after(w_rest, w_a, w_b), COLUMNS, axis=0, tiled=True)
    w_fc1, w_fc2 = w_rest[:, :hidden_units], w_rest[:, hidden_units:]

    start = core * inner
    up_local = lax.dynamic_slice_in_dim(decay_up, start, inner, 1)
    bias_local = lax.dynamic_slice_in_dim(decay_bias, start, inner, 0)
    taps_local = lax.dynamic_slice_in_dim(conv_taps, start, inner, 1)
    lowrank = decay_down.shape[1]
    down_pad = jnp.pad(decay_down, ((0, 0), (0, LANES - lowrank)))
    up_pad = per_head(up_local, heads, LANES).reshape(LANES, heads * LANES)
    bias_pad = per_head(bias_local[None].astype(f32), heads, 1).reshape(1, heads * LANES)
    taps_pad = per_head(taps_local.astype(f32), heads, 16).transpose(1, 0, 2)
    gain_pad = jnp.pad(head_gain.astype(f32), (0, LANES - HDIM))[None]
    turn = (core * (rows // ROWS)).astype(jnp.int32)[None]

    grad_rows = g_rows.astype(f32).reshape(own_slots, slot_rows, width)
    grad_feed = (grad_rows * gate2[:, None, :]).astype(bf16).reshape(rows, width)
    gate2_away = across(gate2)
    grad_feed_away = g_away.astype(f32).reshape(own_slots, slot_rows, width) * gate2_away[:, None, :]
    grad_feed_away = grad_feed_away.astype(bf16).reshape(rows, width)
    qkvg, pre, latent = project(turn, hidden, hidden_away, w_a, w_b, down_pad, up_pad, bias_pad, heads)
    mixed, comb, scores, states = gla_forward(patches, qkvg, pre, taps_pad, gain_pad)
    attn_own, attn_away, mixed_cat = attend(turn, mixed, w_out)
    attention = (attn_own + other(attn_away)).reshape(own_slots, slot_rows, width)
    after_attn = residual + gate1[:, None, :] * attention
    hidden_two, norm_back_two = jax.vjp(modulate, after_attn, shift2, scale2)
    hidden_two = hidden_two.reshape(rows, width).astype(bf16)
    hidden_two_away = across(hidden_two)

    def feed(h, g):
        active, back = jax.vjp(functools.partial(jax.nn.gelu, approximate=True), jnp.dot(h, w_fc1, preferred_element_type=f32))
        return active.astype(bf16), back(jnp.dot(g, w_fc2, preferred_element_type=f32))[0].astype(bf16)

    active, grad_up = feed(hidden_two, grad_feed)
    feed_own = contract(active, w_fc2, 1, 1)
    grad_hidden_two_own = contract(grad_up, w_fc1, 1, 1)
    hidden_two_away = after(hidden_two_away, feed_own, grad_hidden_two_own)
    active_away, grad_up_away = feed(hidden_two_away, grad_feed_away)
    grad_hidden_two_part = contract(grad_up_away, w_fc1, 1, 1).astype(bf16)
    grad_hidden_two = across(grad_hidden_two_part)
    grad_feed_all = jnp.concatenate([grad_feed, grad_feed_away], axis=0)
    hidden_two_all = jnp.concatenate([hidden_two, hidden_two_away], axis=0)
    active_all = jnp.concatenate([active, active_away], axis=0)
    grad_up_all = jnp.concatenate([grad_up, grad_up_away], axis=0)
    feed_away = across(after(contract(active_away, w_fc2, 1, 1).astype(bf16), grad_hidden_two_part))
    grad_fc2 = contract(grad_feed_all, active_all, 0, 0).astype(bf16)
    fc2_grad = lax.psum_scatter(grad_fc2, COLUMNS, scatter_dimension=0, tiled=True).astype(f32).T
    grad_fc1 = contract(hidden_two_all, grad_up_all, 0, 0).astype(bf16)
    fc1_grad = lax.psum_scatter(grad_fc1, COLUMNS, scatter_dimension=0, tiled=True).astype(f32)
    grad_hidden_two = grad_hidden_two_own + after(grad_hidden_two, grad_fc1).astype(f32)

    grad_after, grad_shift_two, grad_scale_two = norm_back_two(grad_hidden_two.reshape(own_slots, slot_rows, width))
    grad_after = grad_after + grad_rows
    grad_gate_one = jnp.sum(grad_after * attention, axis=1)
    grad_attn_all = both((grad_after * gate1[:, None, :]).astype(bf16).reshape(rows, width))
    grad_mixed = attend_back(turn, grad_attn_all, w_out, heads)
    grad_out = contract(grad_attn_all, mixed_cat, 0, 0).astype(bf16)
    out_step = fold_step(grad_out, order_a, 0)
    d_qkvg, d_pre, d_taps, d_vec = gla_backward(
        after(patches, grad_out), qkvg, pre, comb, scores, states, grad_mixed, taps_pad, gain_pad
    )
    feed_out = feed_own + after(feed_away, d_qkvg).astype(f32)
    feed_out = feed_out.reshape(own_slots, slot_rows, width)
    block_out = (after_attn + gate2[:, None, :] * feed_out).reshape(rows, width).astype(bf16)
    grad_gate_two = jnp.sum(grad_rows * feed_out, axis=1)
    cat_a, cat_b = join(after(turn, out_step), d_qkvg)
    part_b = contract(hidden_all, cat_b, 0, 0).astype(bf16)
    part_a = contract(hidden_all, cat_a, 0, 0).astype(bf16)
    b_step = fold_step(part_b, order_b, 0)
    a_step = fold_step(part_a, order_a, 0)
    hidden_own, hidden_far, d_down, d_up = project_back(
        after(turn, part_a, part_b), hidden_all, cat_a, cat_b, d_pre, latent, w_a, w_b, down_pad, up_pad
    )
    hidden_sum = (hidden_own + other(hidden_far)).reshape(own_slots, slot_rows, width)
    grad_residual, grad_shift_one, grad_scale_one = norm_back_one(hidden_sum)
    grad_mod = jnp.concatenate(
        [grad_shift_one, grad_scale_one, grad_gate_one, grad_shift_two, grad_scale_two, grad_gate_two], axis=1
    ).astype(bf16)
    grad_mod = grad_mod.reshape(own_slots, 2 * dq, part).transpose(1, 0, 2)
    got = lax.all_to_all(grad_mod, COLUMNS, split_axis=0, concat_axis=0, tiled=True).reshape(dq, 1, unit_slots, part)
    gates = {2: (grad_mod,), 1: (got,)}
    sums_b = folded_in(b_step, order_b, gates)
    sums_a = folded_in(a_step, order_a, gates)
    sums_out = folded_in(out_step, order_a, {len(order_a) - 1: (sums_b[0],), len(order_a) - 2: (sums_b[1],)})
    block_out = swap(after(block_out, sums_b[0]))
    grad_back = swap(jnp.concatenate([sums_a[-1], sums_b[-1], sums_out[-1]], axis=1))
    input_grad = swap(after(after((grad_residual + grad_after).reshape(rows, width), sums_a[1]), sums_b[1]))

    d_down = d_down[:, :lowrank]

    def placed(value):
        return lax.dynamic_update_slice_in_dim(jnp.zeros((value.shape[0], width), f32), value, start, 1)

    d_up = d_up[:, :lowrank, :HDIM].transpose(1, 0, 2).reshape(lowrank, inner)
    d_taps = d_taps[:, :9, :HDIM].transpose(1, 0, 2).reshape(9, inner)
    d_bias = d_vec[:, 1, :HDIM].reshape(1, inner)
    d_gain = jnp.sum(d_vec[:, 0, :HDIM], axis=0)
    stacked = placed(jnp.concatenate([d_up, d_taps, d_bias], axis=0))
    flat = jnp.concatenate([d_down.reshape(lowrank, width), stacked, jnp.pad(d_gain, (0, width - HDIM))[None]], axis=0)
    flat = flat + other(flat)
    for step, bit in enumerate(bits()):
        flat = after(flat, (sums_a, sums_b)[step % 2][step // 2])
        flat = flat + flipped(flat, bit)
    down_sum = flat[:lowrank].reshape(width, lowrank)
    up_sum = flat[lowrank : 2 * lowrank]
    taps_sum = flat[2 * lowrank : 2 * lowrank + 9]
    bias_sum = flat[2 * lowrank + 9]
    gain_sum = flat[2 * lowrank + 10, :HDIM]

    away = lax.ppermute(got, "mp", FLIP)
    got = jnp.where(y == 0, jnp.concatenate([got, away], axis=1), jnp.concatenate([away, got], axis=1))
    got = got.reshape(2 * dq, unit_slots, part).astype(f32)
    folded = jnp.sum(got, axis=1, keepdims=True)
    first = jnp.arange(unit_slots)[None, :, None] == 0
    got = jnp.where(big_all[:, None, None], jnp.where(first, folded, 0.0), got).reshape(-1, part)
    ada_bias_grad = jnp.sum(got, axis=0)
    ada_weight_grad = jnp.dot(silu_all.astype(f32).T, got, precision=lax.Precision.HIGHEST, preferred_element_type=f32)
    grad_silu = jnp.dot(got, ada_weight.astype(f32).T, precision=lax.Precision.HIGHEST, preferred_element_type=f32)
    grad_silu = lax.all_to_all(grad_silu, COLUMNS, split_axis=0, concat_axis=0, tiled=True)
    grad_silu = jnp.sum(grad_silu.reshape(2 * dq, unit_slots, width), axis=0)
    own_cond = lax.dynamic_slice_in_dim(condition, (2 * lax.axis_index("dq") + core) * unit_slots, unit_slots, 0)
    gate = jax.nn.sigmoid(own_cond)
    cond_grad = grad_silu * (gate * (1.0 + own_cond * (1.0 - gate)))

    proj_grad = grad_back[:, : 4 * inner].reshape(-1, 4, inner).transpose(1, 0, 2)
    return (
        block_out, input_grad, cond_grad, ada_weight_grad, ada_bias_grad, proj_grad, down_sum, up_sum, bias_sum,
        gain_sum, taps_sum, grad_back[:, 4 * inner :].T, fc1_grad, fc2_grad,
    )


def solution(mesh):
    dp, mp = mesh.shape["dp"], mesh.shape["mp"]
    split = Mesh(mesh.devices.reshape(dp // 2, 2, mp), ("dq", "core", "mp"))
    d = ("dq", "core")
    every = ("dq", "core", "mp")
    return jax.shard_map(
        on_device,
        mesh=split,
        in_specs=(
            P(every, None), P(every, None), P(), P(), P(d), P(d), P(d), P(None, d), P(d), P(None, d, "mp"),
            P(), P(), P(), P(), P(), P("mp", d), P(d, "mp"), P("mp", d),
        ),
        out_specs=(
            P(every, None), P(every, None), P(d, None), P(None, d), P(d), P(None, d, "mp"),
            P(), P(), P(), P(), P(), P("mp", d), P(d, "mp"), P("mp", d),
        ),
        check_vma=False,
    )
```

```python
import functools
import math

import jax
import jax.numpy as jnp
from jax import lax
from jax.experimental import pallas as pl
from jax.experimental.pallas import tpu as pltpu
from jax.sharding import Mesh
from jax.sharding import PartitionSpec as P

f32=jnp.float32; bf16=jnp.bfloat16
HDIM=72; SIDE=16; LANES=128; CHUNK=128; MARGIN=64
LEVELS=(64,32,16,8,4,2,1)
GATE_NORM=16.0; head_eps=1e-5
LOG2E=math.log2(math.e)

def cost(us):
    return pl.CostEstimate(flops=us*900*10**6, bytes_accessed=10**6, transcendentals=0)

def parts(x, n):
    out=[]
    for _ in range(n-1):
        p=x.astype(bf16); out.append(p); x=x-p.astype(f32)
    out.append(x.astype(bf16)); return out

def mm(a,b,ca,cb):
    return lax.dot_general(a,b,(((ca,),(cb,)),((),())),preferred_element_type=f32)

def mmx(a,b,ca,cb,n):
    if n==1: return mm(a.astype(bf16),b.astype(bf16),ca,cb)
    ah,al=parts(a,2); bh,bl=parts(b,2)
    return mm(ah,bh,ca,cb)+(mm(ah,bl,ca,cb)+mm(al,bh,ca,cb))

def sel_mm(m,x,n):
    ps=parts(x,n)
    r=mm(m,ps[-1],1,0)
    for p in ps[-2::-1]: r=mm(m,p,1,0)+r
    return r

def iota2(shape,d): return lax.broadcasted_iota(jnp.int32,shape,d)

def level_matrix():
    i=iota2((CHUNK,CHUNK),0); j=iota2((CHUNK,CHUNK),1)
    x=i^j
    lvl=jnp.zeros((CHUNK,CHUNK),jnp.int32)
    for b in LEVELS[::-1]: lvl=jnp.where(x>=b,b,lvl)
    return lvl,i,j

def level_ops(q,k,L,lw):
    row=iota2((CHUNK,LANES),0)
    out=[]
    for b in LEVELS:
        n=CHUNK//(2*b)
        if b>=8:
            L3=L.reshape(n,2*b,LANES); D=L3-L3[:,b-1:b,:]
            E=jnp.exp2(-jnp.abs(D)).reshape(CHUNK,LANES)
            q3=q.reshape(n,2*b,LANES); k3=k.reshape(n,2*b,LANES)
            X=jnp.concatenate([k3[:,:b],q3[:,b:]],axis=1).reshape(CHUNK,LANES)
        else:
            right=(row&b)!=0
            X=jnp.where(right,q,k)
            L3=L.reshape(CHUNK//8,8,LANES)
            if b==4:
                D=(L3-L3[:,3:4,:]).reshape(CHUNK,LANES); E=jnp.exp2(-jnp.abs(D))
            elif b==2:
                s=lax.broadcasted_iota(jnp.int32,L3.shape,1)
                R=jnp.where(s<4,L3[:,1:2,:],L3[:,5:6,:])
                E=jnp.exp2(-jnp.abs(L3-R)).reshape(CHUNK,LANES)
            else:
                E=jnp.exp2(jnp.where(right,lw,0.0))
        out.append((b,E,X*E))
    return out

def log_decay2(pre):
    return (jnp.minimum(pre,0.0)-jnp.log1p(jnp.exp(-jnp.abs(pre))))*(LOG2E/GATE_NORM)

def image_masks(base,rows,width,height):
    p=iota2((rows,LANES),0)+base
    col=p&(width-1)
    r=(p//width)&(height-1)
    return col,r

def conv_forward(vp,up,um,taps,store,total,width,height):
    tiles=total//CHUNK
    for t in range(tiles):
        o=MARGIN+t*CHUNK
        col,_=image_masks(0,CHUNK,width,height)
        c=vp[o:o+CHUNK,:]
        left=jnp.where(col!=0,vp[o-1:o-1+CHUNK,:],0.0)
        right=jnp.where(col!=width-1,vp[o+1:o+1+CHUNK,:],0.0)
        def comb(a): return left*taps[3*a:3*a+1,:]+c*taps[3*a+1:3*a+2,:]+right*taps[3*a+2:3*a+3,:]
        um[o:o+CHUNK,:]=comb(0)
        store(t,comb(1))
        up[o:o+CHUNK,:]=comb(2)

def conv_finish(up,um,add,total,width,height):
    for t in range(total//CHUNK):
        o=MARGIN+t*CHUNK
        _,r=image_masks(t*CHUNK,CHUNK,width,height)
        down=jnp.where(r!=height-1,up[o+width:o+width+CHUNK,:],0.0)
        upv=jnp.where(r!=0,um[o-width:o-width+CHUNK,:],0.0)
        add(t,down+upv)

def fwd_kernel(PS,PA,total,big_ref,q_ref,k_ref,v_ref,g_ref,p_ref,taps_ref,gain_ref,mixed_ref,comb_ref,a_ref,s_ref,vp,up,um,lvl_ref,tri_ref,st):
    chunks=total//CHUNK
    @pl.when(pl.program_id(0)==0)
    def _():
        lvl,i,j=level_matrix()
        lvl_ref[...]=jnp.where(i>j,lvl,jnp.where(i==j,-1,-2))
        tri_ref[...]=jnp.where(i>=j,1.0,0.0).astype(bf16)
        z=jnp.zeros((MARGIN,LANES),f32)
        for r in (vp,up,um):
            r[0:MARGIN,:]=z; r[MARGIN+total:,:]=z
    big=big_ref[0]==4*SIDE*SIDE
    taps=taps_ref[0]; gain=gain_ref[...]
    vp[MARGIN:MARGIN+total,:]=v_ref[0]
    def conv(width):
        def store(t,x): comb_ref[0,t*CHUNK:(t+1)*CHUNK,:]=x
        def add(t,x): comb_ref[0,t*CHUNK:(t+1)*CHUNK,:]+=x
        conv_forward(vp,up,um,taps,store,total,width,width)
        conv_finish(up,um,add,total,width,width)
    @pl.when(big)
    def _(): conv(2*SIDE)
    @pl.when(jnp.logical_not(big))
    def _(): conv(SIDE)
    per=SIDE*SIDE//CHUNK
    def step(c,_):
        rows=pl.ds(pl.multiple_of(c*CHUNK,CHUNK),CHUNK)
        start=jnp.where(big,c==0,lax.rem(c,per)==0)
        S=jnp.where(start,0.0,st[...])
        s_ref[0,c]=S
        q=q_ref[0,rows,:]*(HDIM**-0.5); k=k_ref[0,rows,:]; v=v_ref[0,rows,:]
        lw=log_decay2(p_ref[0,rows,:])
        L=sel_mm(tri_ref[...],lw,3)
        lvl=lvl_ref[...]
        diag=jnp.sum(q*k,axis=1,keepdims=True)
        A=jnp.where(lvl==-1,diag,0.0)
        for b,E,W in level_ops(q,k,L,lw):
            if b>=8:
                n=CHUNK//(2*b)
                late=W.reshape(n,2*b,LANES)[:,b:].reshape(CHUNK//2,LANES)
                part=mmx(late,W,1,1,PS).reshape(n,b,CHUNK)
                A3=A.reshape(n,2*b,CHUNK)
                part=jnp.where(lvl.reshape(n,2*b,CHUNK)[:,b:]==b,part,A3[:,b:])
                A=jnp.concatenate([A3[:,:b],part],axis=1).reshape(CHUNK,CHUNK)
            else:
                A=jnp.where(lvl==b,mmx(W,W,1,1,PS),A)
        a_ref[0,c]=A.astype(a_ref.dtype)
        last=L[CHUNK-1:CHUNK,:]
        o=mmx(A,v,1,0,PA)+mmx(q*jnp.exp2(L),S,1,1,PA)
        st[...]=S*jnp.exp2(last)+mmx(v,k*jnp.exp2(last-L),0,0,PA)
        cb=comb_ref[0,rows,:]+o
        comb_ref[0,rows,:]=cb
        g=g_ref[0,rows,:]
        r=lax.rsqrt(jnp.sum(cb*cb,axis=1,keepdims=True)*(1.0/HDIM)+head_eps)
        mixed_ref[0,rows,:]=(cb*r*gain*(g/(1.0+jnp.exp(-g)))).astype(bf16)
        return 0
    lax.fori_loop(0,chunks,step,0,unroll=4)

def gla_forward(big,qkvg,pre,taps,gain,PS=1,PA=2,adt=f32):
    _,H,total,_=qkvg.shape; chunks=total//CHUNK
    row=pl.BlockSpec((1,total,LANES),lambda h:(h,0,0))
    def of(i): return pl.BlockSpec((None,1,total,LANES),lambda h:(i,h,0,0))
    return pl.pallas_call(
        functools.partial(fwd_kernel,PS,PA,total),
        grid=(H,),
        in_specs=[pl.BlockSpec(memory_space=pltpu.SMEM)]+[of(i) for i in range(4)]+[row]+[pl.BlockSpec((1,16,LANES),lambda h:(h,0,0)),pl.BlockSpec((1,LANES),lambda h:(0,0))],
        out_specs=[row,row,pl.BlockSpec((1,chunks,CHUNK,CHUNK),lambda h:(h,0,0,0)),pl.BlockSpec((1,chunks,LANES,LANES),lambda h:(h,0,0,0))],
        out_shape=[jax.ShapeDtypeStruct((H,total,LANES),bf16),jax.ShapeDtypeStruct((H,total,LANES),f32),
                   jax.ShapeDtypeStruct((H,chunks,CHUNK,CHUNK),adt),jax.ShapeDtypeStruct((H,chunks,LANES,LANES),f32)],
        scratch_shapes=[pltpu.VMEM((total+2*MARGIN,LANES),f32)]*3+[pltpu.VMEM((CHUNK,CHUNK),jnp.int32),pltpu.VMEM((CHUNK,CHUNK),bf16),pltpu.VMEM((LANES,LANES),f32)],
        compiler_params=pltpu.CompilerParams(vmem_limit_bytes=40*2**20,dimension_semantics=("arbitrary",)),
        name="gla_forward", cost_estimate=cost(65),
    )(big,qkvg,qkvg,qkvg,qkvg,pre,taps,gain)

def bwd_kernel(PS,PA,total,big_ref,q_ref,k_ref,v_ref,g_ref,p_ref,comb_ref,a_ref,s_ref,gm_ref,taps_ref,gain_ref,
               dqk_ref,dpre_ref,dtaps_ref,dvec_ref,vp,dcp,gl,gr,dvl,mask_ref,tri_ref,ds,car):
    chunks=total//CHUNK
    @pl.when(pl.program_id(0)==0)
    def _():
        lvl,i,j=level_matrix()
        for at,b in enumerate(LEVELS): mask_ref[at]=jnp.where(lvl==b,1.0,0.0).astype(bf16)
        tri_ref[0]=jnp.where(i>=j,1.0,0.0).astype(bf16)
        tri_ref[1]=jnp.where(i<=j,1.0,0.0).astype(bf16)
        z=jnp.zeros((MARGIN,LANES),f32)
        for r in (vp,dcp,gl,gr):
            r[0:MARGIN,:]=z; r[MARGIN+total:,:]=z
    big=big_ref[0]==4*SIDE*SIDE
    taps=taps_ref[0]; gain=gain_ref[...]
    vp[MARGIN:MARGIN+total,:]=v_ref[0]
    def rowwise(c,acc):
        rows=pl.ds(pl.multiple_of(c*CHUNK,CHUNK),CHUNK)
        cb=comb_ref[0,rows,:]; g=g_ref[0,rows,:]; gm=gm_ref[0,rows,:].astype(f32)
        r=lax.rsqrt(jnp.sum(cb*cb,axis=1,keepdims=True)*(1.0/HDIM)+head_eps)
        n=cb*r
        sg=1.0/(1.0+jnp.exp(-g)); silu=g*sg
        dqk_ref[3,0,rows,:]=(gm*n*gain*(sg+silu*(1.0-sg))).astype(bf16)
        dn=gm*silu
        acc=acc+jnp.sum((dn*n).reshape(CHUNK//8,8,LANES),axis=0)
        dn=dn*gain
        dc=r*(dn-n*(jnp.sum(dn*n,axis=1,keepdims=True)*(1.0/HDIM)))
        dcp[pl.ds(pl.multiple_of(MARGIN+c*CHUNK,MARGIN),CHUNK),:]=dc
        return acc
    dgain=lax.fori_loop(0,chunks,rowwise,jnp.zeros((8,LANES),f32))
    dvec_ref[0,0:1,:]=jnp.sum(dgain,axis=0,keepdims=True)
    def conv(width):
        height=width
        accs=[jnp.zeros((8,LANES),f32) for _ in range(9)]
        for t in range(chunks):
            o=MARGIN+t*CHUNK
            col,r=image_masks(t*CHUNK,CHUNK,width,height)
            zs=[jnp.where(r!=height-1,dcp[o+width:o+width+CHUNK,:],0.0),dcp[o:o+CHUNK,:],jnp.where(r!=0,dcp[o-width:o-width+CHUNK,:],0.0)]
            vs=[jnp.where(col!=0,vp[o-1:o-1+CHUNK,:],0.0),vp[o:o+CHUNK,:],jnp.where(col!=width-1,vp[o+1:o+1+CHUNK,:],0.0)]
            for a in range(3):
                for b in range(3):
                    accs[3*a+b]=accs[3*a+b]+jnp.sum((zs[a]*vs[b]).reshape(CHUNK//8,8,LANES),axis=0)
            def comb(b): return zs[0]*taps[b:b+1,:]+zs[1]*taps[3+b:4+b,:]+zs[2]*taps[6+b:7+b,:]
            gl[o:o+CHUNK,:]=comb(0)
            dvl[t*CHUNK:(t+1)*CHUNK,:]=comb(1)
            gr[o:o+CHUNK,:]=comb(2)
        for i in range(9):
            dtaps_ref[0,i:i+1,:]=jnp.sum(accs[i],axis=0,keepdims=True)
        for t in range(chunks):
            o=MARGIN+t*CHUNK
            col,_=image_masks(0,CHUNK,width,height)
            dvl[t*CHUNK:(t+1)*CHUNK,:]+=jnp.where(col!=width-1,gl[o+1:o+1+CHUNK,:],0.0)+jnp.where(col!=0,gr[o-1:o-1+CHUNK,:],0.0)
    @pl.when(big)
    def _(): conv(2*SIDE)
    @pl.when(jnp.logical_not(big))
    def _(): conv(SIDE)
    per=SIDE*SIDE//CHUNK
    row=iota2((CHUNK,LANES),0)
    def step(i,acc):
        c=chunks-1-i
        rows=pl.ds(pl.multiple_of(c*CHUNK,CHUNK),CHUNK)
        end=jnp.where(big,c==chunks-1,lax.rem(c,per)==per-1)
        dS=jnp.where(end,0.0,ds[...])
        carry=jnp.where(end,0.0,car[0:1,:])
        q=q_ref[0,rows,:]*(HDIM**-0.5); k=k_ref[0,rows,:]; v=v_ref[0,rows,:]
        pre=p_ref[0,rows,:]
        lw=log_decay2(pre)
        L=sel_mm(tri_ref[0],lw,3)
        do=dcp[pl.ds(pl.multiple_of(MARGIN+c*CHUNK,MARGIN),CHUNK),:]
        low=tri_ref[0].astype(f32)>0.5
        G=jnp.where(low,mmx(do,v,1,1,PS),mmx(v,do,1,1,PS))
        last=L[CHUNK-1:CHUNK,:]
        eL=jnp.exp2(L); eR=jnp.exp2(last-L)
        S=s_ref[0,c]
        dq=eL*mmx(do,S,1,0,PA)
        kR=k*eR
        dk=eR*mmx(v,dS,1,0,PA)
        dv=dvl[rows,:]+mmx(a_ref[0,c].astype(f32),do,0,0,PA)+mmx(kR,dS,1,1,PA)
        ds[...]=dS*jnp.exp2(last)+mmx(do,q*eL,0,0,PA)
        Gs=parts(G,PS)
        for at,(b,E,W) in enumerate(level_ops(q,k,L,lw)):
            Gb=[g*mask_ref[at] for g in Gs]
            if PS==1:
                Y=E*mm(Gb[0],W.astype(bf16),1,0)
            else:
                Wh,Wl=parts(W,2)
                Y=E*(mm(jnp.concatenate(Gb,axis=1),jnp.concatenate([Wh,Wh],axis=0),1,0)+mm(Gb[0],Wl,1,0))
            if b>=8:
                n=CHUNK//(2*b)
                Y=Y.reshape(n,2*b,LANES); q3=dq.reshape(n,2*b,LANES); k3=dk.reshape(n,2*b,LANES)
                dq=jnp.concatenate([q3[:,:b],q3[:,b:]+Y[:,b:]],axis=1).reshape(CHUNK,LANES)
                dk=jnp.concatenate([k3[:,:b]+Y[:,:b],k3[:,b:]],axis=1).reshape(CHUNK,LANES)
            else:
                late=jnp.where((row&b)!=0,Y,0.0)
                dq=dq+late; dk=dk+(Y-late)
        z=q*dq-k*dk
        suf=sel_mm(tri_ref[1],z,3)+carry
        car[0:1,:]=suf[0:1,:]
        dp=suf*((1.0/GATE_NORM)/(1.0+jnp.exp(pre)))
        dpre_ref[0,rows,:]=dp
        t=jnp.sum(do*v,axis=1,keepdims=True)
        dqk_ref[0,0,rows,:]=((dq+t*k)*(HDIM**-0.5)).astype(bf16)
        dqk_ref[1,0,rows,:]=(dk+t*q).astype(bf16)
        dqk_ref[2,0,rows,:]=dv.astype(bf16)
        return acc+jnp.sum(dp.reshape(CHUNK//8,8,LANES),axis=0)
    db=lax.fori_loop(0,chunks,step,jnp.zeros((8,LANES),f32),unroll=4)
    dvec_ref[0,1:2,:]=jnp.sum(db,axis=0,keepdims=True)

def gla_backward(base,count,big,qkvg,pre,comb,A,S,gm,taps,gain,PS=2,PA=2):
    _,H,total,_=qkvg.shape; chunks=total//CHUNK
    row=pl.BlockSpec((1,total,LANES),lambda h:(h+base,0,0))
    out=pl.BlockSpec((1,total,LANES),lambda h:(h,0,0))
    def of(i): return pl.BlockSpec((None,1,total,LANES),lambda h:(i,h+base,0,0))
    return pl.pallas_call(
        functools.partial(bwd_kernel,PS,PA,total),
        grid=(count,),
        in_specs=[pl.BlockSpec(memory_space=pltpu.SMEM)]+[of(i) for i in range(4)]+[row]*2+[pl.BlockSpec((1,chunks,CHUNK,CHUNK),lambda h:(h+base,0,0,0)),pl.BlockSpec((1,chunks,LANES,LANES),lambda h:(h+base,0,0,0)),row,
                  pl.BlockSpec((1,16,LANES),lambda h:(h+base,0,0)),pl.BlockSpec((1,LANES),lambda h:(0,0))],
        out_specs=[pl.BlockSpec((4,1,total,LANES),lambda h:(0,h,0,0)),out,pl.BlockSpec((1,16,LANES),lambda h:(h,0,0)),pl.BlockSpec((1,8,LANES),lambda h:(h,0,0))],
        out_shape=[jax.ShapeDtypeStruct((4,count,total,LANES),bf16),jax.ShapeDtypeStruct((count,total,LANES),f32),
                   jax.ShapeDtypeStruct((count,16,LANES),f32),jax.ShapeDtypeStruct((count,8,LANES),f32)],
        scratch_shapes=[pltpu.VMEM((total+2*MARGIN,LANES),f32)]*4+[pltpu.VMEM((total,LANES),f32),pltpu.VMEM((len(LEVELS),CHUNK,CHUNK),bf16),pltpu.VMEM((2,CHUNK,CHUNK),bf16),pltpu.VMEM((LANES,LANES),f32),pltpu.VMEM((8,LANES),f32)],
        compiler_params=pltpu.CompilerParams(vmem_limit_bytes=48*2**20,dimension_semantics=("arbitrary",)),
        name="gla_backward", cost_estimate=cost(10*count),
    )(big,qkvg,qkvg,qkvg,qkvg,pre,comb,A,S,gm,taps,gain)


ROWS = 256


def head_window(res, column):
    base = column // LANES * LANES
    off = column - base
    width = LANES if off + HDIM <= LANES else 2 * LANES
    part = res[:, base : base + width]
    if off:
        part = pltpu.roll(part, width - off, 1)
    part = part[:, :LANES]
    return jnp.where(iota2(part.shape, 1) < HDIM, part, 0.0)


def heads_joined(pieces):
    blocks = [None] * (len(pieces) * HDIM // LANES + 1)

    def put(index, value):
        blocks[index] = value if blocks[index] is None else blocks[index] + value

    for h, x in enumerate(pieces):
        index, off = h * HDIM // LANES, h * HDIM % LANES
        if off == 0:
            put(index, x)
            continue
        r = pltpu.roll(x, off, 1)
        if off + HDIM <= LANES:
            put(index, r)
        else:
            lane = iota2(r.shape, 1)
            put(index, jnp.where(lane >= off, r, 0.0))
            put(index + 1, jnp.where(lane < off, r, 0.0))
    total = len(pieces) * HDIM
    blocks = [b for b in blocks if b is not None]
    return jnp.concatenate(blocks, axis=1)[:, :total]


def first_rows(tiles, width):
    return pl.BlockSpec((ROWS, width), lambda i, t: (jnp.minimum(i, tiles // 2 - 1), 0))


def last_rows(tiles, width):
    return pl.BlockSpec((ROWS, width), lambda i, t: (jnp.maximum(i - tiles // 2, 0), 0))


def put_half(half, value, own_ref, away_ref):
    @pl.when(pl.program_id(0) < half)
    def _():
        own_ref[...] = value.astype(own_ref.dtype)

    @pl.when(pl.program_id(0) >= half)
    def _():
        away_ref[...] = value.astype(away_ref.dtype)


def project_kernel(H, half, turn_ref, x_ref, y_ref, wa_ref, wb_ref, down_ref, up_ref, bias_ref, out_ref, pre_ref, lat_ref):
    x = jnp.where(pl.program_id(0) < half, x_ref[...], y_ref[...])
    span = 2 * H * HDIM
    for s in range(2):
        res = mm(x, (wa_ref, wb_ref)[s][:, :span], 1, 0)
        for i in range(2 * H):
            out_ref[2 * i // H, s * (H // 2) + i % (H // 2)] = head_window(res, i * HDIM)
    latent = mm(x, down_ref[...], 1, 0)
    lat_ref[...] = latent
    pre = bias_ref[...] + sum(mm(p, up_ref[...], 1, 0) for p in parts(latent, 3)[::-1])
    for h in range(H):
        pre_ref[h] = pre[:, h * LANES : (h + 1) * LANES]


def project(turn, x, away, wa, wb, down, up, bias, H):
    total, width = 2 * x.shape[0], x.shape[1]
    tiles = total // ROWS

    def turned(i, t):
        return lax.rem(i + t[0], tiles)

    full = lambda a: pl.BlockSpec(a.shape, lambda i, t: (0, 0))
    return pl.pallas_call(
        functools.partial(project_kernel, H, tiles // 2),
        grid_spec=pltpu.PrefetchScalarGridSpec(
            num_scalar_prefetch=1,
            grid=(tiles,),
            in_specs=[first_rows(tiles, width), last_rows(tiles, width), full(wa), full(wb), full(down), full(up), full(bias)],
            out_specs=[
                pl.BlockSpec((4, H, ROWS, LANES), lambda i, t: (0, 0, turned(i, t), 0)),
                pl.BlockSpec((H, ROWS, LANES), lambda i, t: (0, turned(i, t), 0)),
                pl.BlockSpec((ROWS, LANES), lambda i, t: (turned(i, t), 0)),
            ],
        ),
        out_shape=[
            jax.ShapeDtypeStruct((4, H, total, LANES), f32),
            jax.ShapeDtypeStruct((H, total, LANES), f32),
            jax.ShapeDtypeStruct((total, LANES), f32),
        ],
        compiler_params=pltpu.CompilerParams(vmem_limit_bytes=56 * 2**20, dimension_semantics=("arbitrary",)),
        name="project", cost_estimate=cost(15),
    )(turn, x, away, wa, wb, down, up, bias)


def attend_kernel(H, half, turn_ref, m_ref, w_ref, own_ref, away_ref, cat_ref):
    cat = heads_joined([m_ref[h].astype(f32) for h in range(H)]).astype(bf16)
    cat_ref[...] = cat
    put_half(half, mm(cat, w_ref[...], 1, 1), own_ref, away_ref)


def attend(turn, mixed, w):
    H, total, _ = mixed.shape
    tiles = total // ROWS
    inner = H * HDIM
    return pl.pallas_call(
        functools.partial(attend_kernel, H, tiles // 2),
        grid_spec=pltpu.PrefetchScalarGridSpec(
            num_scalar_prefetch=1,
            grid=(tiles,),
            in_specs=[
                pl.BlockSpec((H, ROWS, LANES), lambda i, t: (0, lax.rem(i + t[0], tiles), 0)),
                pl.BlockSpec(w.shape, lambda i, t: (0, 0)),
            ],
            out_specs=[first_rows(tiles, w.shape[0]), last_rows(tiles, w.shape[0]), pl.BlockSpec((ROWS, inner), lambda i, t: (i, 0))],
        ),
        out_shape=[jax.ShapeDtypeStruct((total // 2, w.shape[0]), f32)] * 2 + [jax.ShapeDtypeStruct((total, inner), bf16)],
        compiler_params=pltpu.CompilerParams(vmem_limit_bytes=40 * 2**20, dimension_semantics=("arbitrary",)),
        name="attend", cost_estimate=cost(4),
    )(turn, mixed, w)


def attend_back_kernel(H, turn_ref, g_ref, w_ref, out_ref):
    res = mm(g_ref[...], w_ref[...], 1, 0)
    res = jnp.concatenate([res, jnp.zeros((ROWS, -res.shape[1] % LANES), f32)], axis=1)
    for h in range(H):
        out_ref[h] = head_window(res, h * HDIM)


def attend_back(turn, grad, w, H):
    total, width = grad.shape
    tiles = total // ROWS
    return pl.pallas_call(
        functools.partial(attend_back_kernel, H),
        grid_spec=pltpu.PrefetchScalarGridSpec(
            num_scalar_prefetch=1,
            grid=(tiles,),
            in_specs=[pl.BlockSpec((ROWS, width), lambda i, t: (i, 0)), pl.BlockSpec(w.shape, lambda i, t: (0, 0))],
            out_specs=pl.BlockSpec((H, ROWS, LANES), lambda i, t: (0, lax.rem(i + t[0], tiles), 0)),
        ),
        out_shape=jax.ShapeDtypeStruct((H, total, LANES), f32),
        compiler_params=pltpu.CompilerParams(vmem_limit_bytes=40 * 2**20, dimension_semantics=("arbitrary",)),
        name="attend_back", cost_estimate=cost(4),
    )(turn, grad, w)


def join_kernel(H, turn_ref, d_ref, cat_ref):
    cat_ref[...] = heads_joined([d_ref[i // H, i % H].astype(f32) for i in range(4 * H)]).astype(bf16)


def join(turn, d):
    _, H, total, _ = d.shape
    tiles = total // ROWS
    cols = 4 * H * HDIM
    return pl.pallas_call(
        functools.partial(join_kernel, H),
        grid_spec=pltpu.PrefetchScalarGridSpec(
            num_scalar_prefetch=1,
            grid=(tiles,),
            in_specs=[pl.BlockSpec((4, H, ROWS, LANES), lambda i, t: (0, 0, lax.rem(i + t[0], tiles), 0))],
            out_specs=pl.BlockSpec((ROWS, cols), lambda i, t: (i, 0)),
        ),
        out_shape=jax.ShapeDtypeStruct((total, cols), bf16),
        compiler_params=pltpu.CompilerParams(vmem_limit_bytes=40 * 2**20, dimension_semantics=("arbitrary",)),
        name="join", cost_estimate=cost(4),
    )(turn, d)


def project_back_kernel(H, half, turn_ref, x_ref, cata_ref, catb_ref, pa_ref, pb_ref, lat_ref, wa_ref, wb_ref, down_ref, up_ref, own_ref, away_ref, ddown_ref, dup_ref):
    @pl.when(pl.program_id(0) == 0)
    def _():
        dup_ref[...] = jnp.zeros_like(dup_ref)
        ddown_ref[...] = jnp.zeros_like(ddown_ref)

    lat = parts(lat_ref[...], 2)
    dp = parts(jnp.concatenate([p[h] for p in (pa_ref, pb_ref) for h in range(H // 2)], axis=1), 2)
    glat = mm(dp[1], up_ref[...], 1, 1) + mm(dp[0], up_ref[...], 1, 1)
    dup_ref[...] += mm(lat[0], dp[1], 0, 0) + mm(lat[1], dp[0], 0, 0) + mm(lat[0], dp[0], 0, 0)
    split = parts(glat, 2)[::-1]
    ddown_ref[...] += sum(mm(p, x_ref[...], 0, 0) for p in split)
    acc = sum(mm(p, down_ref[...], 1, 1) for p in split)
    acc = acc + mm(cata_ref[...], wa_ref[:, : cata_ref.shape[1]], 1, 1) + mm(catb_ref[...], wb_ref[:, : catb_ref.shape[1]], 1, 1)
    put_half(half, acc, own_ref, away_ref)


def project_back(turn, x, cat_a, cat_b, dpre_a, dpre_b, latent, wa, wb, down, up):
    H, total = 2 * dpre_a.shape[0], dpre_a.shape[1]
    tiles = total // ROWS
    width, cols = x.shape[1], cat_a.shape[1]

    def turned(i, t):
        return lax.rem(i + t[0], tiles)

    full = lambda a: pl.BlockSpec(a.shape, lambda i, t: (0, 0))
    return pl.pallas_call(
        functools.partial(project_back_kernel, H, tiles // 2),
        grid_spec=pltpu.PrefetchScalarGridSpec(
            num_scalar_prefetch=1,
            grid=(tiles,),
            in_specs=[
                pl.BlockSpec((ROWS, width), lambda i, t: (i, 0)),
                pl.BlockSpec((ROWS, cols), lambda i, t: (i, 0)),
                pl.BlockSpec((ROWS, cols), lambda i, t: (i, 0)),
                pl.BlockSpec((H // 2, ROWS, LANES), lambda i, t: (0, turned(i, t), 0)),
                pl.BlockSpec((H // 2, ROWS, LANES), lambda i, t: (0, turned(i, t), 0)),
                pl.BlockSpec((ROWS, LANES), lambda i, t: (turned(i, t), 0)),
                full(wa), full(wb), full(down), full(up),
            ],
            out_specs=[
                first_rows(tiles, width),
                last_rows(tiles, width),
                pl.BlockSpec((LANES, width), lambda i, t: (0, 0)),
                pl.BlockSpec((LANES, H * LANES), lambda i, t: (0, 0)),
            ],
        ),
        out_shape=[
            jax.ShapeDtypeStruct((total // 2, width), f32),
            jax.ShapeDtypeStruct((total // 2, width), f32),
            jax.ShapeDtypeStruct((LANES, width), f32),
            jax.ShapeDtypeStruct((LANES, H * LANES), f32),
        ],
        compiler_params=pltpu.CompilerParams(vmem_limit_bytes=56 * 2**20, dimension_semantics=("arbitrary",)),
        name="project_back", cost_estimate=cost(2),
    )(turn, x, cat_a, cat_b, dpre_a, dpre_b, latent, wa, wb, down, up)


NORM_EPS = 1e-06
FLIP = [(0, 1), (1, 0)]
COLUMNS = ("dq", "core")


def swap(x):
    away = lax.ppermute(x, ("core", "mp"), [(1, 2), (2, 1)])
    return jnp.where(lax.axis_index("core") == lax.axis_index("mp"), x, away)


def other(x):
    return lax.ppermute(x, "core", FLIP)


def both(x):
    return jnp.concatenate([x, other(x)], axis=0)


def summed(x):
    half = x.shape[0] // 2
    return x[:half] + other(x[half:])


def across(x):
    return lax.ppermute(x, "mp", FLIP)


def bits():
    count = lax.axis_size("dq").bit_length() - 1
    return [("dq", count - 1 - i) for i in range(count)] + [("mp", 0)]


def flipped(x, bit):
    axis, place = bit
    return lax.ppermute(x, axis, [(i, i ^ (1 << place)) for i in range(lax.axis_size(axis))])


def own_bit(bit):
    return (lax.axis_index(bit[0]) >> bit[1]) & 1


def orders():
    count = len(bits())
    far = list(range(count - 2))
    return far + [count - 1, count - 2], far + [count - 2, count - 1]


def spread(x, order, steps, work=()):
    names = bits()
    for step in steps:
        place = order[step]
        away, mine = flipped(x, names[place]), own_bit(names[place])
        at = sum(h < place for h in order[:step])
        x = after(x, *work) if work else x
        x = jnp.stack([jnp.where(mine == 0, x, away), jnp.where(mine == 0, away, x)], axis=at)
    return x.reshape(-1, x.shape[-1]) if len(order) - 1 in steps else x


def fold_split(x, order, step):
    names = bits()
    if step == 0:
        x = x.reshape((2,) * len(names) + (-1, x.shape[-1]))
    left = sorted(order[: len(order) - step])
    place = order[len(order) - 1 - step]
    at, mine = left.index(place), own_bit(names[place])
    return lax.dynamic_index_in_dim(x, 1 - mine, at, keepdims=False), lax.dynamic_index_in_dim(x, mine, at, keepdims=False)


def fold_sum(split, order, step, work=()):
    send, keep = split
    keep = after(keep, *work) if work else keep
    x = keep.astype(f32) + flipped(send, bits()[order[len(order) - 1 - step]]).astype(f32)
    return x if step == len(order) - 1 else x.astype(bf16)


def fold_step(x, order, step):
    return fold_sum(fold_split(x, order, step), order, step)


def after(x, *first):
    marks = sum(f[(0,) * f.ndim].astype(f32) for f in first)
    return jnp.where(jnp.isnan(marks), jnp.zeros_like(x), x)


def modulate(rows, shift, scale):
    center = rows - jnp.mean(rows, axis=-1, keepdims=True)
    normed = center * lax.rsqrt(jnp.mean(center * center, axis=-1, keepdims=True) + NORM_EPS)
    return normed * (1.0 + scale[:, None, :]) + shift[:, None, :]


def per_head(x, heads, rows):
    x = x.reshape(x.shape[0], heads, HDIM)
    return jnp.pad(x, ((0, rows - x.shape[0]), (0, 0), (0, LANES - HDIM)))


def contract(a, b, i, j):
    return lax.dot_general(a, b, (((i,), (j,)), ((), ())), preferred_element_type=f32)


def silu(v):
    return v * jax.nn.sigmoid(v)


def on_device(
    block_input, out_grad, time_table, class_table, time_ids, class_ids, image_patches, ada_weight, ada_bias,
    proj_weight, decay_down, decay_up, decay_bias, head_gain, conv_taps, out_weight, fc1_weight, fc2_weight,
):
    rows, width = block_input.shape
    inner = proj_weight.shape[2]
    heads = inner // HDIM
    core = lax.axis_index("core")
    y = lax.axis_index("mp")
    dq = lax.axis_size("dq")
    slot_rows = SIDE * SIDE
    own_slots = rows // slot_rows
    unit_slots = 2 * own_slots

    cut = 2 * inner
    order_a, order_b = orders()
    last = len(order_a)
    w_part = swap(proj_weight.reshape(4, -1, 2, inner // 2).transpose(1, 2, 0, 3).reshape(-1, 4 * inner))
    w_out = swap(out_weight.T)
    w_a = spread(w_part[:, :cut], order_a, range(1))
    w_b = spread(w_part[:, cut:], order_b, range(1))

    ids = jnp.concatenate([time_ids, class_ids, image_patches])[None]
    ids = after(ids, w_part, w_out)
    w_out = lax.all_gather(w_out, ("dq", "mp"), axis=0, tiled=True)
    ids = lax.all_to_all(jnp.broadcast_to(ids, (2 * dq, ids.shape[1])), COLUMNS, split_axis=0, concat_axis=0, tiled=True)
    ids = after(ids, w_a, w_b)
    away = across(after(out_grad, w_a, w_b))
    w_a = spread(w_a, order_a, range(1, last - 2))
    w_b = spread(w_b, order_b, range(1, last - 2))

    x = swap(block_input)
    t_all, c_all = ids[:, :unit_slots].reshape(-1), ids[:, unit_slots : 2 * unit_slots].reshape(-1)
    big_all = ids[:, 2 * unit_slots] == 4 * slot_rows
    me = 2 * lax.axis_index("dq") + y
    patches = lax.dynamic_slice_in_dim(ids[:, 2 * unit_slots], me, 1)
    condition = time_table[t_all].astype(f32) + class_table[c_all].astype(f32)
    silu_all = silu(condition).astype(bf16)
    columns = jnp.dot(silu_all, ada_weight, preferred_element_type=f32) + ada_bias.astype(f32)
    part = columns.shape[1]
    columns = columns.reshape(2 * dq, unit_slots, part)
    columns = jnp.where(big_all[:, None, None], columns[:, :1], columns)
    columns = lax.dynamic_index_in_dim(columns.reshape(dq, 2, 2, own_slots, part), y, 1, keepdims=False)
    columns = after(columns.reshape(2 * dq, own_slots, part), w_a, w_b)
    received = lax.all_to_all(columns, COLUMNS, split_axis=0, concat_axis=0, tiled=True)
    modulation = received.transpose(1, 0, 2).reshape(own_slots, 6 * width)
    shift1, scale1, gate1, shift2, scale2, gate2 = jnp.split(modulation, 6, axis=1)
    residual = x.astype(f32).reshape(own_slots, slot_rows, width)
    hidden, norm_back_one = jax.vjp(modulate, residual, shift1, scale1)
    hidden = hidden.reshape(rows, width).astype(bf16)
    hidden_away = other(hidden)
    hidden_all = jnp.concatenate([hidden, hidden_away], axis=0)

    start = core * inner
    up_local = lax.dynamic_slice_in_dim(decay_up, start, inner, 1)
    bias_local = lax.dynamic_slice_in_dim(decay_bias, start, inner, 0)
    taps_local = lax.dynamic_slice_in_dim(conv_taps, start, inner, 1)
    lowrank = decay_down.shape[1]
    down_pad = jnp.pad(decay_down, ((0, 0), (0, LANES - lowrank)))
    up_pad = per_head(up_local, heads, LANES).reshape(LANES, heads * LANES)
    bias_pad = per_head(bias_local[None].astype(f32), heads, 1).reshape(1, heads * LANES)
    taps_pad = per_head(taps_local.astype(f32), heads, 16).transpose(1, 0, 2)
    gain_pad = jnp.pad(head_gain.astype(f32), (0, LANES - HDIM))[None]
    turn = (core * (rows // ROWS)).astype(jnp.int32)[None]

    straight = core == y
    g_rows = jnp.where(straight, out_grad, other(away))
    g_away = jnp.where(straight, other(out_grad), away)
    w_a = spread(after(w_a, x, away), order_a, range(last - 2, last - 1))
    w_b = spread(after(w_b, x, away), order_b, range(last - 2, last - 1))
    w_a = spread(after(w_a, received), order_a, range(last - 1, last))
    w_b = spread(after(w_b, hidden), order_b, range(last - 1, last), (hidden_away, up_pad, bias_pad, taps_pad, down_pad, g_away))
    hidden_units = fc1_weight.shape[1]
    w_rest = jnp.concatenate([fc1_weight, fc2_weight.T], axis=1)
    w_rest = lax.all_gather(after(w_rest, w_a, w_b), COLUMNS, axis=0, tiled=True)
    w_fc1, w_fc2 = w_rest[:, :hidden_units], w_rest[:, hidden_units:]

    grad_rows = g_rows.astype(f32).reshape(own_slots, slot_rows, width)
    grad_feed = (grad_rows * gate2[:, None, :]).astype(bf16).reshape(rows, width)
    gate2_away = across(gate2)
    grad_feed_away = g_away.astype(f32).reshape(own_slots, slot_rows, width) * gate2_away[:, None, :]
    grad_feed_away = grad_feed_away.astype(bf16).reshape(rows, width)
    qkvg, pre, latent = project(turn, hidden, hidden_away, w_a, w_b, down_pad, up_pad, bias_pad, heads)
    mixed, comb, scores, states = gla_forward(after(patches, grad_feed_away, grad_feed), qkvg, pre, taps_pad, gain_pad)
    attn_own, attn_away, mixed_cat = attend(turn, mixed, w_out)
    attention = (attn_own + other(attn_away)).reshape(own_slots, slot_rows, width)
    after_attn = residual + gate1[:, None, :] * attention
    hidden_two, norm_back_two = jax.vjp(modulate, after_attn, shift2, scale2)
    hidden_two = hidden_two.reshape(rows, width).astype(bf16)
    hidden_two_away = across(hidden_two)

    def feed(h, g):
        active, back = jax.vjp(functools.partial(jax.nn.gelu, approximate=True), jnp.dot(h, w_fc1, preferred_element_type=f32))
        return active.astype(bf16), back(jnp.dot(g, w_fc2, preferred_element_type=f32))[0].astype(bf16)

    active, grad_up = feed(hidden_two, grad_feed)
    feed_own = contract(active, w_fc2, 1, 1)
    grad_hidden_two_own = contract(grad_up, w_fc1, 1, 1)
    hidden_two_away = after(hidden_two_away, feed_own, grad_hidden_two_own)
    active_away, grad_up_away = feed(hidden_two_away, grad_feed_away)
    grad_hidden_two_part = contract(grad_up_away, w_fc1, 1, 1).astype(bf16)
    grad_hidden_two = across(grad_hidden_two_part)
    grad_feed_all = jnp.concatenate([grad_feed, grad_feed_away], axis=0)
    hidden_two_all = jnp.concatenate([hidden_two, hidden_two_away], axis=0)
    active_all = after(jnp.concatenate([active, active_away], axis=0), grad_hidden_two_part)
    grad_up_all = after(jnp.concatenate([grad_up, grad_up_away], axis=0), grad_hidden_two_part)
    feed_away = across(after(contract(active_away, w_fc2, 1, 1).astype(bf16), grad_hidden_two_part))
    grad_fc2 = contract(grad_feed_all, active_all, 0, 0).astype(bf16)
    fc2_grad = lax.psum_scatter(grad_fc2, COLUMNS, scatter_dimension=0, tiled=True).astype(f32).T
    grad_fc1 = contract(hidden_two_all, grad_up_all, 0, 0).astype(bf16)
    fc1_grad = lax.psum_scatter(grad_fc1, COLUMNS, scatter_dimension=0, tiled=True).astype(f32)
    grad_hidden_two = grad_hidden_two_own + after(grad_hidden_two, grad_fc1, grad_fc2).astype(f32)

    grad_after, grad_shift_two, grad_scale_two = norm_back_two(grad_hidden_two.reshape(own_slots, slot_rows, width))
    grad_after = grad_after + grad_rows
    grad_gate_one = jnp.sum(grad_after * attention, axis=1)
    grad_attn_all = both((grad_after * gate1[:, None, :]).astype(bf16).reshape(rows, width))
    grad_mixed = attend_back(turn, grad_attn_all, w_out, heads)
    grad_out = contract(grad_attn_all, mixed_cat, 0, 0).astype(bf16)
    grad_out = lax.psum_scatter(grad_out, ("dq", "mp"), scatter_dimension=0, tiled=True)
    kept = (qkvg, pre, comb, scores, states, grad_mixed, taps_pad, gain_pad)
    d_qkvg_a, d_pre_a, d_taps_a, d_vec_a = gla_backward(0, heads // 2, patches, *kept)
    cat_a = join(turn, d_qkvg_a)
    split_a = fold_split(contract(hidden_all, cat_a, 0, 0).astype(bf16), order_a, 0)
    d_qkvg_b, d_pre_b, d_taps_b, d_vec_b = gla_backward(heads // 2, heads // 2, after(patches, *split_a), *kept)
    sum_a = fold_sum(split_a, order_a, 0, (d_qkvg_b,))
    feed_out = feed_own + after(feed_away, d_qkvg_b).astype(f32)
    feed_out = feed_out.reshape(own_slots, slot_rows, width)
    block_out = (after_attn + gate2[:, None, :] * feed_out).reshape(rows, width).astype(bf16)
    grad_gate_two = jnp.sum(grad_rows * feed_out, axis=1)
    cat_b = join(after(turn, sum_a), d_qkvg_b)
    split_b = fold_split(contract(hidden_all, cat_b, 0, 0).astype(bf16), order_a, 0)
    split_a = fold_split(sum_a, order_a, 1)
    hidden_own, hidden_far, d_down, d_up = project_back(
        after(turn, *split_a, *split_b), hidden_all, cat_a, cat_b, d_pre_a, d_pre_b, latent, w_a, w_b, down_pad, up_pad
    )
    hidden_sum = (hidden_own + other(hidden_far)).reshape(own_slots, slot_rows, width)
    grad_residual, grad_shift_one, grad_scale_one = norm_back_one(hidden_sum)
    input_grad = (grad_residual + grad_after).reshape(rows, width)

    grad_mod = jnp.concatenate(
        [grad_shift_one, grad_scale_one, grad_gate_one, grad_shift_two, grad_scale_two, grad_gate_two], axis=1
    )
    grad_mod = grad_mod.reshape(own_slots, 2 * dq, part).transpose(1, 0, 2).reshape(2 * dq, own_slots * part)

    def placed(value):
        return lax.dynamic_update_slice_in_dim(jnp.zeros((value.shape[0], width), f32), value, start, 1)

    d_vec = jnp.concatenate([d_vec_a, d_vec_b], axis=0)
    d_taps = jnp.concatenate([d_taps_a, d_taps_b], axis=0)
    d_down = d_down[:lowrank].T
    d_up = d_up[:lowrank].reshape(lowrank, heads, LANES)[:, :, :HDIM].reshape(lowrank, inner)
    d_taps = d_taps[:, :9, :HDIM].transpose(1, 0, 2).reshape(9, inner)
    d_bias = d_vec[:, 1, :HDIM].reshape(1, inner)
    d_gain = jnp.sum(d_vec[:, 0, :HDIM], axis=0)
    stacked = placed(jnp.concatenate([d_up, d_taps, d_bias], axis=0))
    flat = jnp.concatenate([d_down.reshape(lowrank, width), stacked, jnp.pad(d_gain, (0, width - HDIM))[None]], axis=0)
    flat_rows = flat.shape[0]
    flat = flat.reshape(-1)
    flat = jnp.pad(flat, (0, -flat.shape[0] % (2 * dq))).reshape(2 * dq, -1)
    packed = jnp.concatenate([grad_mod, flat], axis=1)

    names = bits()
    sum_b = fold_sum(split_b, order_a, 0, (packed, input_grad))
    sum_a = fold_sum(split_a, order_a, 1, (packed, input_grad))
    got = lax.all_to_all(packed, COLUMNS, split_axis=0, concat_axis=0, tiled=True)
    split_b = fold_split(sum_b, order_a, 1)
    split_a = fold_split(after(sum_a, sum_b), order_a, 2)
    sum_b = fold_sum(split_b, order_a, 1, (got,))
    sum_a = fold_sum(split_a, order_a, 2, (got,))
    flat = jnp.sum(got[:, own_slots * part :], axis=0)
    got = jnp.concatenate([got[:, : own_slots * part].reshape(-1), flat])
    away = lax.ppermute(got, "mp", FLIP)
    count = 2 * dq * own_slots * part
    flat = flat + away[count:]
    got = jnp.where(y == 0, jnp.stack([got[:count], away[:count]]), jnp.stack([away[:count], got[:count]]))
    got = got.reshape(2, dq, unit_slots, part).transpose(1, 0, 2, 3).reshape(2 * dq, unit_slots, part)
    folded = jnp.sum(got, axis=1, keepdims=True)
    first = jnp.arange(unit_slots)[None, :, None] == 0
    got = jnp.where(big_all[:, None, None], jnp.where(first, folded, 0.0), got).reshape(-1, part)
    grad_silu = jnp.dot(got, ada_weight.astype(f32).T, precision=lax.Precision.HIGHEST, preferred_element_type=f32)
    packed = jnp.concatenate(
        [grad_silu.reshape(2 * dq, unit_slots * width), jnp.broadcast_to(flat[None], (2 * dq, flat.shape[0]))], axis=1
    )
    split_b = fold_split(sum_b, order_a, 2)
    split_a = fold_split(after(sum_a, sum_b), order_a, 3)
    block_out = swap(after(block_out, sum_b))
    input_grad = swap(after(input_grad, sum_b))
    sum_b = fold_sum(split_b, order_a, 2, (packed,))
    sum_a = fold_sum(split_a, order_a, 3, (packed,))
    packed = lax.all_to_all(packed, COLUMNS, split_axis=0, concat_axis=0, tiled=True)
    ada_bias_grad = jnp.sum(got, axis=0)
    ada_weight_grad = jnp.dot(silu_all.astype(f32).T, got, precision=lax.Precision.HIGHEST, preferred_element_type=f32)
    sum_b = fold_step(sum_b, order_a, 3)
    for step in range(4, last):
        sum_a, sum_b = fold_step(sum_a, order_a, step), fold_step(sum_b, order_a, step)
    grad_back = swap(jnp.concatenate([sum_a, sum_b, grad_out.astype(f32)], axis=1))
    flat = packed[:, unit_slots * width :].reshape(-1)[: flat_rows * width].reshape(flat_rows, width)
    down_sum = flat[:lowrank].reshape(width, lowrank)
    up_sum = flat[lowrank : 2 * lowrank]
    taps_sum = flat[2 * lowrank : 2 * lowrank + 9]
    bias_sum = flat[2 * lowrank + 9]
    gain_sum = flat[2 * lowrank + 10, :HDIM]
    grad_silu = jnp.sum(packed[:, : unit_slots * width].reshape(2 * dq, unit_slots, width), axis=0)
    own_cond = lax.dynamic_slice_in_dim(condition, (2 * lax.axis_index("dq") + core) * unit_slots, unit_slots, 0)
    gate = jax.nn.sigmoid(own_cond)
    cond_grad = grad_silu * (gate * (1.0 + own_cond * (1.0 - gate)))
    proj_grad = grad_back[:, : 4 * inner].reshape(-1, 2, 4, inner // 2).transpose(2, 0, 1, 3).reshape(4, -1, inner)
    return (
        block_out, input_grad, cond_grad, ada_weight_grad, ada_bias_grad, proj_grad, down_sum, up_sum, bias_sum,
        gain_sum, taps_sum, grad_back[:, 4 * inner :].T, fc1_grad, fc2_grad,
    )


def solution(mesh):
    dp, mp = mesh.shape["dp"], mesh.shape["mp"]
    split = Mesh(mesh.devices.reshape(dp // 2, 2, mp), ("dq", "core", "mp"))
    d = ("dq", "core")
    every = ("dq", "core", "mp")
    return jax.shard_map(
        on_device,
        mesh=split,
        in_specs=(
            P(every, None), P(every, None), P(), P(), P(d), P(d), P(d), P(None, d), P(d), P(None, d, "mp"),
            P(), P(), P(), P(), P(), P("mp", d), P(d, "mp"), P("mp", d),
        ),
        out_specs=(
            P(every, None), P(every, None), P(d, None), P(None, d), P(d), P(None, d, "mp"),
            P(), P(), P(), P(), P(), P("mp", d), P(d, "mp"), P("mp", d),
        ),
        check_vma=False,
    )
```

```python
import functools
import math

import jax
import jax.numpy as jnp
from jax import lax
from jax.experimental import pallas as pl
from jax.experimental.pallas import tpu as pltpu
from jax.sharding import Mesh
from jax.sharding import PartitionSpec as P

f32=jnp.float32; bf16=jnp.bfloat16
HDIM=72; SIDE=16; LANES=128; CHUNK=128; MARGIN=64
LEVELS=(64,32,16,8,4,2,1)
GATE_NORM=16.0; head_eps=1e-5
LOG2E=math.log2(math.e)

def cost(us):
    return pl.CostEstimate(flops=us*900*10**6, bytes_accessed=10**6, transcendentals=0)

def parts(x, n):
    out=[]
    for _ in range(n-1):
        p=x.astype(bf16); out.append(p); x=x-p.astype(f32)
    out.append(x.astype(bf16)); return out

def mm(a,b,ca,cb):
    return lax.dot_general(a,b,(((ca,),(cb,)),((),())),preferred_element_type=f32)

def mmx(a,b,ca,cb,n):
    if n==1: return mm(a.astype(bf16),b.astype(bf16),ca,cb)
    ah,al=parts(a,2); bh,bl=parts(b,2)
    return mm(ah,bh,ca,cb)+(mm(ah,bl,ca,cb)+mm(al,bh,ca,cb))

def sel_mm(m,x,n):
    ps=parts(x,n)
    r=mm(m,ps[-1],1,0)
    for p in ps[-2::-1]: r=mm(m,p,1,0)+r
    return r

def iota2(shape,d): return lax.broadcasted_iota(jnp.int32,shape,d)

def level_matrix():
    i=iota2((CHUNK,CHUNK),0); j=iota2((CHUNK,CHUNK),1)
    x=i^j
    lvl=jnp.zeros((CHUNK,CHUNK),jnp.int32)
    for b in LEVELS[::-1]: lvl=jnp.where(x>=b,b,lvl)
    return lvl,i,j

def level_ops(q,k,L,lw):
    row=iota2((CHUNK,LANES),0)
    out=[]
    for b in LEVELS:
        n=CHUNK//(2*b)
        if b>=8:
            L3=L.reshape(n,2*b,LANES); D=L3-L3[:,b-1:b,:]
            E=jnp.exp2(-jnp.abs(D)).reshape(CHUNK,LANES)
            q3=q.reshape(n,2*b,LANES); k3=k.reshape(n,2*b,LANES)
            X=jnp.concatenate([k3[:,:b],q3[:,b:]],axis=1).reshape(CHUNK,LANES)
        else:
            right=(row&b)!=0
            X=jnp.where(right,q,k)
            L3=L.reshape(CHUNK//8,8,LANES)
            if b==4:
                D=(L3-L3[:,3:4,:]).reshape(CHUNK,LANES); E=jnp.exp2(-jnp.abs(D))
            elif b==2:
                s=lax.broadcasted_iota(jnp.int32,L3.shape,1)
                R=jnp.where(s<4,L3[:,1:2,:],L3[:,5:6,:])
                E=jnp.exp2(-jnp.abs(L3-R)).reshape(CHUNK,LANES)
            else:
                E=jnp.exp2(jnp.where(right,lw,0.0))
        out.append((b,E,X*E))
    return out

def log_decay2(pre):
    return (jnp.minimum(pre,0.0)-jnp.log1p(jnp.exp(-jnp.abs(pre))))*(LOG2E/GATE_NORM)

def image_masks(base,rows,width,height):
    p=iota2((rows,LANES),0)+base
    col=p&(width-1)
    r=(p//width)&(height-1)
    return col,r

def conv_forward(vp,up,um,taps,store,total,width,height):
    tiles=total//CHUNK
    for t in range(tiles):
        o=MARGIN+t*CHUNK
        col,_=image_masks(0,CHUNK,width,height)
        c=vp[o:o+CHUNK,:]
        left=jnp.where(col!=0,vp[o-1:o-1+CHUNK,:],0.0)
        right=jnp.where(col!=width-1,vp[o+1:o+1+CHUNK,:],0.0)
        def comb(a): return left*taps[3*a:3*a+1,:]+c*taps[3*a+1:3*a+2,:]+right*taps[3*a+2:3*a+3,:]
        um[o:o+CHUNK,:]=comb(0)
        store(t,comb(1))
        up[o:o+CHUNK,:]=comb(2)

def conv_finish(up,um,add,total,width,height):
    for t in range(total//CHUNK):
        o=MARGIN+t*CHUNK
        _,r=image_masks(t*CHUNK,CHUNK,width,height)
        down=jnp.where(r!=height-1,up[o+width:o+width+CHUNK,:],0.0)
        upv=jnp.where(r!=0,um[o-width:o-width+CHUNK,:],0.0)
        add(t,down+upv)

def fwd_kernel(PS,PA,total,big_ref,q_ref,k_ref,v_ref,g_ref,p_ref,taps_ref,gain_ref,mixed_ref,comb_ref,a_ref,s_ref,vp,up,um,lvl_ref,tri_ref,st):
    chunks=total//CHUNK
    @pl.when(pl.program_id(0)==0)
    def _():
        lvl,i,j=level_matrix()
        lvl_ref[...]=jnp.where(i>j,lvl,jnp.where(i==j,-1,-2))
        tri_ref[...]=jnp.where(i>=j,1.0,0.0).astype(bf16)
        z=jnp.zeros((MARGIN,LANES),f32)
        for r in (vp,up,um):
            r[0:MARGIN,:]=z; r[MARGIN+total:,:]=z
    big=big_ref[0]==4*SIDE*SIDE
    taps=taps_ref[0]; gain=gain_ref[...]
    vp[MARGIN:MARGIN+total,:]=v_ref[0]
    def conv(width):
        def store(t,x): comb_ref[0,t*CHUNK:(t+1)*CHUNK,:]=x
        def add(t,x): comb_ref[0,t*CHUNK:(t+1)*CHUNK,:]+=x
        conv_forward(vp,up,um,taps,store,total,width,width)
        conv_finish(up,um,add,total,width,width)
    @pl.when(big)
    def _(): conv(2*SIDE)
    @pl.when(jnp.logical_not(big))
    def _(): conv(SIDE)
    per=SIDE*SIDE//CHUNK
    def step(c,_):
        rows=pl.ds(pl.multiple_of(c*CHUNK,CHUNK),CHUNK)
        start=jnp.where(big,c==0,lax.rem(c,per)==0)
        S=jnp.where(start,0.0,st[...])
        s_ref[0,c]=S
        q=q_ref[0,rows,:]*(HDIM**-0.5); k=k_ref[0,rows,:]; v=v_ref[0,rows,:]
        lw=log_decay2(p_ref[0,rows,:])
        L=sel_mm(tri_ref[...],lw,3)
        lvl=lvl_ref[...]
        diag=jnp.sum(q*k,axis=1,keepdims=True)
        A=jnp.where(lvl==-1,diag,0.0)
        for b,E,W in level_ops(q,k,L,lw):
            if b>=8:
                n=CHUNK//(2*b)
                late=W.reshape(n,2*b,LANES)[:,b:].reshape(CHUNK//2,LANES)
                part=mmx(late,W,1,1,PS).reshape(n,b,CHUNK)
                A3=A.reshape(n,2*b,CHUNK)
                part=jnp.where(lvl.reshape(n,2*b,CHUNK)[:,b:]==b,part,A3[:,b:])
                A=jnp.concatenate([A3[:,:b],part],axis=1).reshape(CHUNK,CHUNK)
            else:
                A=jnp.where(lvl==b,mmx(W,W,1,1,PS),A)
        a_ref[0,c]=A.astype(a_ref.dtype)
        last=L[CHUNK-1:CHUNK,:]
        o=mmx(A,v,1,0,PA)+mmx(q*jnp.exp2(L),S,1,1,PA)
        st[...]=S*jnp.exp2(last)+mmx(v,k*jnp.exp2(last-L),0,0,PA)
        cb=comb_ref[0,rows,:]+o
        comb_ref[0,rows,:]=cb
        g=g_ref[0,rows,:]
        r=lax.rsqrt(jnp.sum(cb*cb,axis=1,keepdims=True)*(1.0/HDIM)+head_eps)
        mixed_ref[0,rows,:]=(cb*r*gain*(g/(1.0+jnp.exp(-g)))).astype(bf16)
        return 0
    lax.fori_loop(0,chunks,step,0,unroll=4)

def gla_forward(big,qkvg,pre,taps,gain,PS=1,PA=2,adt=f32):
    _,H,total,_=qkvg.shape; chunks=total//CHUNK
    row=pl.BlockSpec((1,total,LANES),lambda h:(h,0,0))
    def of(i): return pl.BlockSpec((None,1,total,LANES),lambda h:(i,h,0,0))
    return pl.pallas_call(
        functools.partial(fwd_kernel,PS,PA,total),
        grid=(H,),
        in_specs=[pl.BlockSpec(memory_space=pltpu.SMEM)]+[of(i) for i in range(4)]+[row]+[pl.BlockSpec((1,16,LANES),lambda h:(h,0,0)),pl.BlockSpec((1,LANES),lambda h:(0,0))],
        out_specs=[row,row,pl.BlockSpec((1,chunks,CHUNK,CHUNK),lambda h:(h,0,0,0)),pl.BlockSpec((1,chunks,LANES,LANES),lambda h:(h,0,0,0))],
        out_shape=[jax.ShapeDtypeStruct((H,total,LANES),bf16),jax.ShapeDtypeStruct((H,total,LANES),f32),
                   jax.ShapeDtypeStruct((H,chunks,CHUNK,CHUNK),adt),jax.ShapeDtypeStruct((H,chunks,LANES,LANES),f32)],
        scratch_shapes=[pltpu.VMEM((total+2*MARGIN,LANES),f32)]*3+[pltpu.VMEM((CHUNK,CHUNK),jnp.int32),pltpu.VMEM((CHUNK,CHUNK),bf16),pltpu.VMEM((LANES,LANES),f32)],
        compiler_params=pltpu.CompilerParams(vmem_limit_bytes=40*2**20,dimension_semantics=("arbitrary",)),
        name="gla_forward", cost_estimate=cost(65),
    )(big,qkvg,qkvg,qkvg,qkvg,pre,taps,gain)

def bwd_kernel(PS,PA,total,big_ref,q_ref,k_ref,v_ref,g_ref,p_ref,comb_ref,a_ref,s_ref,gm_ref,taps_ref,gain_ref,
               dqk_ref,dpre_ref,dtaps_ref,dvec_ref,vp,dcp,gl,gr,dvl,mask_ref,tri_ref,ds,car):
    chunks=total//CHUNK
    @pl.when(pl.program_id(0)==0)
    def _():
        lvl,i,j=level_matrix()
        for at,b in enumerate(LEVELS): mask_ref[at]=jnp.where(lvl==b,1.0,0.0).astype(bf16)
        tri_ref[0]=jnp.where(i>=j,1.0,0.0).astype(bf16)
        tri_ref[1]=jnp.where(i<=j,1.0,0.0).astype(bf16)
        z=jnp.zeros((MARGIN,LANES),f32)
        for r in (vp,dcp,gl,gr):
            r[0:MARGIN,:]=z; r[MARGIN+total:,:]=z
    big=big_ref[0]==4*SIDE*SIDE
    taps=taps_ref[0]; gain=gain_ref[...]
    vp[MARGIN:MARGIN+total,:]=v_ref[0]
    def rowwise(c,acc):
        rows=pl.ds(pl.multiple_of(c*CHUNK,CHUNK),CHUNK)
        cb=comb_ref[0,rows,:]; g=g_ref[0,rows,:]; gm=gm_ref[0,rows,:].astype(f32)
        r=lax.rsqrt(jnp.sum(cb*cb,axis=1,keepdims=True)*(1.0/HDIM)+head_eps)
        n=cb*r
        sg=1.0/(1.0+jnp.exp(-g)); silu=g*sg
        dqk_ref[3,0,rows,:]=(gm*n*gain*(sg+silu*(1.0-sg))).astype(bf16)
        dn=gm*silu
        acc=acc+jnp.sum((dn*n).reshape(CHUNK//8,8,LANES),axis=0)
        dn=dn*gain
        dc=r*(dn-n*(jnp.sum(dn*n,axis=1,keepdims=True)*(1.0/HDIM)))
        dcp[pl.ds(pl.multiple_of(MARGIN+c*CHUNK,MARGIN),CHUNK),:]=dc
        return acc
    dgain=lax.fori_loop(0,chunks,rowwise,jnp.zeros((8,LANES),f32))
    dvec_ref[0,0:1,:]=jnp.sum(dgain,axis=0,keepdims=True)
    def conv(width):
        height=width
        accs=[jnp.zeros((8,LANES),f32) for _ in range(9)]
        for t in range(chunks):
            o=MARGIN+t*CHUNK
            col,r=image_masks(t*CHUNK,CHUNK,width,height)
            zs=[jnp.where(r!=height-1,dcp[o+width:o+width+CHUNK,:],0.0),dcp[o:o+CHUNK,:],jnp.where(r!=0,dcp[o-width:o-width+CHUNK,:],0.0)]
            vs=[jnp.where(col!=0,vp[o-1:o-1+CHUNK,:],0.0),vp[o:o+CHUNK,:],jnp.where(col!=width-1,vp[o+1:o+1+CHUNK,:],0.0)]
            for a in range(3):
                for b in range(3):
                    accs[3*a+b]=accs[3*a+b]+jnp.sum((zs[a]*vs[b]).reshape(CHUNK//8,8,LANES),axis=0)
            def comb(b): return zs[0]*taps[b:b+1,:]+zs[1]*taps[3+b:4+b,:]+zs[2]*taps[6+b:7+b,:]
            gl[o:o+CHUNK,:]=comb(0)
            dvl[t*CHUNK:(t+1)*CHUNK,:]=comb(1)
            gr[o:o+CHUNK,:]=comb(2)
        for i in range(9):
            dtaps_ref[0,i:i+1,:]=jnp.sum(accs[i],axis=0,keepdims=True)
        for t in range(chunks):
            o=MARGIN+t*CHUNK
            col,_=image_masks(0,CHUNK,width,height)
            dvl[t*CHUNK:(t+1)*CHUNK,:]+=jnp.where(col!=width-1,gl[o+1:o+1+CHUNK,:],0.0)+jnp.where(col!=0,gr[o-1:o-1+CHUNK,:],0.0)
    @pl.when(big)
    def _(): conv(2*SIDE)
    @pl.when(jnp.logical_not(big))
    def _(): conv(SIDE)
    per=SIDE*SIDE//CHUNK
    row=iota2((CHUNK,LANES),0)
    def step(i,acc):
        c=chunks-1-i
        rows=pl.ds(pl.multiple_of(c*CHUNK,CHUNK),CHUNK)
        end=jnp.where(big,c==chunks-1,lax.rem(c,per)==per-1)
        dS=jnp.where(end,0.0,ds[...])
        carry=jnp.where(end,0.0,car[0:1,:])
        q=q_ref[0,rows,:]*(HDIM**-0.5); k=k_ref[0,rows,:]; v=v_ref[0,rows,:]
        pre=p_ref[0,rows,:]
        lw=log_decay2(pre)
        L=sel_mm(tri_ref[0],lw,3)
        do=dcp[pl.ds(pl.multiple_of(MARGIN+c*CHUNK,MARGIN),CHUNK),:]
        low=tri_ref[0].astype(f32)>0.5
        G=jnp.where(low,mmx(do,v,1,1,PS),mmx(v,do,1,1,PS))
        last=L[CHUNK-1:CHUNK,:]
        eL=jnp.exp2(L); eR=jnp.exp2(last-L)
        S=s_ref[0,c]
        dq=eL*mmx(do,S,1,0,PA)
        kR=k*eR
        dk=eR*mmx(v,dS,1,0,PA)
        dv=dvl[rows,:]+mmx(a_ref[0,c].astype(f32),do,0,0,PA)+mmx(kR,dS,1,1,PA)
        ds[...]=dS*jnp.exp2(last)+mmx(do,q*eL,0,0,PA)
        Gs=parts(G,PS)
        for at,(b,E,W) in enumerate(level_ops(q,k,L,lw)):
            Gb=[g*mask_ref[at] for g in Gs]
            if PS==1:
                Y=E*mm(Gb[0],W.astype(bf16),1,0)
            else:
                Wh,Wl=parts(W,2)
                Y=E*(mm(jnp.concatenate(Gb,axis=1),jnp.concatenate([Wh,Wh],axis=0),1,0)+mm(Gb[0],Wl,1,0))
            if b>=8:
                n=CHUNK//(2*b)
                Y=Y.reshape(n,2*b,LANES); q3=dq.reshape(n,2*b,LANES); k3=dk.reshape(n,2*b,LANES)
                dq=jnp.concatenate([q3[:,:b],q3[:,b:]+Y[:,b:]],axis=1).reshape(CHUNK,LANES)
                dk=jnp.concatenate([k3[:,:b]+Y[:,:b],k3[:,b:]],axis=1).reshape(CHUNK,LANES)
            else:
                late=jnp.where((row&b)!=0,Y,0.0)
                dq=dq+late; dk=dk+(Y-late)
        z=q*dq-k*dk
        suf=sel_mm(tri_ref[1],z,3)+carry
        car[0:1,:]=suf[0:1,:]
        dp=suf*((1.0/GATE_NORM)/(1.0+jnp.exp(pre)))
        dpre_ref[0,rows,:]=dp
        t=jnp.sum(do*v,axis=1,keepdims=True)
        dqk_ref[0,0,rows,:]=((dq+t*k)*(HDIM**-0.5)).astype(bf16)
        dqk_ref[1,0,rows,:]=(dk+t*q).astype(bf16)
        dqk_ref[2,0,rows,:]=dv.astype(bf16)
        return acc+jnp.sum(dp.reshape(CHUNK//8,8,LANES),axis=0)
    db=lax.fori_loop(0,chunks,step,jnp.zeros((8,LANES),f32),unroll=4)
    dvec_ref[0,1:2,:]=jnp.sum(db,axis=0,keepdims=True)

def gla_backward(base,count,big,qkvg,pre,comb,A,S,gm,taps,gain,PS=2,PA=2):
    _,H,total,_=qkvg.shape; chunks=total//CHUNK
    row=pl.BlockSpec((1,total,LANES),lambda h:(h+base,0,0))
    out=pl.BlockSpec((1,total,LANES),lambda h:(h,0,0))
    def of(i): return pl.BlockSpec((None,1,total,LANES),lambda h:(i,h+base,0,0))
    return pl.pallas_call(
        functools.partial(bwd_kernel,PS,PA,total),
        grid=(count,),
        in_specs=[pl.BlockSpec(memory_space=pltpu.SMEM)]+[of(i) for i in range(4)]+[row]*2+[pl.BlockSpec((1,chunks,CHUNK,CHUNK),lambda h:(h+base,0,0,0)),pl.BlockSpec((1,chunks,LANES,LANES),lambda h:(h+base,0,0,0)),row,
                  pl.BlockSpec((1,16,LANES),lambda h:(h+base,0,0)),pl.BlockSpec((1,LANES),lambda h:(0,0))],
        out_specs=[pl.BlockSpec((4,1,total,LANES),lambda h:(0,h,0,0)),out,pl.BlockSpec((1,16,LANES),lambda h:(h,0,0)),pl.BlockSpec((1,8,LANES),lambda h:(h,0,0))],
        out_shape=[jax.ShapeDtypeStruct((4,count,total,LANES),bf16),jax.ShapeDtypeStruct((count,total,LANES),f32),
                   jax.ShapeDtypeStruct((count,16,LANES),f32),jax.ShapeDtypeStruct((count,8,LANES),f32)],
        scratch_shapes=[pltpu.VMEM((total+2*MARGIN,LANES),f32)]*4+[pltpu.VMEM((total,LANES),f32),pltpu.VMEM((len(LEVELS),CHUNK,CHUNK),bf16),pltpu.VMEM((2,CHUNK,CHUNK),bf16),pltpu.VMEM((LANES,LANES),f32),pltpu.VMEM((8,LANES),f32)],
        compiler_params=pltpu.CompilerParams(vmem_limit_bytes=48*2**20,dimension_semantics=("arbitrary",)),
        name="gla_backward", cost_estimate=cost(10*count),
    )(big,qkvg,qkvg,qkvg,qkvg,pre,comb,A,S,gm,taps,gain)


ROWS = 256


def head_window(res, column):
    base = column // LANES * LANES
    off = column - base
    width = LANES if off + HDIM <= LANES else 2 * LANES
    part = res[:, base : base + width]
    if off:
        part = pltpu.roll(part, width - off, 1)
    part = part[:, :LANES]
    return jnp.where(iota2(part.shape, 1) < HDIM, part, 0.0)


def heads_joined(pieces):
    blocks = [None] * (len(pieces) * HDIM // LANES + 1)

    def put(index, value):
        blocks[index] = value if blocks[index] is None else blocks[index] + value

    for h, x in enumerate(pieces):
        index, off = h * HDIM // LANES, h * HDIM % LANES
        if off == 0:
            put(index, x)
            continue
        r = pltpu.roll(x, off, 1)
        if off + HDIM <= LANES:
            put(index, r)
        else:
            lane = iota2(r.shape, 1)
            put(index, jnp.where(lane >= off, r, 0.0))
            put(index + 1, jnp.where(lane < off, r, 0.0))
    total = len(pieces) * HDIM
    blocks = [b for b in blocks if b is not None]
    return jnp.concatenate(blocks, axis=1)[:, :total]


def first_rows(tiles, width):
    return pl.BlockSpec((ROWS, width), lambda i, t: (jnp.minimum(i, tiles // 2 - 1), 0))


def last_rows(tiles, width):
    return pl.BlockSpec((ROWS, width), lambda i, t: (jnp.maximum(i - tiles // 2, 0), 0))


def put_half(half, value, own_ref, away_ref):
    @pl.when(pl.program_id(0) < half)
    def _():
        own_ref[...] = value.astype(own_ref.dtype)

    @pl.when(pl.program_id(0) >= half)
    def _():
        away_ref[...] = value.astype(away_ref.dtype)


def project_kernel(H, half, turn_ref, x_ref, y_ref, wa_ref, wb_ref, down_ref, up_ref, bias_ref, out_ref, pre_ref, lat_ref):
    x = jnp.where(pl.program_id(0) < half, x_ref[...], y_ref[...])
    span = 2 * H * HDIM
    for s in range(2):
        res = mm(x, (wa_ref, wb_ref)[s][:, :span], 1, 0)
        for i in range(2 * H):
            out_ref[2 * i // H, s * (H // 2) + i % (H // 2)] = head_window(res, i * HDIM)
    latent = mm(x, down_ref[...], 1, 0)
    lat_ref[...] = latent
    pre = bias_ref[...] + sum(mm(p, up_ref[...], 1, 0) for p in parts(latent, 3)[::-1])
    for h in range(H):
        pre_ref[h] = pre[:, h * LANES : (h + 1) * LANES]


def project(turn, x, away, wa, wb, down, up, bias, H):
    total, width = 2 * x.shape[0], x.shape[1]
    tiles = total // ROWS

    def turned(i, t):
        return lax.rem(i + t[0], tiles)

    full = lambda a: pl.BlockSpec(a.shape, lambda i, t: (0, 0))
    return pl.pallas_call(
        functools.partial(project_kernel, H, tiles // 2),
        grid_spec=pltpu.PrefetchScalarGridSpec(
            num_scalar_prefetch=1,
            grid=(tiles,),
            in_specs=[first_rows(tiles, width), last_rows(tiles, width), full(wa), full(wb), full(down), full(up), full(bias)],
            out_specs=[
                pl.BlockSpec((4, H, ROWS, LANES), lambda i, t: (0, 0, turned(i, t), 0)),
                pl.BlockSpec((H, ROWS, LANES), lambda i, t: (0, turned(i, t), 0)),
                pl.BlockSpec((ROWS, LANES), lambda i, t: (turned(i, t), 0)),
            ],
        ),
        out_shape=[
            jax.ShapeDtypeStruct((4, H, total, LANES), f32),
            jax.ShapeDtypeStruct((H, total, LANES), f32),
            jax.ShapeDtypeStruct((total, LANES), f32),
        ],
        compiler_params=pltpu.CompilerParams(vmem_limit_bytes=56 * 2**20, dimension_semantics=("arbitrary",)),
        name="project", cost_estimate=cost(15),
    )(turn, x, away, wa, wb, down, up, bias)


def attend_kernel(H, half, turn_ref, m_ref, w_ref, own_ref, away_ref, cat_ref):
    cat = heads_joined([m_ref[h].astype(f32) for h in range(H)]).astype(bf16)
    cat_ref[...] = cat
    put_half(half, mm(cat, w_ref[...], 1, 1), own_ref, away_ref)


def attend(turn, mixed, w):
    H, total, _ = mixed.shape
    tiles = total // ROWS
    inner = H * HDIM
    return pl.pallas_call(
        functools.partial(attend_kernel, H, tiles // 2),
        grid_spec=pltpu.PrefetchScalarGridSpec(
            num_scalar_prefetch=1,
            grid=(tiles,),
            in_specs=[
                pl.BlockSpec((H, ROWS, LANES), lambda i, t: (0, lax.rem(i + t[0], tiles), 0)),
                pl.BlockSpec(w.shape, lambda i, t: (0, 0)),
            ],
            out_specs=[first_rows(tiles, w.shape[0]), last_rows(tiles, w.shape[0]), pl.BlockSpec((ROWS, inner), lambda i, t: (i, 0))],
        ),
        out_shape=[jax.ShapeDtypeStruct((total // 2, w.shape[0]), f32)] * 2 + [jax.ShapeDtypeStruct((total, inner), bf16)],
        compiler_params=pltpu.CompilerParams(vmem_limit_bytes=40 * 2**20, dimension_semantics=("arbitrary",)),
        name="attend", cost_estimate=cost(4),
    )(turn, mixed, w)


def attend_back_kernel(H, turn_ref, g_ref, w_ref, out_ref):
    res = mm(g_ref[...], w_ref[...], 1, 0)
    res = jnp.concatenate([res, jnp.zeros((ROWS, -res.shape[1] % LANES), f32)], axis=1)
    for h in range(H):
        out_ref[h] = head_window(res, h * HDIM)


def attend_back(turn, grad, w, H):
    total, width = grad.shape
    tiles = total // ROWS
    return pl.pallas_call(
        functools.partial(attend_back_kernel, H),
        grid_spec=pltpu.PrefetchScalarGridSpec(
            num_scalar_prefetch=1,
            grid=(tiles,),
            in_specs=[pl.BlockSpec((ROWS, width), lambda i, t: (i, 0)), pl.BlockSpec(w.shape, lambda i, t: (0, 0))],
            out_specs=pl.BlockSpec((H, ROWS, LANES), lambda i, t: (0, lax.rem(i + t[0], tiles), 0)),
        ),
        out_shape=jax.ShapeDtypeStruct((H, total, LANES), f32),
        compiler_params=pltpu.CompilerParams(vmem_limit_bytes=40 * 2**20, dimension_semantics=("arbitrary",)),
        name="attend_back", cost_estimate=cost(4),
    )(turn, grad, w)


def join_kernel(H, turn_ref, d_ref, cat_ref):
    cat_ref[...] = heads_joined([d_ref[i // H, i % H].astype(f32) for i in range(4 * H)]).astype(bf16)


def join(turn, d):
    _, H, total, _ = d.shape
    tiles = total // ROWS
    cols = 4 * H * HDIM
    return pl.pallas_call(
        functools.partial(join_kernel, H),
        grid_spec=pltpu.PrefetchScalarGridSpec(
            num_scalar_prefetch=1,
            grid=(tiles,),
            in_specs=[pl.BlockSpec((4, H, ROWS, LANES), lambda i, t: (0, 0, lax.rem(i + t[0], tiles), 0))],
            out_specs=pl.BlockSpec((ROWS, cols), lambda i, t: (i, 0)),
        ),
        out_shape=jax.ShapeDtypeStruct((total, cols), bf16),
        compiler_params=pltpu.CompilerParams(vmem_limit_bytes=40 * 2**20, dimension_semantics=("arbitrary",)),
        name="join", cost_estimate=cost(4),
    )(turn, d)


def project_back_kernel(H, half, turn_ref, x_ref, cata_ref, catb_ref, pa_ref, pb_ref, lat_ref, wa_ref, wb_ref, down_ref, up_ref, own_ref, away_ref, ddown_ref, dup_ref):
    @pl.when(pl.program_id(0) == 0)
    def _():
        dup_ref[...] = jnp.zeros_like(dup_ref)
        ddown_ref[...] = jnp.zeros_like(ddown_ref)

    lat = parts(lat_ref[...], 2)
    dp = parts(jnp.concatenate([p[h] for p in (pa_ref, pb_ref) for h in range(H // 2)], axis=1), 2)
    glat = mm(dp[1], up_ref[...], 1, 1) + mm(dp[0], up_ref[...], 1, 1)
    dup_ref[...] += mm(lat[0], dp[1], 0, 0) + mm(lat[1], dp[0], 0, 0) + mm(lat[0], dp[0], 0, 0)
    split = parts(glat, 2)[::-1]
    ddown_ref[...] += sum(mm(p, x_ref[...], 0, 0) for p in split)
    acc = sum(mm(p, down_ref[...], 1, 1) for p in split)
    acc = acc + mm(cata_ref[...], wa_ref[:, : cata_ref.shape[1]], 1, 1) + mm(catb_ref[...], wb_ref[:, : catb_ref.shape[1]], 1, 1)
    put_half(half, acc, own_ref, away_ref)


def project_back(turn, x, cat_a, cat_b, dpre_a, dpre_b, latent, wa, wb, down, up):
    H, total = 2 * dpre_a.shape[0], dpre_a.shape[1]
    tiles = total // ROWS
    width, cols = x.shape[1], cat_a.shape[1]

    def turned(i, t):
        return lax.rem(i + t[0], tiles)

    full = lambda a: pl.BlockSpec(a.shape, lambda i, t: (0, 0))
    return pl.pallas_call(
        functools.partial(project_back_kernel, H, tiles // 2),
        grid_spec=pltpu.PrefetchScalarGridSpec(
            num_scalar_prefetch=1,
            grid=(tiles,),
            in_specs=[
                pl.BlockSpec((ROWS, width), lambda i, t: (i, 0)),
                pl.BlockSpec((ROWS, cols), lambda i, t: (i, 0)),
                pl.BlockSpec((ROWS, cols), lambda i, t: (i, 0)),
                pl.BlockSpec((H // 2, ROWS, LANES), lambda i, t: (0, turned(i, t), 0)),
                pl.BlockSpec((H // 2, ROWS, LANES), lambda i, t: (0, turned(i, t), 0)),
                pl.BlockSpec((ROWS, LANES), lambda i, t: (turned(i, t), 0)),
                full(wa), full(wb), full(down), full(up),
            ],
            out_specs=[
                first_rows(tiles, width),
                last_rows(tiles, width),
                pl.BlockSpec((LANES, width), lambda i, t: (0, 0)),
                pl.BlockSpec((LANES, H * LANES), lambda i, t: (0, 0)),
            ],
        ),
        out_shape=[
            jax.ShapeDtypeStruct((total // 2, width), f32),
            jax.ShapeDtypeStruct((total // 2, width), f32),
            jax.ShapeDtypeStruct((LANES, width), f32),
            jax.ShapeDtypeStruct((LANES, H * LANES), f32),
        ],
        compiler_params=pltpu.CompilerParams(vmem_limit_bytes=56 * 2**20, dimension_semantics=("arbitrary",)),
        name="project_back", cost_estimate=cost(2),
    )(turn, x, cat_a, cat_b, dpre_a, dpre_b, latent, wa, wb, down, up)


NORM_EPS = 1e-06
FLIP = [(0, 1), (1, 0)]
COLUMNS = ("dq", "core")


def swap(x):
    away = lax.ppermute(x, ("core", "mp"), [(1, 2), (2, 1)])
    return jnp.where(lax.axis_index("core") == lax.axis_index("mp"), x, away)


def other(x):
    return lax.ppermute(x, "core", FLIP)


def both(x):
    return jnp.concatenate([x, other(x)], axis=0)


def summed(x):
    half = x.shape[0] // 2
    return x[:half] + other(x[half:])


def across(x):
    return lax.ppermute(x, "mp", FLIP)


def bits():
    count = lax.axis_size("dq").bit_length() - 1
    return [("dq", count - 1 - i) for i in range(count)] + [("mp", 0)]


def flipped(x, bit):
    axis, place = bit
    return lax.ppermute(x, axis, [(i, i ^ (1 << place)) for i in range(lax.axis_size(axis))])


def own_bit(bit):
    return (lax.axis_index(bit[0]) >> bit[1]) & 1


def orders():
    count = len(bits())
    far = list(range(count - 2))
    return far + [count - 1, count - 2], far + [count - 2, count - 1]


def spread(x, order, steps, work=()):
    names = bits()
    for step in steps:
        place = order[step]
        away, mine = flipped(x, names[place]), own_bit(names[place])
        at = sum(h < place for h in order[:step])
        x = after(x, *work) if work else x
        x = jnp.stack([jnp.where(mine == 0, x, away), jnp.where(mine == 0, away, x)], axis=at)
    return x.reshape(-1, x.shape[-1]) if len(order) - 1 in steps else x


def fold_split(x, order, step):
    names = bits()
    if step == 0:
        x = x.reshape((2,) * len(names) + (-1, x.shape[-1]))
    left = sorted(order[: len(order) - step])
    place = order[len(order) - 1 - step]
    at, mine = left.index(place), own_bit(names[place])
    return lax.dynamic_index_in_dim(x, 1 - mine, at, keepdims=False), lax.dynamic_index_in_dim(x, mine, at, keepdims=False)


def fold_sum(split, order, step, work=()):
    send, keep = split
    keep = after(keep, *work) if work else keep
    x = keep.astype(f32) + flipped(send, bits()[order[len(order) - 1 - step]]).astype(f32)
    return x if step == len(order) - 1 else x.astype(bf16)


def fold_step(x, order, step):
    return fold_sum(fold_split(x, order, step), order, step)


def after(x, *first):
    marks = sum(f[(0,) * f.ndim].astype(f32) for f in first)
    return jnp.where(jnp.isnan(marks), jnp.zeros_like(x), x)


def modulate(rows, shift, scale):
    center = rows - jnp.mean(rows, axis=-1, keepdims=True)
    normed = center * lax.rsqrt(jnp.mean(center * center, axis=-1, keepdims=True) + NORM_EPS)
    return normed * (1.0 + scale[:, None, :]) + shift[:, None, :]


def per_head(x, heads, rows):
    x = x.reshape(x.shape[0], heads, HDIM)
    return jnp.pad(x, ((0, rows - x.shape[0]), (0, 0), (0, LANES - HDIM)))


def contract(a, b, i, j):
    return lax.dot_general(a, b, (((i,), (j,)), ((), ())), preferred_element_type=f32)


def silu(v):
    return v * jax.nn.sigmoid(v)


def on_device(
    block_input, out_grad, time_table, class_table, time_ids, class_ids, image_patches, ada_weight, ada_bias,
    proj_weight, decay_down, decay_up, decay_bias, head_gain, conv_taps, out_weight, fc1_weight, fc2_weight,
):
    rows, width = block_input.shape
    inner = proj_weight.shape[2]
    heads = inner // HDIM
    core = lax.axis_index("core")
    y = lax.axis_index("mp")
    dq = lax.axis_size("dq")
    slot_rows = SIDE * SIDE
    own_slots = rows // slot_rows
    unit_slots = 2 * own_slots

    cut = 2 * inner
    order_a, order_b = orders()
    last = len(order_a)
    w_part = swap(proj_weight.reshape(4, -1, 2, inner // 2).transpose(1, 2, 0, 3).reshape(-1, 4 * inner))
    w_out = swap(out_weight.T)
    w_a = spread(w_part[:, :cut], order_a, range(1))
    w_b = spread(w_part[:, cut:], order_b, range(1))

    ids = jnp.concatenate([time_ids, class_ids, image_patches])[None]
    ids = after(ids, w_part, w_out)
    w_out = lax.all_gather(w_out, ("dq", "mp"), axis=0, tiled=True)
    ids = lax.all_to_all(jnp.broadcast_to(ids, (2 * dq, ids.shape[1])), COLUMNS, split_axis=0, concat_axis=0, tiled=True)
    ids = after(ids, w_a, w_b)
    away = across(after(out_grad, w_a, w_b))
    w_a = spread(w_a, order_a, range(1, last - 2))
    w_b = spread(w_b, order_b, range(1, last - 2))

    x = swap(block_input)
    t_all, c_all = ids[:, :unit_slots].reshape(-1), ids[:, unit_slots : 2 * unit_slots].reshape(-1)
    big_all = ids[:, 2 * unit_slots] == 4 * slot_rows
    me = 2 * lax.axis_index("dq") + y
    patches = lax.dynamic_slice_in_dim(ids[:, 2 * unit_slots], me, 1)
    condition = time_table[t_all].astype(f32) + class_table[c_all].astype(f32)
    silu_all = silu(condition).astype(bf16)
    columns = jnp.dot(silu_all, ada_weight, preferred_element_type=f32) + ada_bias.astype(f32)
    part = columns.shape[1]
    columns = columns.reshape(2 * dq, unit_slots, part)
    columns = jnp.where(big_all[:, None, None], columns[:, :1], columns)
    columns = lax.dynamic_index_in_dim(columns.reshape(dq, 2, 2, own_slots, part), y, 1, keepdims=False)
    columns = after(columns.reshape(2 * dq, own_slots, part), w_a, w_b)
    received = lax.all_to_all(columns, COLUMNS, split_axis=0, concat_axis=0, tiled=True)
    modulation = received.transpose(1, 0, 2).reshape(own_slots, 6 * width)
    shift1, scale1, gate1, shift2, scale2, gate2 = jnp.split(modulation, 6, axis=1)
    residual = x.astype(f32).reshape(own_slots, slot_rows, width)
    hidden, norm_back_one = jax.vjp(modulate, residual, shift1, scale1)
    hidden = hidden.reshape(rows, width).astype(bf16)
    hidden_away = other(hidden)
    hidden_all = jnp.concatenate([hidden, hidden_away], axis=0)

    start = core * inner
    up_local = lax.dynamic_slice_in_dim(decay_up, start, inner, 1)
    bias_local = lax.dynamic_slice_in_dim(decay_bias, start, inner, 0)
    taps_local = lax.dynamic_slice_in_dim(conv_taps, start, inner, 1)
    lowrank = decay_down.shape[1]
    down_pad = jnp.pad(decay_down, ((0, 0), (0, LANES - lowrank)))
    up_pad = per_head(up_local, heads, LANES).reshape(LANES, heads * LANES)
    bias_pad = per_head(bias_local[None].astype(f32), heads, 1).reshape(1, heads * LANES)
    taps_pad = per_head(taps_local.astype(f32), heads, 16).transpose(1, 0, 2)
    gain_pad = jnp.pad(head_gain.astype(f32), (0, LANES - HDIM))[None]
    turn = (core * (rows // ROWS)).astype(jnp.int32)[None]

    straight = core == y
    g_rows = jnp.where(straight, out_grad, other(away))
    g_away = jnp.where(straight, other(out_grad), away)
    w_a = spread(after(w_a, x, away), order_a, range(last - 2, last - 1))
    w_b = spread(after(w_b, x, away), order_b, range(last - 2, last - 1))
    w_a = spread(after(w_a, received), order_a, range(last - 1, last))
    w_b = spread(after(w_b, hidden), order_b, range(last - 1, last), (hidden_away, up_pad, bias_pad, taps_pad, down_pad, g_away))
    hidden_units = fc1_weight.shape[1]
    w_rest = jnp.concatenate([fc1_weight, fc2_weight.T], axis=1)
    w_rest = lax.all_gather(after(w_rest, w_a, w_b), COLUMNS, axis=0, tiled=True)
    w_fc1, w_fc2 = w_rest[:, :hidden_units], w_rest[:, hidden_units:]

    grad_rows = g_rows.astype(f32).reshape(own_slots, slot_rows, width)
    grad_feed = (grad_rows * gate2[:, None, :]).astype(bf16).reshape(rows, width)
    gate2_away = across(gate2)
    grad_feed_away = g_away.astype(f32).reshape(own_slots, slot_rows, width) * gate2_away[:, None, :]
    grad_feed_away = grad_feed_away.astype(bf16).reshape(rows, width)
    qkvg, pre, latent = project(turn, hidden, hidden_away, w_a, w_b, down_pad, up_pad, bias_pad, heads)
    mixed, comb, scores, states = gla_forward(after(patches, grad_feed_away, grad_feed), qkvg, pre, taps_pad, gain_pad)
    attn_own, attn_away, mixed_cat = attend(turn, mixed, w_out)
    attention = (attn_own + other(attn_away)).reshape(own_slots, slot_rows, width)
    after_attn = residual + gate1[:, None, :] * attention
    hidden_two, norm_back_two = jax.vjp(modulate, after_attn, shift2, scale2)
    hidden_two = hidden_two.reshape(rows, width).astype(bf16)
    hidden_two_away = across(hidden_two)

    def feed(h, g):
        active, back = jax.vjp(functools.partial(jax.nn.gelu, approximate=True), jnp.dot(h, w_fc1, preferred_element_type=f32))
        return active.astype(bf16), back(jnp.dot(g, w_fc2, preferred_element_type=f32))[0].astype(bf16)

    active, grad_up = feed(hidden_two, grad_feed)
    feed_own = contract(active, w_fc2, 1, 1)
    grad_hidden_two_own = contract(grad_up, w_fc1, 1, 1)
    hidden_two_away = after(hidden_two_away, feed_own, grad_hidden_two_own)
    active_away, grad_up_away = feed(hidden_two_away, grad_feed_away)
    grad_hidden_two_part = contract(grad_up_away, w_fc1, 1, 1).astype(bf16)
    grad_hidden_two = across(grad_hidden_two_part)
    grad_feed_all = jnp.concatenate([grad_feed, grad_feed_away], axis=0)
    hidden_two_all = jnp.concatenate([hidden_two, hidden_two_away], axis=0)
    active_all = after(jnp.concatenate([active, active_away], axis=0), grad_hidden_two_part)
    grad_up_all = after(jnp.concatenate([grad_up, grad_up_away], axis=0), grad_hidden_two_part)
    feed_away = across(after(contract(active_away, w_fc2, 1, 1).astype(bf16), grad_hidden_two_part))
    grad_fc2 = contract(grad_feed_all, active_all, 0, 0).astype(bf16)
    fc2_grad = lax.psum_scatter(grad_fc2, COLUMNS, scatter_dimension=0, tiled=True).astype(f32).T
    grad_fc1 = contract(hidden_two_all, grad_up_all, 0, 0).astype(bf16)
    fc1_grad = lax.psum_scatter(grad_fc1, COLUMNS, scatter_dimension=0, tiled=True).astype(f32)
    grad_hidden_two = grad_hidden_two_own + after(grad_hidden_two, grad_fc1, grad_fc2).astype(f32)

    grad_after, grad_shift_two, grad_scale_two = norm_back_two(grad_hidden_two.reshape(own_slots, slot_rows, width))
    grad_after = grad_after + grad_rows
    grad_gate_one = jnp.sum(grad_after * attention, axis=1)
    grad_attn_all = both((grad_after * gate1[:, None, :]).astype(bf16).reshape(rows, width))
    grad_mixed = attend_back(turn, grad_attn_all, w_out, heads)
    grad_out = contract(grad_attn_all, mixed_cat, 0, 0).astype(bf16)
    grad_out = lax.psum_scatter(grad_out, ("dq", "mp"), scatter_dimension=0, tiled=True)
    kept = (qkvg, pre, comb, scores, states, grad_mixed, taps_pad, gain_pad)
    d_qkvg_a, d_pre_a, d_taps_a, d_vec_a = gla_backward(0, heads // 2, patches, *kept)
    cat_a = join(turn, d_qkvg_a)
    split_a = fold_split(contract(hidden_all, cat_a, 0, 0).astype(bf16), order_a, 0)
    d_qkvg_b, d_pre_b, d_taps_b, d_vec_b = gla_backward(heads // 2, heads // 2, after(patches, *split_a), *kept)
    sum_a = fold_sum(split_a, order_a, 0, (d_qkvg_b,))
    feed_out = feed_own + after(feed_away, d_qkvg_b).astype(f32)
    feed_out = feed_out.reshape(own_slots, slot_rows, width)
    block_out = (after_attn + gate2[:, None, :] * feed_out).reshape(rows, width).astype(bf16)
    grad_gate_two = jnp.sum(grad_rows * feed_out, axis=1)
    cat_b = join(after(turn, sum_a), d_qkvg_b)
    split_b = fold_split(contract(hidden_all, cat_b, 0, 0).astype(bf16), order_a, 0)
    split_a = fold_split(sum_a, order_a, 1)
    hidden_own, hidden_far, d_down, d_up = project_back(
        after(turn, *split_a, *split_b), hidden_all, cat_a, cat_b, d_pre_a, d_pre_b, latent, w_a, w_b, down_pad, up_pad
    )
    hidden_sum = (hidden_own + other(hidden_far)).reshape(own_slots, slot_rows, width)
    grad_residual, grad_shift_one, grad_scale_one = norm_back_one(hidden_sum)
    input_grad = (grad_residual + grad_after).reshape(rows, width)

    grad_mod = jnp.concatenate(
        [grad_shift_one, grad_scale_one, grad_gate_one, grad_shift_two, grad_scale_two, grad_gate_two], axis=1
    )
    grad_mod = grad_mod.reshape(own_slots, 2 * dq, part).transpose(1, 0, 2).reshape(2 * dq, own_slots * part)

    def placed(value):
        return lax.dynamic_update_slice_in_dim(jnp.zeros((value.shape[0], width), f32), value, start, 1)

    d_vec = jnp.concatenate([d_vec_a, d_vec_b], axis=0)
    d_taps = jnp.concatenate([d_taps_a, d_taps_b], axis=0)
    d_down = d_down[:lowrank].T
    d_up = d_up[:lowrank].reshape(lowrank, heads, LANES)[:, :, :HDIM].reshape(lowrank, inner)
    d_taps = d_taps[:, :9, :HDIM].transpose(1, 0, 2).reshape(9, inner)
    d_bias = d_vec[:, 1, :HDIM].reshape(1, inner)
    d_gain = jnp.sum(d_vec[:, 0, :HDIM], axis=0)
    stacked = placed(jnp.concatenate([d_up, d_taps, d_bias], axis=0))
    flat = jnp.concatenate([d_down.reshape(lowrank, width), stacked, jnp.pad(d_gain, (0, width - HDIM))[None]], axis=0)
    flat_rows = flat.shape[0]
    flat = flat.reshape(-1)
    flat = jnp.pad(flat, (0, -flat.shape[0] % (2 * dq))).reshape(2 * dq, -1)
    packed = jnp.concatenate([grad_mod, flat], axis=1)

    names = bits()
    sum_b = fold_sum(split_b, order_a, 0, (packed, input_grad))
    sum_a = fold_sum(split_a, order_a, 1, (packed, input_grad))
    got = lax.all_to_all(packed, COLUMNS, split_axis=0, concat_axis=0, tiled=True)
    split_b = fold_split(sum_b, order_a, 1)
    split_a = fold_split(after(sum_a, sum_b), order_a, 2)
    sum_b = fold_sum(split_b, order_a, 1, (got,))
    sum_a = fold_sum(split_a, order_a, 2, (got,))
    flat = jnp.sum(got[:, own_slots * part :], axis=0)
    got = jnp.concatenate([got[:, : own_slots * part].reshape(-1), flat])
    away = lax.ppermute(got, "mp", FLIP)
    count = 2 * dq * own_slots * part
    flat = flat + away[count:]
    got = jnp.where(y == 0, jnp.stack([got[:count], away[:count]]), jnp.stack([away[:count], got[:count]]))
    got = got.reshape(2, dq, unit_slots, part).transpose(1, 0, 2, 3).reshape(2 * dq, unit_slots, part)
    folded = jnp.sum(got, axis=1, keepdims=True)
    first = jnp.arange(unit_slots)[None, :, None] == 0
    got = jnp.where(big_all[:, None, None], jnp.where(first, folded, 0.0), got).reshape(-1, part)
    grad_silu = jnp.dot(got, ada_weight.astype(f32).T, precision=lax.Precision.HIGHEST, preferred_element_type=f32)
    packed = jnp.concatenate(
        [grad_silu.reshape(2 * dq, unit_slots * width), jnp.broadcast_to(flat[None], (2 * dq, flat.shape[0]))], axis=1
    )
    split_b = fold_split(sum_b, order_a, 2)
    split_a = fold_split(after(sum_a, sum_b), order_a, 3)
    block_out = swap(after(block_out, sum_b))
    input_grad = swap(after(input_grad, sum_b).astype(bf16)).astype(f32)
    sum_b = fold_sum(split_b, order_a, 2, (packed,))
    sum_a = fold_sum(split_a, order_a, 3, (packed,))
    packed = lax.all_to_all(packed, COLUMNS, split_axis=0, concat_axis=0, tiled=True)
    ada_bias_grad = jnp.sum(got, axis=0)
    ada_weight_grad = jnp.dot(silu_all.astype(f32).T, got, precision=lax.Precision.HIGHEST, preferred_element_type=f32)
    sum_b = fold_step(sum_b, order_a, 3)
    for step in range(4, last):
        sum_a, sum_b = fold_step(sum_a, order_a, step), fold_step(sum_b, order_a, step)
    grad_back = swap(jnp.concatenate([sum_a, sum_b, grad_out.astype(f32)], axis=1).astype(bf16)).astype(f32)
    flat = packed[:, unit_slots * width :].reshape(-1)[: flat_rows * width].reshape(flat_rows, width)
    down_sum = flat[:lowrank].reshape(width, lowrank)
    up_sum = flat[lowrank : 2 * lowrank]
    taps_sum = flat[2 * lowrank : 2 * lowrank + 9]
    bias_sum = flat[2 * lowrank + 9]
    gain_sum = flat[2 * lowrank + 10, :HDIM]
    grad_silu = jnp.sum(packed[:, : unit_slots * width].reshape(2 * dq, unit_slots, width), axis=0)
    own_cond = lax.dynamic_slice_in_dim(condition, (2 * lax.axis_index("dq") + core) * unit_slots, unit_slots, 0)
    gate = jax.nn.sigmoid(own_cond)
    cond_grad = grad_silu * (gate * (1.0 + own_cond * (1.0 - gate)))
    proj_grad = grad_back[:, : 4 * inner].reshape(-1, 2, 4, inner // 2).transpose(2, 0, 1, 3).reshape(4, -1, inner)
    return (
        block_out, input_grad, cond_grad, ada_weight_grad, ada_bias_grad, proj_grad, down_sum, up_sum, bias_sum,
        gain_sum, taps_sum, grad_back[:, 4 * inner :].T, fc1_grad, fc2_grad,
    )


def solution(mesh):
    dp, mp = mesh.shape["dp"], mesh.shape["mp"]
    split = Mesh(mesh.devices.reshape(dp // 2, 2, mp), ("dq", "core", "mp"))
    d = ("dq", "core")
    every = ("dq", "core", "mp")
    return jax.shard_map(
        on_device,
        mesh=split,
        in_specs=(
            P(every, None), P(every, None), P(), P(), P(d), P(d), P(d), P(None, d), P(d), P(None, d, "mp"),
            P(), P(), P(), P(), P(), P("mp", d), P(d, "mp"), P("mp", d),
        ),
        out_specs=(
            P(every, None), P(every, None), P(d, None), P(None, d), P(d), P(None, d, "mp"),
            P(), P(), P(), P(), P(), P("mp", d), P(d, "mp"), P("mp", d),
        ),
        check_vma=False,
    )
```
